32 devices in a mesh: tgroup: 4 (over z), chan: 8 (over y, x, core).
Axes of the slice: x: 2, y: 2, z: 4, core: 2. Of those that a mesh axis runs over, the one named last changes fastest.
Arguments:
- raw_strain: float32 [16384, 10240], P(('tgroup', 'chan')), may hold values from -6 to 6
- whitening_taps: float32 [255], replicated, may hold values from -0.375 to 0.375
- first_block: int32 [16], P('chan'), may hold values from 0 to 159, as said below
- pair_owner: int32 [128, 1], P('chan'), may hold values from 0 to 3; in each aligned block of 16 rows (0 to 15, 16 to 31, ...) at most 5 rows name the same one
Outputs:
- stacks: float32 [160, 8, 8, 1001], P(('tgroup', 'chan'))
The draws below stay inside these ranges and needn't reach their ends.
Inputs may be any that keep to these rules, and one draw needn't show every extreme that they name: `first_block`: each chan index lists 2 stripes; its first stripe starts within the last 7 of its 160 blocks; chan index 0 lists block 159 first and block 0 second. `pair_owner`: pair blocks are ordered by chan index, stripe, then partner offset. Among the 16 pair blocks of one chan index at most 5 share an owner, and exactly 5 do in some chan index.
All inputs are finite; a program needn't handle non-finite values.
Results may differ from the reference program's by a relative error of at most 0.02.
Values may be sent and summed in bfloat16 or wider, within the bound.
No kernel may reach another device: no remote copies, remote signals or barrier semaphores. Data moves between devices by JAX's collectives and lax.ppermute only.
A program may use at most 192 MiB of HBM per device.

```python
import math
import jax
import jax.numpy as jnp
import numpy as np
from jax import lax

CHANNELS = 10240
TAPS = 255
MAXLAG = 500
CB = 8
K = 8
STRIPES = 2
SLOTS = 5
TS = 4096
TD = 2048
LAGS = 1001
TIME = 16384
BPD = 160
N_TGROUP = 4
N_CHAN = 8


def draw_first_block(key, part):
    key = jax.random.fold_in(key, 11)
    key_near, key_rest = jax.random.split(key)
    near = jax.random.randint(key_near, (N_CHAN, 1), BPD - K + 1, BPD)
    remaining = jax.random.randint(key_rest, (N_CHAN, STRIPES - 1), 0, BPD)
    near = near.at[0, 0].set(BPD - 1)
    remaining = remaining.at[0, 0].set(0)
    return jnp.concatenate([near, remaining], 1).reshape(N_CHAN * STRIPES).astype(jnp.int32)


def level_of(rng, dims, cuts, smallest, largest):
    level, own = 1.0, jax.random.fold_in(rng, 6)
    for axis_at, shards_of in cuts:
        steps = jnp.exp(jax.random.uniform(jax.random.fold_in(own, axis_at), (shards_of,), jnp.float32, smallest / len(cuts), largest / len(cuts)))
        level = level * jnp.repeat(steps, dims[axis_at] // shards_of).reshape([-1 if axis == axis_at else 1 for axis in range(len(dims))])
    return level


def deal_out(stream_key, own, number, rows, count, top, bound, slope):
    ranking = jax.random.permutation(stream_key, count)
    crowded, usual = portions_of(count, rows * top, bound, slope, True), portions_of(count, rows * top, bound, slope, False)
    places = jnp.arange(count)

    def named(lengths, offset_by):
        used = int((lengths > 0).sum())
        fixed = max(1, used // 4)
        shifted = fixed + (places - fixed + offset_by * (used - fixed)) % max(1, count - fixed)
        return jnp.zeros((count,), jnp.int32).at[ranking[jnp.where(places < fixed, places, shifted)]].set(jnp.asarray(lengths, jnp.int32))

    lengths = jnp.where(number % 4 == 0, named(crowded, number // 4), named(usual, number - number // 4 - 1))
    mixed = jax.random.permutation(jax.random.fold_in(own, 3), count)
    donor, sink = mixed[0:count // 2 * 2:2], mixed[1:count // 2 * 2:2]
    margin = jnp.minimum(lengths[donor] - 1, bound - lengths[sink]) // 2
    margin = jnp.where((donor == ranking[0]) | (sink == ranking[0]) | (lengths[sink] == 0), 0, jnp.maximum(margin, 0))
    shifted = jax.random.randint(jax.random.fold_in(own, 4), (count // 2,), 0, 1 << 20) % (margin + 1)
    lengths = lengths.at[donor].add(-shifted).at[sink].add(shifted)
    labels = jnp.searchsorted(jnp.cumsum(lengths), jnp.arange(rows * top), side="right").astype(jnp.int32)
    table = labels.reshape(top, rows).T
    table = table[jax.random.permutation(jax.random.fold_in(own, 1), rows)]
    offset_by = jax.random.randint(jax.random.fold_in(own, 2), (rows, 1), 0, top)
    return jnp.take_along_axis(table, (jnp.arange(top)[None, :] + offset_by) % top, axis=1)


def portions_of(number_of, total, reach, slope, full):
    weights = [(1 << 20) // math.isqrt(rank ** slope) + 1 for rank in range(1, number_of + 1)]
    largest = reach if full else min(reach, max(-(-total // number_of), total * weights[0] // sum(weights)))
    least = 1 if total - largest >= number_of - 1 else 0
    holding, spare = [largest] + [least] * (number_of - 1), total - largest - least * (number_of - 1)
    while spare > 0:
        movable = [i for i in range(1, number_of) if holding[i] < largest] or [i for i in range(1, number_of) if holding[i] < reach]
        pool, budget = sum([weights[i] for i in movable]), spare
        for i in movable:
            extra = min(reach - holding[i], max(1, budget * weights[i] // pool), spare)
            holding[i] = holding[i] + extra
            spare = spare - extra
    return np.array(holding)


def centred(stream_key, dims, scale, most, pieces=(), kind=jnp.bfloat16):
    factor_of = level_of(stream_key, dims, pieces, -0.22, 0.18) if pieces else 1.0
    drawn = jax.random.normal(stream_key, dims, jnp.float32) * scale * factor_of
    return jnp.minimum(jnp.maximum(drawn, -most), most).astype(kind)


def setup_inputs(seed: int = 0) -> dict:
    keys = jax.random.split(jax.random.key(seed), 5)
    raw_strain = centred(keys[0], (TIME, CHANNELS), 1.0, 6.0, ((0, 32),), jnp.float32)
    whitening_taps = centred(keys[1], (TAPS,), TAPS ** -0.5, 0.375, (), jnp.float32)
    first_block = draw_first_block(jax.random.fold_in(keys[4], 71), 0)
    pair_owner_keys = jax.random.split(jax.random.fold_in(keys[3], 1), (N_CHAN * STRIPES * K) // (STRIPES * K))
    pair_owner_turns = jax.random.permutation(jax.random.fold_in(keys[3], 3), (N_CHAN * STRIPES * K) // (STRIPES * K))
    pair_owner = jax.vmap(lambda own, number: deal_out(jax.random.fold_in(keys[3], 2), own, number, STRIPES * K, N_TGROUP, 1, SLOTS, 2))(pair_owner_keys, pair_owner_turns).reshape((N_CHAN * STRIPES * K, 1))
    return {"raw_strain": raw_strain, "whitening_taps": whitening_taps, "first_block": first_block, "pair_owner": pair_owner}


def whiten_segment(segment, whitening_taps):
    series = segment.T
    fft_length = 1 << (TS + TAPS).bit_length()
    reversed_taps = jnp.flip(whitening_taps)
    spectrum = jnp.fft.rfft(series, n=fft_length, axis=1) * jnp.fft.rfft(reversed_taps, n=fft_length)[None, :]
    convolved = jnp.fft.irfft(spectrum, n=fft_length, axis=1)
    half_taps = (TAPS - 1) // 2
    return convolved[:, half_taps:half_taps + TS:2].astype(jnp.bfloat16)

def correlate_segment(filtered, first_block):
    extended = jnp.concatenate([filtered.astype(jnp.float32), jnp.zeros(((K - 1) * CB, TD), jnp.float32)], 0)
    fft_length = 1 << (TD + LAGS).bit_length()
    spectra = jnp.fft.rfft(extended, n=fft_length, axis=1)
    column_starts = jnp.arange(N_CHAN * STRIPES, dtype=jnp.int32) // STRIPES * (CHANNELS // N_CHAN) + first_block * CB
    factor = 1.0 / math.sqrt(TD)

    def one_stripe(offset_row):
        leading = lax.dynamic_slice_in_dim(spectra, offset_row, CB, 0)
        partners = lax.dynamic_slice_in_dim(spectra, offset_row, K * CB, 0)
        cross = jnp.conj(leading)[:, None, :] * partners[None, :, :]
        circular = jnp.fft.irfft(cross, n=fft_length, axis=2)
        lagged = jnp.concatenate([circular[:, :, fft_length - MAXLAG:], circular[:, :, :MAXLAG + 1]], 2)
        scaled = (lagged * factor).astype(jnp.bfloat16)
        return scaled.reshape(CB, K, CB, LAGS).transpose(1, 0, 2, 3)
    stacked = lax.map(one_stripe, column_starts.astype(jnp.int32))
    return stacked.reshape(N_CHAN * STRIPES * K, CB, CB, LAGS)

def reference(raw_strain, whitening_taps, first_block, pair_owner):
    segments = raw_strain.reshape(N_TGROUP, TS, CHANNELS)

    def accumulate(running, segment):
        filtered = whiten_segment(segment, whitening_taps)
        partial_value = correlate_segment(filtered, first_block)
        return (running + partial_value.astype(jnp.float32), None)
    pair_total = N_CHAN * STRIPES * K
    summed = lax.scan(accumulate, jnp.zeros((pair_total, CB, CB, LAGS), jnp.float32), segments)[0]
    owners_grid = pair_owner[:, 0].reshape(N_CHAN, STRIPES * K)
    owner_hot = (owners_grid[:, :, None] == jnp.arange(N_TGROUP, dtype=jnp.int32)[None, None, :]).astype(jnp.int32)
    earlier = jnp.cumsum(owner_hot, axis=1) - owner_hot
    slot_index = lax.optimization_barrier(jnp.sum(earlier * owner_hot, axis=2))
    column = jnp.arange(N_CHAN, dtype=jnp.int32)[:, None]
    target = ((owners_grid * N_CHAN + column) * SLOTS + slot_index).reshape(pair_total).astype(jnp.int32)
    stacks = jnp.zeros((N_TGROUP * N_CHAN * SLOTS, CB, CB, LAGS), jnp.float32).at[target].set(summed)
    return stacks
```

```python
import functools
import math

import jax
import jax.numpy as jnp
from jax import lax
from jax.experimental import pallas as pl
from jax.experimental.pallas import tpu as pltpu
from jax.sharding import PartitionSpec as P

MAXLAG = 500
LAGS = 2 * MAXLAG + 1
CB = 8
K = 8
STRIPES = 2
SLOTS = 5
PAIRS = STRIPES * K
BLOCKS = STRIPES + SLOTS
WIDE = K * CB
SPILL = 64
LANES = 128
SHIFTS = 32
FRONT = -(-MAXLAG // LANES) * LANES
NT = (((1,), (1,)), ((), ()))


def params(megabytes):
    return pltpu.CompilerParams(vmem_limit_bytes=megabytes << 20)


def vmem():
    return pl.BlockSpec(memory_space=pltpu.VMEM)


def smem():
    return pl.BlockSpec(memory_space=pltpu.SMEM)


def from_behind(value, axis, steps):
    count = lax.axis_size(axis)
    first, last = (max(0, -steps), min(count, count - steps))
    return lax.ppermute(value, axis, [(source, source + steps) for source in range(first, last)])


def fir_matrix(taps, rows, outs):
    all_outs = outs + 2 * SPILL
    padded = jnp.concatenate(
        [jnp.zeros((1,), taps.dtype), taps, jnp.zeros((2 * all_outs,), taps.dtype)]
    )
    length = padded.shape[0]
    tiled = jnp.tile(padded, all_outs + 1)[: all_outs * (length - 2)]
    matrix = tiled.reshape(all_outs, length - 2)[:, 4 * SPILL : 4 * SPILL + rows]
    matrix = matrix.astype(jnp.bfloat16)
    spills = jnp.concatenate([matrix[:SPILL], matrix[SPILL + outs :]], 0)
    return matrix[SPILL : SPILL + outs], spills


def select_kernel(n_chan, n_tgroup, meta, raw, main_taps, spill_taps, main, left, right, table, window, picked, sems):
    rows, channels = raw.shape
    stripes = n_chan * STRIPES
    blocks_per = channels // n_chan // CB
    span = window.shape[2]

    def place(p):
        c, k = p // STRIPES, p % STRIPES
        start = (meta[c, k] + c * blocks_per) * CB
        base = jnp.minimum(start - lax.rem(start, LANES), channels - span)
        return start, pl.multiple_of(base, LANES)

    def copy(p):
        base = place(p)[1]
        return pltpu.make_async_copy(raw.at[:, pl.ds(base, span)], window.at[p], sems.at[p])

    for p in range(stripes):
        copy(p).start()

    def slots(c, carry):
        counts = jnp.int32(0)
        for q in range(PAIRS):
            owner = meta[c, STRIPES + q]
            slot = (counts >> (3 * owner)) & 7
            counts = counts + (jnp.int32(1) << (3 * owner))
            table[c * PAIRS + q] = (owner * n_chan + c) * BLOCKS + STRIPES + slot
        return carry

    lax.fori_loop(0, n_chan, slots, 0)

    row = lax.broadcasted_iota(jnp.int32, (WIDE, span), 0)
    lane = lax.broadcasted_iota(jnp.int32, (WIDE, span), 1)
    for p in range(stripes):
        copy(p).wait()
        start, base = place(p)
        hot = (lane == row + (start - base)) & (row < channels - start)
        hot = jnp.where(hot, 1.0, 0.0).astype(jnp.bfloat16)
        block = window[p].astype(jnp.bfloat16)
        chosen = lax.dot_general(hot, block, NT, preferred_element_type=jnp.float32)
        picked[p * WIDE : (p + 1) * WIDE, :] = chosen.astype(jnp.bfloat16)

    taken = picked[...]
    main[...] = lax.dot_general(taken, main_taps[...], NT, preferred_element_type=jnp.float32)
    spilled = lax.dot_general(taken, spill_taps[...], NT, preferred_element_type=jnp.float32)
    half = spilled.shape[0] // 2
    low, high = spilled[:half], spilled[half:]
    low_turned, high_turned = pltpu.roll(low, SPILL, 1), pltpu.roll(high, SPILL, 1)
    early = lax.broadcasted_iota(jnp.int32, low.shape, 1) < SPILL
    left[...] = jnp.where(early, low, high_turned).astype(jnp.bfloat16)
    right[...] = jnp.where(early, low_turned, high).astype(jnp.bfloat16)


def place_kernel(n_chan, n_tgroup, table, main, from_left, from_right, payload, total):
    count, outs = main.shape
    half = count // 2
    lanes = payload.shape[2]
    zero = jnp.zeros(payload.shape[1:], payload.dtype)

    total[...] = main[...]
    left, right = from_left[...].astype(jnp.float32), from_right[...].astype(jnp.float32)
    left_turned, right_turned = pltpu.roll(left, SPILL, 1), pltpu.roll(right, SPILL, 1)
    if outs >= LANES:
        early = lax.broadcasted_iota(jnp.int32, left.shape, 1) < SPILL
        total[:half, :LANES] += jnp.where(early, left, 0.0)
        total[half:, :LANES] += jnp.where(early, left_turned, 0.0)
        total[:half, outs - LANES :] += jnp.where(early, 0.0, right_turned)
        total[half:, outs - LANES :] += jnp.where(early, 0.0, right)
    else:
        total[:half, :] += (left + right)[:, :outs]
        total[half:, :] += (left_turned + right_turned)[:, :outs]

    def folded(block):
        value = total[pl.ds(pl.multiple_of(block * CB, CB), CB), :]
        parts = [value[:, at : at + lanes] for at in range(0, outs, lanes)]
        return jnp.concatenate(parts, 0).astype(payload.dtype)

    def one(c, carry):
        leads = [folded(c * PAIRS + p * K) for p in range(STRIPES)]
        for g in range(n_tgroup):
            at = (g * n_chan + c) * BLOCKS
            for p in range(STRIPES):
                payload[at + p] = leads[p]
            for s in range(SLOTS):
                payload[at + STRIPES + s] = zero
        for q in range(PAIRS):
            payload[table[c * PAIRS + q]] = folded(c * PAIRS + q)
        return carry

    lax.fori_loop(0, n_chan, one, 0)


def correlate_kernel(n_chan, n_tgroup, factor, first_count, arrived, out, lead, window_a, window_b):
    samples = lead.shape[2] // n_tgroup - LANES
    span = samples + LANES
    cols = span // LANES
    lag_blocks = -(-LAGS // LANES)
    step = LANES // SHIFTS
    high = step * CB
    ahead = FRONT // LANES - 1
    windows = (window_a, window_b)

    def series(g, block):
        if arrived.shape[0] == n_tgroup * BLOCKS:
            value = arrived[g * BLOCKS + block].astype(jnp.float32)
        else:
            parts = []
            for c in range(n_chan):
                piece = arrived[(g * n_chan + c) * BLOCKS + block].astype(jnp.float32)
                parts += [piece[at : at + CB] for at in range(0, piece.shape[0], CB)]
            value = jnp.concatenate(parts, 1)
        return jnp.concatenate([value, jnp.zeros((CB, LANES), jnp.float32)], 1)

    for p in range(STRIPES):
        for g in range(n_tgroup):
            value = series(g, p)
            for a in range(CB):
                spread = jnp.broadcast_to(value[a : a + 1], (SHIFTS, span))
                turned = pltpu.roll(spread, 0, 1, stride=1, stride_axis=0)
                lead[p, a * SHIFTS : (a + 1) * SHIFTS, g * span : (g + 1) * span] = turned.astype(
                    jnp.bfloat16
                )

    def bounds(i):
        return max(0, ahead - i), min(cols, ahead + cols - i)

    for window in windows:
        for g in range(n_tgroup):
            for i in range(lag_blocks):
                first, last = bounds(i)
                rows = slice(i * high, (i + 1) * high)
                if first > 0:
                    window[rows, g * span : g * span + first * LANES] = jnp.zeros(
                        (high, first * LANES), jnp.bfloat16
                    )
                if last < cols:
                    window[rows, g * span + last * LANES : (g + 1) * span] = jnp.zeros(
                        (high, (cols - last) * LANES), jnp.bfloat16
                    )

    group = lax.broadcasted_iota(jnp.int32, (CB, LANES), 1) // SHIFTS
    for s in range(SLOTS):
        window = windows[s % 2]
        for g in range(n_tgroup):
            value = series(g, STRIPES + s)
            turned = [
                pltpu.roll(value, span - (FRONT - MAXLAG + SHIFTS * n), 1) for n in range(step)
            ]
            stacked = jnp.concatenate(turned, 0).astype(jnp.bfloat16)
            stacked = jnp.concatenate([stacked[:, samples:], stacked[:, :samples]], 1)
            for i in range(lag_blocks):
                first, last = bounds(i)
                window[
                    i * high : (i + 1) * high, g * span + first * LANES : g * span + last * LANES
                ] = stacked[:, (first + i - ahead) * LANES : (last + i - ahead) * LANES]
        which = jnp.where(s < first_count[0], 0, 1)
        summed = lax.dot_general(window[...], lead[which], NT, preferred_element_type=jnp.float32)
        summed = summed * factor
        for i in range(lag_blocks):
            width = min(LANES, LAGS - i * LANES)
            for h in range(CB // step):
                parts = [
                    summed[(i * step + n) * CB : (i * step + n + 1) * CB, h * LANES : (h + 1) * LANES]
                    for n in range(step)
                ]
                for a in range(step):
                    value = parts[a]
                    for n in range(step):
                        if n != a:
                            moved = pltpu.roll(parts[n], (SHIFTS * (n - a)) % LANES, 1)
                            value = jnp.where(group == n, moved, value)
                    out[s, h * step + a, :, i * LANES : i * LANES + width] = value[:, :width]


def local(raw_strain, whitening_taps, first_block, pair_owner):
    n_chan, n_tgroup = lax.axis_size("chan"), lax.axis_size("tgroup")
    n_dev = n_chan * n_tgroup
    rows, channels = raw_strain.shape
    outs = rows // 2
    samples = outs * n_chan
    count = n_chan * STRIPES * WIDE
    span = 2 * LANES

    own = jnp.concatenate([first_block, pair_owner[:, 0]])
    meta = lax.all_gather(own, "chan")
    me = lax.axis_index("tgroup")
    first_count = jnp.sum((pair_owner[:K, 0] == me).astype(jnp.int32)).reshape(1)
    main_taps, spill_taps = fir_matrix(whitening_taps, rows, outs)

    main, left, right, table = pl.pallas_call(
        functools.partial(select_kernel, n_chan, n_tgroup),
        out_shape=(
            jax.ShapeDtypeStruct((count, outs), jnp.float32),
            jax.ShapeDtypeStruct((count // 2, LANES), jnp.bfloat16),
            jax.ShapeDtypeStruct((count // 2, LANES), jnp.bfloat16),
            jax.ShapeDtypeStruct((n_chan * PAIRS,), jnp.int32),
        ),
        in_specs=[smem(), pl.BlockSpec(memory_space=pl.ANY), vmem(), vmem()],
        out_specs=(vmem(), vmem(), vmem(), smem()),
        scratch_shapes=[
            pltpu.VMEM((n_chan * STRIPES, rows, span), jnp.float32),
            pltpu.VMEM((count, rows), jnp.bfloat16),
            pltpu.SemaphoreType.DMA((n_chan * STRIPES,)),
        ],
        compiler_params=params(40),
        name="select_filter",
    )(meta, raw_strain, main_taps, spill_taps)

    from_right = from_behind(left, "chan", -1)
    from_left = from_behind(right, "chan", 1)

    lanes = min(LANES, outs)
    fold = CB * (outs // lanes)
    payload = pl.pallas_call(
        functools.partial(place_kernel, n_chan, n_tgroup),
        out_shape=jax.ShapeDtypeStruct((n_dev * BLOCKS, fold, lanes), jnp.bfloat16),
        in_specs=[smem(), vmem(), vmem(), vmem()],
        out_specs=vmem(),
        scratch_shapes=[pltpu.VMEM((count, outs), jnp.float32)],
        compiler_params=params(40),
        name="place_blocks",
    )(table, main, from_left, from_right)

    arrived = lax.all_to_all(
        payload.reshape(n_dev, BLOCKS, fold, lanes),
        ("tgroup", "chan"),
        split_axis=0,
        concat_axis=0,
        tiled=True,
    )
    if lanes == LANES:
        arrived = arrived.reshape(n_dev * BLOCKS, fold, lanes)
    else:
        arrived = arrived.reshape(n_tgroup, n_chan, BLOCKS, CB, lanes)
        arrived = arrived.transpose(0, 2, 3, 1, 4).reshape(n_tgroup * BLOCKS, CB, samples)

    depth = n_tgroup * (samples + LANES)
    return pl.pallas_call(
        functools.partial(correlate_kernel, n_chan, n_tgroup, 1.0 / math.sqrt(samples)),
        out_shape=jax.ShapeDtypeStruct((SLOTS, CB, CB, LAGS), jnp.float32),
        in_specs=[smem(), vmem()],
        out_specs=vmem(),
        scratch_shapes=[
            pltpu.VMEM((STRIPES, CB * SHIFTS, depth), jnp.bfloat16),
            pltpu.VMEM((-(-LAGS // SHIFTS) * CB, depth), jnp.bfloat16),
            pltpu.VMEM((-(-LAGS // SHIFTS) * CB, depth), jnp.bfloat16),
        ],
        compiler_params=params(56),
        name="correlate",
    )(first_count, arrived)


def solution(mesh):
    in_specs = (P(("tgroup", "chan"), None), P(), P("chan"), P("chan", None))
    out_specs = P(("tgroup", "chan"), None, None, None)
    return jax.shard_map(local, mesh=mesh, in_specs=in_specs, out_specs=out_specs, check_vma=False)
```

```python
import functools
import math

import jax
import jax.numpy as jnp
from jax import lax
from jax.experimental import pallas as pl
from jax.experimental.pallas import tpu as pltpu
from jax.sharding import PartitionSpec as P

MAXLAG = 500
LAGS = 2 * MAXLAG + 1
TAPS = 255
CB = 8
K = 8
STRIPES = 2
SLOTS = 5
PAIRS = STRIPES * K
BLOCKS = STRIPES + SLOTS
WIDE = K * CB
SPILL = 64
LANES = 128
SHIFTS = 32
STEP = LANES // SHIFTS
LAG_BLOCKS = -(-LAGS // LANES)
FRONT = -(-MAXLAG // LANES) * LANES
NT = (((1,), (1,)), ((), ()))


def params(megabytes):
    return pltpu.CompilerParams(vmem_limit_bytes=megabytes << 20)


def vmem():
    return pl.BlockSpec(memory_space=pltpu.VMEM)


def smem():
    return pl.BlockSpec(memory_space=pltpu.SMEM)


def select_kernel(n_chan, firsts, raw, taps, sent, window, picked, line, sems):
    rows, channels = raw.shape
    outs = rows // 2
    stripes = n_chan * STRIPES
    blocks_per = channels // n_chan // CB
    span = window.shape[2]

    def place(p):
        c, k = p // STRIPES, p % STRIPES
        start = (firsts[c, k] + c * blocks_per) * CB
        base = jnp.minimum(start - lax.rem(start, LANES), channels - span)
        return start, pl.multiple_of(base, LANES)

    def copy(p):
        base = place(p)[1]
        return pltpu.make_async_copy(raw.at[:, pl.ds(base, span)], window.at[p], sems.at[p])

    for p in range(stripes):
        copy(p).start()

    width = line.shape[1]
    line[...] = jnp.zeros_like(line)
    line[0:1, :TAPS] = taps[...]
    spread = jnp.broadcast_to(line[0:1, :], (outs + 2 * SPILL, width))
    weights = pltpu.roll(spread, width - 4 * SPILL + 1, 1, stride=2, stride_axis=0)[:, :rows]
    weights = weights.astype(jnp.bfloat16)
    weights = jnp.concatenate(
        [weights[SPILL : SPILL + outs], weights[SPILL + outs :], weights[:SPILL]], 0
    )

    row = lax.broadcasted_iota(jnp.int32, (WIDE, span), 0)
    lane = lax.broadcasted_iota(jnp.int32, (WIDE, span), 1)
    batch = 4
    for first in range(0, stripes, batch):
        for p in range(first, first + batch):
            copy(p).wait()
            start, base = place(p)
            hot = (lane == row + (start - base)) & (row < channels - start)
            hot = jnp.where(hot, 1.0, 0.0).astype(jnp.bfloat16)
            block = window[p].astype(jnp.bfloat16)
            chosen = lax.dot_general(hot, block, NT, preferred_element_type=jnp.float32)
            picked[p * WIDE : (p + 1) * WIDE, :] = chosen.astype(jnp.bfloat16)
        part = slice(first * WIDE, (first + batch) * WIDE)
        result = lax.dot_general(picked[part, :], weights, NT, preferred_element_type=jnp.float32)
        sent[part, :] = result.astype(jnp.bfloat16)


def add_spills(n_chan, outs, got, total):
    count = total.shape[0]
    early = lax.broadcasted_iota(jnp.int32, (count, LANES), 1) < SPILL

    def spill(c):
        return got[c * count : (c + 1) * count, outs:].astype(jnp.float32)

    spills = [spill(c) for c in range(n_chan)]
    for c in range(n_chan):
        value = got[c * count : (c + 1) * count, :outs].astype(jnp.float32)
        parts = [value[:, at : at + LANES] for at in range(0, outs, LANES)]
        if c > 0:
            parts[0] = parts[0] + jnp.where(early, spills[c - 1], 0.0)
        if c < n_chan - 1:
            parts[-1] = parts[-1] + jnp.where(early, 0.0, spills[c + 1])
        for at, part in enumerate(parts):
            total[:, c * outs + at * LANES : c * outs + (at + 1) * LANES] = part


def place_kernel(n_chan, n_tgroup, outs, owners, got, *refs):
    sends, (total, pairs) = refs[:n_tgroup], refs[n_tgroup:]
    me = lax.axis_index("tgroup")
    if got.dtype == jnp.float32:
        total[...] = got[...]
    else:
        add_spills(n_chan, outs, got, total)

    for at in range(n_tgroup * SLOTS):
        pairs[at] = -1
    counts = jnp.int32(0)
    for q in range(PAIRS):
        owner = owners[q]
        slot = (counts >> (3 * owner)) & 7
        counts = counts + (jnp.int32(1) << (3 * owner))
        pairs[lax.rem(owner - me + n_tgroup, n_tgroup) * SLOTS + slot] = q

    half = total.shape[1] // 2

    def folded(q):
        value = total[pl.ds(pl.multiple_of(q * CB, CB), CB), :]
        return jnp.concatenate([value[:, :half], value[:, half:]], 0)

    leads = [folded(p * K).astype(jnp.bfloat16) for p in range(STRIPES)]
    for shift in range(n_tgroup):
        for p in range(STRIPES):
            sends[shift][p] = leads[p]
        for s in range(SLOTS):
            q = pairs[shift * SLOTS + s]
            value = jnp.where(q >= 0, folded(jnp.maximum(q, 0)), 0.0)
            sends[shift][STRIPES + s] = value.astype(jnp.bfloat16)


def correlate_kernel(factor, last, owners, *refs):
    lead, window_a, window_b = refs[-3:]
    out = refs[-4]
    arrived, before = refs[0], (refs[1] if len(refs) == 6 else None)
    windows = (window_a, window_b)
    span = lead.shape[2]
    samples = span - LANES
    cols = span // LANES
    high = STEP * CB
    ahead = FRONT // LANES - 1
    me = lax.axis_index("tgroup")
    first_count = jnp.int32(0)
    for q in range(K):
        first_count += jnp.where(owners[q] == me, 1, 0)

    def series(block):
        value = arrived[block].astype(jnp.float32)
        return jnp.concatenate([value[:CB], value[CB:], jnp.zeros((CB, LANES), jnp.float32)], 1)

    for p in range(STRIPES):
        value = series(p)
        for a in range(CB):
            spread = jnp.broadcast_to(value[a : a + 1], (SHIFTS, span))
            turned = pltpu.roll(spread, 0, 1, stride=1, stride_axis=0)
            lead[p, a * SHIFTS : (a + 1) * SHIFTS, :] = turned.astype(jnp.bfloat16)

    def bounds(i):
        return max(0, ahead - i), min(cols, ahead + cols - i)

    for window in windows:
        for i in range(LAG_BLOCKS):
            first, end = bounds(i)
            rows = slice(i * high, (i + 1) * high)
            if first > 0:
                window[rows, : first * LANES] = jnp.zeros((high, first * LANES), jnp.bfloat16)
            if end < cols:
                window[rows, end * LANES :] = jnp.zeros((high, (cols - end) * LANES), jnp.bfloat16)

    group = lax.broadcasted_iota(jnp.int32, (CB, LANES), 1) // SHIFTS
    for s in range(SLOTS):
        window = windows[s % 2]
        value = series(STRIPES + s)
        turned = [pltpu.roll(value, span - (FRONT - MAXLAG + SHIFTS * n), 1) for n in range(STEP)]
        stacked = jnp.concatenate(turned, 0).astype(jnp.bfloat16)
        stacked = jnp.concatenate([stacked[:, samples:], stacked[:, :samples]], 1)
        for i in range(LAG_BLOCKS):
            first, end = bounds(i)
            window[i * high : (i + 1) * high, first * LANES : end * LANES] = stacked[
                :, (first + i - ahead) * LANES : (end + i - ahead) * LANES
            ]
        which = jnp.where(s < first_count, 0, 1)
        summed = lax.dot_general(window[...], lead[which], NT, preferred_element_type=jnp.float32)
        if before is not None:
            summed = summed + before[s]
        if not last:
            out[s] = summed
            continue
        summed = summed * factor
        for i in range(LAG_BLOCKS):
            width = min(LANES, LAGS - i * LANES)
            for h in range(CB // STEP):
                parts = [
                    summed[(i * STEP + n) * CB : (i * STEP + n + 1) * CB, h * LANES : (h + 1) * LANES]
                    for n in range(STEP)
                ]
                for a in range(STEP):
                    value = parts[a]
                    for n in range(STEP):
                        if n != a:
                            moved = pltpu.roll(parts[n], (SHIFTS * (n - a)) % LANES, 1)
                            value = jnp.where(group == n, moved, value)
                    out[s, h * STEP + a, :, i * LANES : i * LANES + width] = value[:, :width]


def correlate(owners, arrived, before, factor, last, samples):
    high, wide = STEP * LAG_BLOCKS * CB, CB * SHIFTS
    if last:
        shape = jax.ShapeDtypeStruct((SLOTS, CB, CB, LAGS), jnp.float32)
    else:
        shape = jax.ShapeDtypeStruct((SLOTS, high, wide), jnp.float32)
    operands = (owners, arrived) + (() if before is None else (before,))
    return pl.pallas_call(
        functools.partial(correlate_kernel, factor, last),
        out_shape=shape,
        in_specs=[smem()] + [vmem()] * (len(operands) - 1),
        out_specs=vmem(),
        scratch_shapes=[
            pltpu.VMEM((STRIPES, wide, samples + LANES), jnp.bfloat16),
            pltpu.VMEM((high, samples + LANES), jnp.bfloat16),
            pltpu.VMEM((high, samples + LANES), jnp.bfloat16),
        ],
        compiler_params=params(40),
        name="correlate_last" if last else "correlate",
    )(*operands)


def local(raw_strain, whitening_taps, first_block, pair_owner):
    n_chan, n_tgroup = lax.axis_size("chan"), lax.axis_size("tgroup")
    rows, channels = raw_strain.shape
    outs = rows // 2
    samples = outs * n_chan
    count = PAIRS * CB
    owners = pair_owner[:, 0]

    firsts = lax.all_to_all(
        jnp.broadcast_to(first_block[None, :], (n_chan, STRIPES)),
        "chan",
        split_axis=0,
        concat_axis=0,
        tiled=True,
    )
    line = -(-(rows + 2 * outs + 4 * SPILL) // (2 * LANES)) * 2 * LANES
    sent = pl.pallas_call(
        functools.partial(select_kernel, n_chan),
        out_shape=jax.ShapeDtypeStruct((n_chan * count, outs + 2 * SPILL), jnp.bfloat16),
        in_specs=[smem(), pl.BlockSpec(memory_space=pl.ANY), vmem()],
        out_specs=vmem(),
        scratch_shapes=[
            pltpu.VMEM((n_chan * STRIPES, rows, 2 * LANES), jnp.float32),
            pltpu.VMEM((n_chan * count, rows), jnp.bfloat16),
            pltpu.VMEM((8, line), jnp.float32),
            pltpu.SemaphoreType.DMA((n_chan * STRIPES,)),
        ],
        compiler_params=params(40),
        name="select_filter",
    )(firsts, raw_strain, whitening_taps.reshape(1, TAPS))

    got = lax.all_to_all(
        sent.reshape(n_chan, count, outs + 2 * SPILL),
        "chan",
        split_axis=0,
        concat_axis=0,
        tiled=True,
    )
    if outs % LANES == 0:
        got = got.reshape(n_chan * count, outs + 2 * SPILL)
    else:
        wide = got.astype(jnp.float32)
        none = jnp.zeros((1, count, outs - SPILL), jnp.float32)
        zero = jnp.zeros((1, count, SPILL), jnp.float32)
        right = jnp.concatenate([zero, wide[:-1, :, outs : outs + SPILL]], 0)
        left = jnp.concatenate([wide[1:, :, outs + SPILL :], zero], 0)
        none = jnp.broadcast_to(none, (n_chan,) + none.shape[1:])
        added = wide[:, :, :outs] + jnp.concatenate([right, none], 2) + jnp.concatenate([none, left], 2)
        got = added.transpose(1, 0, 2).reshape(count, samples)

    packed = jax.ShapeDtypeStruct((BLOCKS, 2 * CB, samples // 2), jnp.bfloat16)
    sends = pl.pallas_call(
        functools.partial(place_kernel, n_chan, n_tgroup, outs),
        out_shape=(packed,) * n_tgroup,
        in_specs=[smem(), vmem()],
        out_specs=(vmem(),) * n_tgroup,
        scratch_shapes=[
            pltpu.VMEM((count, samples), jnp.float32),
            pltpu.SMEM((n_tgroup * SLOTS,), jnp.int32),
        ],
        compiler_params=params(40),
        name="place_blocks",
    )(owners, got)

    order = sorted(range(1, n_tgroup), key=lambda s: min(s, n_tgroup - s))
    arrived = [sends[0]]
    for shift in order:
        route = [(g, (g + shift) % n_tgroup) for g in range(n_tgroup)]
        arrived.append(lax.ppermute(sends[shift], "tgroup", route))

    value = None
    factor = 1.0 / math.sqrt(samples)
    for at, block in enumerate(arrived):
        value = correlate(owners, block, value, factor, at == n_tgroup - 1, samples)
    return value


def solution(mesh):
    in_specs = (P(("tgroup", "chan"), None), P(), P("chan"), P("chan", None))
    out_specs = P(("tgroup", "chan"), None, None, None)
    return jax.shard_map(local, mesh=mesh, in_specs=in_specs, out_specs=out_specs, check_vma=False)
```

```python
import functools
import math

import jax
import jax.numpy as jnp
from jax import lax
from jax.experimental import pallas as pl
from jax.experimental.pallas import tpu as pltpu
from jax.sharding import PartitionSpec as P

MAXLAG = 500
LAGS = 2 * MAXLAG + 1
TAPS = 255
CB = 8
K = 8
STRIPES = 2
SLOTS = 5
PAIRS = STRIPES * K
BLOCKS = STRIPES + SLOTS
WIDE = K * CB
SPILL = 64
LANES = 128
SHIFTS = 32
STEP = LANES // SHIFTS
LAG_BLOCKS = -(-LAGS // LANES)
FRONT = -(-MAXLAG // LANES) * LANES
NT = (((1,), (1,)), ((), ()))


def params(megabytes):
    return pltpu.CompilerParams(vmem_limit_bytes=megabytes << 20)


def vmem():
    return pl.BlockSpec(memory_space=pltpu.VMEM)


def smem():
    return pl.BlockSpec(memory_space=pltpu.SMEM)


def select_kernel(n_chan, firsts, raw, taps, *refs):
    sends, (window, picked, line, tap_sem, sems) = refs[:n_chan], refs[n_chan:]
    rows, channels = raw.shape
    outs = rows // 2
    stripes = n_chan * STRIPES
    blocks_per = channels // n_chan // CB
    span = window.shape[2]
    me = lax.axis_index("chan")

    def place(p):
        c, k = me ^ (p // STRIPES), p % STRIPES
        start = (firsts[c, k] + c * blocks_per) * CB
        base = jnp.minimum(start - lax.rem(start, LANES), channels - span)
        return start, pl.multiple_of(base, LANES)

    def copy(p):
        base = place(p)[1]
        return pltpu.make_async_copy(raw.at[:, pl.ds(base, span)], window.at[p], sems.at[p])

    line[...] = jnp.zeros_like(line)
    tap_copy = pltpu.make_async_copy(taps, line.at[0:1, : taps.shape[1]], tap_sem)
    tap_copy.start()
    for p in range(stripes):
        copy(p).start()

    width = line.shape[1]
    tap_copy.wait()
    spread = jnp.broadcast_to(line[0:1, :], (outs + 2 * SPILL, width))
    weights = pltpu.roll(spread, width - 4 * SPILL + 1, 1, stride=2, stride_axis=0)[:, :rows]
    weights = weights.astype(jnp.bfloat16)
    weights = jnp.concatenate(
        [weights[SPILL : SPILL + outs], weights[SPILL + outs :], weights[:SPILL]], 0
    )

    row = lax.broadcasted_iota(jnp.int32, (WIDE, span), 0)
    lane = lax.broadcasted_iota(jnp.int32, (WIDE, span), 1)
    batch = 2 * STRIPES
    for first in range(0, stripes, batch):
        for p in range(first, first + batch):
            copy(p).wait()
            start, base = place(p)
            hot = (lane == row + (start - base)) & (row < channels - start)
            hot = jnp.where(hot, 1.0, 0.0).astype(jnp.bfloat16)
            block = window[p].astype(jnp.bfloat16)
            chosen = lax.dot_general(hot, block, NT, preferred_element_type=jnp.float32)
            picked[p * WIDE : (p + 1) * WIDE, :] = chosen.astype(jnp.bfloat16)
        part = slice(first * WIDE, (first + batch) * WIDE)
        result = lax.dot_general(picked[part, :], weights, NT, preferred_element_type=jnp.float32)
        result = result.astype(jnp.bfloat16)
        for at in range(batch // STRIPES):
            sends[first // STRIPES + at][...] = result[at * STRIPES * WIDE : (at + 1) * STRIPES * WIDE]


def add_spills(n_chan, outs, got, total):
    count = total.shape[0]
    early = lax.broadcasted_iota(jnp.int32, (count, LANES), 1) < SPILL
    chunks = [lax.axis_index("chan") ^ k for k in range(n_chan)]
    for chunk, value in zip(chunks, got):
        at = pl.ds(pl.multiple_of(chunk * outs, LANES), outs)
        total[:, at] = value[:, :outs].astype(jnp.float32)
    for chunk, value in zip(chunks, got):
        spill = value[:, outs:].astype(jnp.float32)
        after = jnp.minimum(chunk + 1, n_chan - 1) * outs
        after = pl.ds(pl.multiple_of(after, LANES), LANES)
        total[:, after] += jnp.where(early & (chunk < n_chan - 1), spill, 0.0)
        before = jnp.maximum(chunk * outs, LANES) - LANES
        before = pl.ds(pl.multiple_of(before, LANES), LANES)
        total[:, before] += jnp.where(early | (chunk == 0), 0.0, spill)


def tile_of(group, width, vectors):
    half = vectors // 2
    if group == 0:
        return jnp.where(width == 0, 0, half + 1), half - 1
    return jnp.where(width == 0, half - 1, 0), half + 1


def own_half(n_chan):
    return jnp.where(lax.axis_index("chan") < n_chan // 2, 0, 1)


def place_kernel(n_chan, n_tgroup, outs, group, owners, *refs):
    got, (total, pairs) = refs[: -n_tgroup - 2], refs[-2:]
    sends = refs[-n_tgroup - 2 : -2]
    me = lax.axis_index("tgroup")
    if len(got) == 1:
        total[...] = got[0][...]
    else:
        add_spills(n_chan, outs, got, total)

    for at in range(n_tgroup * SLOTS):
        pairs[at] = -1
    counts = jnp.int32(0)
    for q in range(PAIRS):
        owner = owners[q]
        slot = (counts >> (3 * owner)) & 7
        counts = counts + (jnp.int32(1) << (3 * owner))
        pairs[lax.rem(owner - me + n_tgroup, n_tgroup) * SLOTS + slot] = q

    base, per = tile_of(group, own_half(n_chan), total.shape[1] // LANES)

    def tiles(q):
        rows = pl.ds(pl.multiple_of(q * CB, CB), CB)
        return [
            total[rows, pl.ds(pl.multiple_of((base + j) * LANES, LANES), LANES)] for j in range(per)
        ]

    zero = jnp.zeros((CB, LANES), jnp.float32)
    leads = sum([tiles(p * K) for p in range(STRIPES)], [])
    for shift in range(n_tgroup):
        parts = list(leads)
        for s in range(SLOTS):
            q = pairs[shift * SLOTS + s]
            parts += [jnp.where(q >= 0, tile, 0.0) for tile in tiles(jnp.maximum(q, 0))]
        parts += [zero] * (len(parts) % 2)
        for at in range(0, len(parts), 2):
            value = jnp.concatenate(parts[at : at + 2], 0)
            sends[shift][at // 2] = value.astype(jnp.bfloat16)


def correlate_kernel(n_chan, factor, last, owners, *refs):
    lead, window_a, window_b, whole = refs[-4:]
    out = refs[-5]
    arrived, before = refs[:2], (refs[2] if len(refs) == 8 else None)
    windows = (window_a, window_b)
    span = lead.shape[2]
    samples = span - LANES
    cols = span // LANES
    high = STEP * CB
    ahead = FRONT // LANES - 1
    me = lax.axis_index("tgroup")
    first_count = jnp.int32(0)
    for q in range(K):
        first_count += jnp.where(owners[q] == me, 1, 0)

    for group in range(2):
        base, per = tile_of(group, own_half(n_chan), samples // LANES)
        for at in range(arrived[group].shape[0]):
            value = arrived[group][at].astype(jnp.float32)
            for part in range(2):
                block, j = (2 * at + part) // per, (2 * at + part) % per
                if block < BLOCKS:
                    lanes = pl.ds(pl.multiple_of((base + j) * LANES, LANES), LANES)
                    whole[block, :, lanes] = value[part * CB : (part + 1) * CB]

    def series(block):
        return jnp.concatenate([whole[block], jnp.zeros((CB, LANES), jnp.float32)], 1)

    for p in range(STRIPES):
        value = series(p)
        for a in range(CB):
            spread = jnp.broadcast_to(value[a : a + 1], (SHIFTS, span))
            turned = pltpu.roll(spread, 0, 1, stride=1, stride_axis=0)
            lead[p, a * SHIFTS : (a + 1) * SHIFTS, :] = turned.astype(jnp.bfloat16)

    def bounds(i):
        return max(0, ahead - i), min(cols, ahead + cols - i)

    for window in windows:
        for i in range(LAG_BLOCKS):
            first, end = bounds(i)
            rows = slice(i * high, (i + 1) * high)
            if first > 0:
                window[rows, : first * LANES] = jnp.zeros((high, first * LANES), jnp.bfloat16)
            if end < cols:
                window[rows, end * LANES :] = jnp.zeros((high, (cols - end) * LANES), jnp.bfloat16)

    group = lax.broadcasted_iota(jnp.int32, (CB, LANES), 1) // SHIFTS
    for s in range(SLOTS):
        window = windows[s % 2]
        value = series(STRIPES + s)
        turned = [pltpu.roll(value, span - (FRONT - MAXLAG + SHIFTS * n), 1) for n in range(STEP)]
        stacked = jnp.concatenate(turned, 0).astype(jnp.bfloat16)
        stacked = jnp.concatenate([stacked[:, samples:], stacked[:, :samples]], 1)
        for i in range(LAG_BLOCKS):
            first, end = bounds(i)
            window[i * high : (i + 1) * high, first * LANES : end * LANES] = stacked[
                :, (first + i - ahead) * LANES : (end + i - ahead) * LANES
            ]
        which = jnp.where(s < first_count, 0, 1)
        summed = lax.dot_general(window[...], lead[which], NT, preferred_element_type=jnp.float32)
        if before is not None:
            summed = summed + before[s]
        if not last:
            out[s] = summed
            continue
        summed = summed * factor
        for i in range(LAG_BLOCKS):
            width = min(LANES, LAGS - i * LANES)
            for h in range(CB // STEP):
                parts = [
                    summed[(i * STEP + n) * CB : (i * STEP + n + 1) * CB, h * LANES : (h + 1) * LANES]
                    for n in range(STEP)
                ]
                for a in range(STEP):
                    value = parts[a]
                    for n in range(STEP):
                        if n != a:
                            moved = pltpu.roll(parts[n], (SHIFTS * (n - a)) % LANES, 1)
                            value = jnp.where(group == n, moved, value)
                    out[s, h * STEP + a, :, i * LANES : i * LANES + width] = value[:, :width]


def correlate(n_chan, owners, arrived, before, factor, last, samples):
    high, wide = STEP * LAG_BLOCKS * CB, CB * SHIFTS
    if last:
        shape = jax.ShapeDtypeStruct((SLOTS, CB, CB, LAGS), jnp.float32)
    else:
        shape = jax.ShapeDtypeStruct((SLOTS, high, wide), jnp.float32)
    operands = (owners,) + arrived + (() if before is None else (before,))
    return pl.pallas_call(
        functools.partial(correlate_kernel, n_chan, factor, last),
        out_shape=shape,
        in_specs=[smem()] + [vmem()] * (len(operands) - 1),
        out_specs=vmem(),
        scratch_shapes=[
            pltpu.VMEM((STRIPES, wide, samples + LANES), jnp.bfloat16),
            pltpu.VMEM((high, samples + LANES), jnp.bfloat16),
            pltpu.VMEM((high, samples + LANES), jnp.bfloat16),
            pltpu.VMEM((BLOCKS, CB, samples), jnp.float32),
        ],
        compiler_params=params(40),
        name="correlate_last" if last else "correlate",
    )(*operands)


def local(raw_strain, whitening_taps, first_block, pair_owner):
    n_chan, n_tgroup = lax.axis_size("chan"), lax.axis_size("tgroup")
    rows, channels = raw_strain.shape
    outs = rows // 2
    samples = outs * n_chan
    count = PAIRS * CB
    owners = pair_owner[:, 0]

    firsts = lax.all_to_all(
        jnp.broadcast_to(first_block[None, :], (n_chan, STRIPES)),
        "chan",
        split_axis=0,
        concat_axis=0,
        tiled=True,
    )
    line = -(-(rows + 2 * outs + 4 * SPILL) // (2 * LANES)) * 2 * LANES
    sends = pl.pallas_call(
        functools.partial(select_kernel, n_chan),
        out_shape=(jax.ShapeDtypeStruct((count, outs + 2 * SPILL), jnp.bfloat16),) * n_chan,
        in_specs=[smem(), pl.BlockSpec(memory_space=pl.ANY), pl.BlockSpec(memory_space=pl.ANY)],
        out_specs=(vmem(),) * n_chan,
        scratch_shapes=[
            pltpu.VMEM((n_chan * STRIPES, rows, 2 * LANES), jnp.float32),
            pltpu.VMEM((n_chan * count, rows), jnp.bfloat16),
            pltpu.VMEM((8, line), jnp.float32),
            pltpu.SemaphoreType.DMA,
            pltpu.SemaphoreType.DMA((n_chan * STRIPES,)),
        ],
        compiler_params=params(40),
        name="select_filter",
    )(firsts, raw_strain, jnp.pad(whitening_taps, (0, 1)).reshape(1, TAPS + 1))

    got = [sends[0]]
    for k in range(1, n_chan):
        got.append(lax.ppermute(sends[k], "chan", [(c, c ^ k) for c in range(n_chan)]))
    if outs % LANES:
        wide = jnp.stack(got).astype(jnp.float32)
        wide = jnp.take(wide, lax.axis_index("chan") ^ jnp.arange(n_chan), axis=0)
        none = jnp.zeros((n_chan, count, outs - SPILL), jnp.float32)
        zero = jnp.zeros((1, count, SPILL), jnp.float32)
        right = jnp.concatenate([zero, wide[:-1, :, outs : outs + SPILL]], 0)
        left = jnp.concatenate([wide[1:, :, outs + SPILL :], zero], 0)
        added = wide[:, :, :outs] + jnp.concatenate([right, none], 2) + jnp.concatenate([none, left], 2)
        got = added.transpose(1, 0, 2).reshape(count, samples)

    order = sorted(range(1, n_tgroup), key=lambda s: min(s, n_tgroup - s))
    arrived = [[] for _ in range(n_tgroup)]
    for group in range(2):
        if outs % LANES:
            use = [got]
        else:
            use = got[: n_chan // 2] if group == 0 else got
        vectors = samples // LANES // 2 + (1 if group else -1)
        packed = jax.ShapeDtypeStruct((-(-BLOCKS * vectors // 2), 2 * CB, LANES), jnp.bfloat16)
        sends = pl.pallas_call(
            functools.partial(place_kernel, n_chan, n_tgroup, outs, group),
            out_shape=(packed,) * n_tgroup,
            in_specs=[smem()] + [vmem()] * len(use),
            out_specs=(vmem(),) * n_tgroup,
            scratch_shapes=[
                pltpu.VMEM((count, samples), jnp.float32),
                pltpu.SMEM((n_tgroup * SLOTS,), jnp.int32),
            ],
            compiler_params=params(40),
            name="place_first" if group == 0 else "place_second",
        )(owners, *use)
        arrived[0].append(sends[0])
        for shift in order:
            route = [(g, (g + shift) % n_tgroup) for g in range(n_tgroup)]
            arrived[shift].append(lax.ppermute(sends[shift], "tgroup", route))

    value = None
    factor = 1.0 / math.sqrt(samples)
    for at, shift in enumerate([0] + order):
        last = at == n_tgroup - 1
        value = correlate(n_chan, owners, tuple(arrived[shift]), value, factor, last, samples)
    return value


def solution(mesh):
    in_specs = (P(("tgroup", "chan"), None), P(), P("chan"), P("chan", None))
    out_specs = P(("tgroup", "chan"), None, None, None)
    return jax.shard_map(local, mesh=mesh, in_specs=in_specs, out_specs=out_specs, check_vma=False)
```

```python
import functools
import math

import jax
import jax.numpy as jnp
from jax import lax
from jax.experimental import pallas as pl
from jax.experimental.pallas import tpu as pltpu
from jax.sharding import PartitionSpec as P

MAXLAG = 500
LAGS = 2 * MAXLAG + 1
TAPS = 255
CB = 8
K = 8
STRIPES = 2
SLOTS = 5
PAIRS = STRIPES * K
BLOCKS = STRIPES + SLOTS
WIDE = K * CB
SPILL = 64
LANES = 128
SHIFTS = 32
STEP = LANES // SHIFTS
LAG_BLOCKS = -(-LAGS // LANES)
FRONT = -(-MAXLAG // LANES) * LANES
NT = (((1,), (1,)), ((), ()))


def params(megabytes):
    return pltpu.CompilerParams(vmem_limit_bytes=megabytes << 20)


def vmem():
    return pl.BlockSpec(memory_space=pltpu.VMEM)


def smem():
    return pl.BlockSpec(memory_space=pltpu.SMEM)


def select_kernel(n_chan, firsts, raw, taps, *refs):
    sends, (window, picked, line, tap_sem, sems) = refs[:n_chan], refs[n_chan:]
    rows, channels = raw.shape
    outs = rows // 2
    stripes = n_chan * STRIPES
    blocks_per = channels // n_chan // CB
    span = window.shape[2]
    me = lax.axis_index("chan")

    def place(p):
        c, k = me ^ (p // STRIPES), p % STRIPES
        start = (firsts[c, k] + c * blocks_per) * CB
        base = jnp.minimum(start - lax.rem(start, LANES), channels - span)
        return start, pl.multiple_of(base, LANES)

    def copy(p):
        base = place(p)[1]
        return pltpu.make_async_copy(raw.at[:, pl.ds(base, span)], window.at[p], sems.at[p])

    line[...] = jnp.zeros_like(line)
    tap_copy = pltpu.make_async_copy(taps, line.at[0:1, : taps.shape[1]], tap_sem)
    tap_copy.start()
    for p in range(stripes):
        copy(p).start()

    width = line.shape[1]
    tap_copy.wait()
    spread = jnp.broadcast_to(line[0:1, :], (outs + 2 * SPILL, width))
    weights = pltpu.roll(spread, width - 4 * SPILL + 1, 1, stride=2, stride_axis=0)[:, :rows]
    weights = weights.astype(jnp.bfloat16)
    weights = jnp.concatenate(
        [weights[SPILL : SPILL + outs], weights[SPILL + outs :], weights[:SPILL]], 0
    )

    row = lax.broadcasted_iota(jnp.int32, (WIDE, span), 0)
    lane = lax.broadcasted_iota(jnp.int32, (WIDE, span), 1)
    batch = 2 * STRIPES
    for first in range(0, stripes, batch):
        for p in range(first, first + batch):
            copy(p).wait()
            start, base = place(p)
            hot = (lane == row + (start - base)) & (row < channels - start)
            hot = jnp.where(hot, 1.0, 0.0).astype(jnp.bfloat16)
            block = window[p].astype(jnp.bfloat16)
            chosen = lax.dot_general(hot, block, NT, preferred_element_type=jnp.float32)
            picked[p * WIDE : (p + 1) * WIDE, :] = chosen.astype(jnp.bfloat16)
        part = slice(first * WIDE, (first + batch) * WIDE)
        result = lax.dot_general(picked[part, :], weights, NT, preferred_element_type=jnp.float32)
        result = result.astype(jnp.bfloat16)
        for at in range(batch // STRIPES):
            sends[first // STRIPES + at][...] = result[at * STRIPES * WIDE : (at + 1) * STRIPES * WIDE]


def add_spills(n_chan, outs, got, total):
    count = total.shape[0]
    early = lax.broadcasted_iota(jnp.int32, (count, LANES), 1) < SPILL
    chunks = [lax.axis_index("chan") ^ k for k in range(n_chan)]
    for chunk, value in zip(chunks, got):
        at = pl.ds(pl.multiple_of(chunk * outs, LANES), outs)
        total[:, at] = value[:, :outs].astype(jnp.float32)
    for chunk, value in zip(chunks, got):
        spill = value[:, outs:].astype(jnp.float32)
        after = jnp.minimum(chunk + 1, n_chan - 1) * outs
        after = pl.ds(pl.multiple_of(after, LANES), LANES)
        total[:, after] += jnp.where(early & (chunk < n_chan - 1), spill, 0.0)
        before = jnp.maximum(chunk * outs, LANES) - LANES
        before = pl.ds(pl.multiple_of(before, LANES), LANES)
        total[:, before] += jnp.where(early | (chunk == 0), 0.0, spill)


def tile_of(group, width, vectors):
    half = vectors // 2
    if group == 0:
        return jnp.where(width == 0, 0, half + 1), half - 1
    return jnp.where(width == 0, half - 1, 0), half + 1


def own_half(n_chan):
    return jnp.where(lax.axis_index("chan") < n_chan // 2, 0, 1)


def place_kernel(n_chan, n_tgroup, outs, group, owners, *refs):
    total, pairs = refs[-2:]
    if group == 0:
        got, sends, me = refs[:-3], refs[-3], 0
    else:
        got, sends = refs[: -n_tgroup - 2], refs[-n_tgroup - 2 : -2]
        me = lax.axis_index("tgroup")
    if len(got) == 1:
        total[...] = got[0][...]
    else:
        add_spills(n_chan, outs, got, total)

    for at in range(n_tgroup * SLOTS):
        pairs[at] = -1
    counts = jnp.int32(0)
    for q in range(PAIRS):
        owner = owners[q]
        slot = (counts >> (3 * owner)) & 7
        counts = counts + (jnp.int32(1) << (3 * owner))
        pairs[lax.rem(owner - me + n_tgroup, n_tgroup) * SLOTS + slot] = q

    base, per = tile_of(group, own_half(n_chan), total.shape[1] // LANES)

    def tiles(q):
        rows = pl.ds(pl.multiple_of(q * CB, CB), CB)
        return [
            total[rows, pl.ds(pl.multiple_of((base + j) * LANES, LANES), LANES)] for j in range(per)
        ]

    zero = jnp.zeros((CB, LANES), jnp.float32)
    leads = sum([tiles(p * K) for p in range(STRIPES)], [])
    for shift in range(n_tgroup):
        parts = list(leads)
        for s in range(SLOTS):
            q = pairs[shift * SLOTS + s]
            parts += [jnp.where(q >= 0, tile, 0.0) for tile in tiles(jnp.maximum(q, 0))]
        parts += [zero] * (len(parts) % 2)
        for at in range(0, len(parts), 2):
            value = jnp.concatenate(parts[at : at + 2], 0)
            if group == 0:
                sends[shift, at // 2] = value.astype(jnp.bfloat16)
            else:
                sends[shift][at // 2] = value.astype(jnp.bfloat16)


def correlate_kernel(n_chan, n_tgroup, shift, factor, last, owners, *refs):
    lead, window_a, window_b, whole = refs[-4:]
    out = refs[-5]
    arrived, before = refs[:2], (refs[2] if len(refs) == 8 else None)
    windows = (window_a, window_b)
    span = lead.shape[2]
    samples = span - LANES
    cols = span // LANES
    high = STEP * CB
    ahead = FRONT // LANES - 1
    me = lax.axis_index("tgroup")
    first_count = jnp.int32(0)
    for q in range(K):
        first_count += jnp.where(owners[q] == me, 1, 0)

    source = lax.rem(lax.axis_index("tgroup") + n_tgroup - shift, n_tgroup)
    for group in range(2):
        base, per = tile_of(group, own_half(n_chan), samples // LANES)
        for at in range(arrived[group].shape[-3]):
            value = arrived[0][source, at] if group == 0 else arrived[1][at]
            value = value.astype(jnp.float32)
            for part in range(2):
                block, j = (2 * at + part) // per, (2 * at + part) % per
                if block < BLOCKS:
                    lanes = pl.ds(pl.multiple_of((base + j) * LANES, LANES), LANES)
                    whole[block, :, lanes] = value[part * CB : (part + 1) * CB]

    def series(block):
        return jnp.concatenate([whole[block], jnp.zeros((CB, LANES), jnp.float32)], 1)

    for p in range(STRIPES):
        value = series(p)
        for a in range(CB):
            spread = jnp.broadcast_to(value[a : a + 1], (SHIFTS, span))
            turned = pltpu.roll(spread, 0, 1, stride=1, stride_axis=0)
            lead[p, a * SHIFTS : (a + 1) * SHIFTS, :] = turned.astype(jnp.bfloat16)

    def bounds(i):
        return max(0, ahead - i), min(cols, ahead + cols - i)

    for window in windows:
        for i in range(LAG_BLOCKS):
            first, end = bounds(i)
            rows = slice(i * high, (i + 1) * high)
            if first > 0:
                window[rows, : first * LANES] = jnp.zeros((high, first * LANES), jnp.bfloat16)
            if end < cols:
                window[rows, end * LANES :] = jnp.zeros((high, (cols - end) * LANES), jnp.bfloat16)

    group = lax.broadcasted_iota(jnp.int32, (CB, LANES), 1) // SHIFTS
    for s in range(SLOTS):
        window = windows[s % 2]
        value = series(STRIPES + s)
        turned = [pltpu.roll(value, span - (FRONT - MAXLAG + SHIFTS * n), 1) for n in range(STEP)]
        stacked = jnp.concatenate(turned, 0).astype(jnp.bfloat16)
        stacked = jnp.concatenate([stacked[:, samples:], stacked[:, :samples]], 1)
        for i in range(LAG_BLOCKS):
            first, end = bounds(i)
            window[i * high : (i + 1) * high, first * LANES : end * LANES] = stacked[
                :, (first + i - ahead) * LANES : (end + i - ahead) * LANES
            ]
        which = jnp.where(s < first_count, 0, 1)
        summed = lax.dot_general(window[...], lead[which], NT, preferred_element_type=jnp.float32)
        if before is not None:
            summed = summed + before[s]
        if not last:
            out[s] = summed
            continue
        summed = summed * factor
        for i in range(LAG_BLOCKS):
            width = min(LANES, LAGS - i * LANES)
            for h in range(CB // STEP):
                parts = [
                    summed[(i * STEP + n) * CB : (i * STEP + n + 1) * CB, h * LANES : (h + 1) * LANES]
                    for n in range(STEP)
                ]
                for a in range(STEP):
                    value = parts[a]
                    for n in range(STEP):
                        if n != a:
                            moved = pltpu.roll(parts[n], (SHIFTS * (n - a)) % LANES, 1)
                            value = jnp.where(group == n, moved, value)
                    out[s, h * STEP + a, :, i * LANES : i * LANES + width] = value[:, :width]


def correlate(n_chan, n_tgroup, shift, owners, arrived, before, factor, last, samples):
    high, wide = STEP * LAG_BLOCKS * CB, CB * SHIFTS
    if last:
        shape = jax.ShapeDtypeStruct((SLOTS, CB, CB, LAGS), jnp.float32)
    else:
        shape = jax.ShapeDtypeStruct((SLOTS, high, wide), jnp.float32)
    operands = (owners,) + arrived + (() if before is None else (before,))
    return pl.pallas_call(
        functools.partial(correlate_kernel, n_chan, n_tgroup, shift, factor, last),
        out_shape=shape,
        in_specs=[smem()] + [vmem()] * (len(operands) - 1),
        out_specs=vmem(),
        scratch_shapes=[
            pltpu.VMEM((STRIPES, wide, samples + LANES), jnp.bfloat16),
            pltpu.VMEM((high, samples + LANES), jnp.bfloat16),
            pltpu.VMEM((high, samples + LANES), jnp.bfloat16),
            pltpu.VMEM((BLOCKS, CB, samples), jnp.float32),
        ],
        compiler_params=params(40),
        name="correlate_last" if last else "correlate",
    )(*operands)


def local(raw_strain, whitening_taps, first_block, pair_owner):
    n_chan, n_tgroup = lax.axis_size("chan"), lax.axis_size("tgroup")
    rows, channels = raw_strain.shape
    outs = rows // 2
    samples = outs * n_chan
    count = PAIRS * CB
    owners = pair_owner[:, 0]

    firsts = lax.all_to_all(
        jnp.broadcast_to(first_block[None, :], (n_chan, STRIPES)),
        "chan",
        split_axis=0,
        concat_axis=0,
        tiled=True,
    )
    line = -(-(rows + 2 * outs + 4 * SPILL) // (2 * LANES)) * 2 * LANES
    sends = pl.pallas_call(
        functools.partial(select_kernel, n_chan),
        out_shape=(jax.ShapeDtypeStruct((count, outs + 2 * SPILL), jnp.bfloat16),) * n_chan,
        in_specs=[smem(), pl.BlockSpec(memory_space=pl.ANY), pl.BlockSpec(memory_space=pl.ANY)],
        out_specs=(vmem(),) * n_chan,
        scratch_shapes=[
            pltpu.VMEM((n_chan * STRIPES, rows, 2 * LANES), jnp.float32),
            pltpu.VMEM((n_chan * count, rows), jnp.bfloat16),
            pltpu.VMEM((8, line), jnp.float32),
            pltpu.SemaphoreType.DMA,
            pltpu.SemaphoreType.DMA((n_chan * STRIPES,)),
        ],
        compiler_params=params(40),
        name="select_filter",
    )(firsts, raw_strain, jnp.pad(whitening_taps, (0, 1)).reshape(1, TAPS + 1))

    got = [sends[0]]
    for k in range(1, n_chan):
        got.append(lax.ppermute(sends[k], "chan", [(c, c ^ k) for c in range(n_chan)]))
    if outs % LANES:
        wide = jnp.stack(got).astype(jnp.float32)
        wide = jnp.take(wide, lax.axis_index("chan") ^ jnp.arange(n_chan), axis=0)
        none = jnp.zeros((n_chan, count, outs - SPILL), jnp.float32)
        zero = jnp.zeros((1, count, SPILL), jnp.float32)
        right = jnp.concatenate([zero, wide[:-1, :, outs : outs + SPILL]], 0)
        left = jnp.concatenate([wide[1:, :, outs + SPILL :], zero], 0)
        added = wide[:, :, :outs] + jnp.concatenate([right, none], 2) + jnp.concatenate([none, left], 2)
        got = added.transpose(1, 0, 2).reshape(count, samples)

    order = sorted(range(1, n_tgroup), key=lambda s: min(s, n_tgroup - s))
    for group in range(2):
        if outs % LANES:
            use = [got]
        else:
            use = got[: n_chan // 2] if group == 0 else got
        vectors = samples // LANES // 2 + (1 if group else -1)
        shape = (-(-BLOCKS * vectors // 2), 2 * CB, LANES)
        if group == 0:
            packed, specs = jax.ShapeDtypeStruct((n_tgroup,) + shape, jnp.bfloat16), vmem()
        else:
            packed, specs = (jax.ShapeDtypeStruct(shape, jnp.bfloat16),) * n_tgroup, (vmem(),) * n_tgroup
        sends = pl.pallas_call(
            functools.partial(place_kernel, n_chan, n_tgroup, outs, group),
            out_shape=packed,
            in_specs=[smem()] + [vmem()] * len(use),
            out_specs=specs,
            scratch_shapes=[
                pltpu.VMEM((count, samples), jnp.float32),
                pltpu.SMEM((n_tgroup * SLOTS,), jnp.int32),
            ],
            compiler_params=params(40),
            name="place_first" if group == 0 else "place_second",
        )(owners, *use)
        if group == 0:
            moved = lax.all_to_all(sends, "tgroup", split_axis=0, concat_axis=0, tiled=True)
            arrived = [[sends]] + [[moved] for _ in order]
            continue
        arrived[0].append(sends[0])
        for shift in order:
            route = [(g, (g + shift) % n_tgroup) for g in range(n_tgroup)]
            arrived[shift].append(lax.ppermute(sends[shift], "tgroup", route))

    value = None
    factor = 1.0 / math.sqrt(samples)
    for at, shift in enumerate([0] + order):
        last = at == n_tgroup - 1
        operands = (owners, tuple(arrived[shift]), value)
        value = correlate(n_chan, n_tgroup, shift, *operands, factor, last, samples)
    return value


def solution(mesh):
    in_specs = (P(("tgroup", "chan"), None), P(), P("chan"), P("chan", None))
    out_specs = P(("tgroup", "chan"), None, None, None)
    return jax.shard_map(local, mesh=mesh, in_specs=in_specs, out_specs=out_specs, check_vma=False)
```

```python
import functools
import math

import jax
import jax.numpy as jnp
from jax import lax
from jax.experimental import pallas as pl
from jax.experimental.pallas import tpu as pltpu
from jax.sharding import PartitionSpec as P

MAXLAG = 500
LAGS = 2 * MAXLAG + 1
TAPS = 255
CB = 8
K = 8
STRIPES = 2
SLOTS = 5
PAIRS = STRIPES * K
BLOCKS = STRIPES + SLOTS
WIDE = K * CB
SPILL = 64
LANES = 128
SHIFTS = 32
STEP = LANES // SHIFTS
LAG_BLOCKS = -(-LAGS // LANES)
FRONT = -(-MAXLAG // LANES) * LANES
NT = (((1,), (1,)), ((), ()))


def params(megabytes):
    return pltpu.CompilerParams(vmem_limit_bytes=megabytes << 20)


def vmem():
    return pl.BlockSpec(memory_space=pltpu.VMEM)


def smem():
    return pl.BlockSpec(memory_space=pltpu.SMEM)


def weights_kernel(taps, weights, held, line, sem):
    copy = pltpu.make_async_copy(taps, held, sem)
    copy.start()
    rows, outs, width = weights.shape[1], weights.shape[0] - 2 * SPILL, line.shape[1]
    line[...] = jnp.zeros_like(line)
    copy.wait()
    line[0:1, :TAPS] = held[...]
    spread = jnp.broadcast_to(line[0:1, :], (outs + 2 * SPILL, width))
    value = pltpu.roll(spread, width - 4 * SPILL + 1, 1, stride=2, stride_axis=0)[:, :rows]
    value = value.astype(jnp.bfloat16)
    weights[:outs, :] = value[SPILL : SPILL + outs]
    weights[outs : outs + SPILL, :] = value[SPILL + outs :]
    weights[outs + SPILL :, :] = value[:SPILL]


def select_kernel(n_chan, groups, firsts, raw, weights, *refs):
    sends, (window, picked, sems) = refs[: len(groups)], refs[len(groups) :]
    rows, channels = raw.shape
    steps = [k for group in groups for k in group]
    stripes = n_chan * STRIPES
    blocks_per = channels // n_chan // CB
    span = window.shape[2]
    me = lax.axis_index("chan")

    def place(p):
        c, k = me ^ steps[p // STRIPES], p % STRIPES
        start = (firsts[c, k] + c * blocks_per) * CB
        base = jnp.minimum(start - lax.rem(start, LANES), channels - span)
        return start, pl.multiple_of(base, LANES)

    def copy(p):
        base = place(p)[1]
        return pltpu.make_async_copy(raw.at[:, pl.ds(base, span)], window.at[p], sems.at[p])

    for p in range(stripes):
        copy(p).start()

    row = lax.broadcasted_iota(jnp.int32, (WIDE, span), 0)
    lane = lax.broadcasted_iota(jnp.int32, (WIDE, span), 1)
    batch = 2 * STRIPES
    for first in range(0, stripes, batch):
        for p in range(first, first + batch):
            copy(p).wait()
            start, base = place(p)
            hot = (lane == row + (start - base)) & (row < channels - start)
            hot = jnp.where(hot, 1.0, 0.0).astype(jnp.bfloat16)
            block = window[p].astype(jnp.bfloat16)
            chosen = lax.dot_general(hot, block, NT, preferred_element_type=jnp.float32)
            picked[p * WIDE : (p + 1) * WIDE, :] = chosen.astype(jnp.bfloat16)
        part = slice(first * WIDE, (first + batch) * WIDE)
        result = lax.dot_general(
            picked[part, :], weights[...], NT, preferred_element_type=jnp.float32
        ).astype(jnp.bfloat16)
        height = STRIPES * WIDE
        for at in range(batch // STRIPES):
            k = steps[first // STRIPES + at]
            out, where = [(o, g.index(k)) for o, g in enumerate(groups) if k in g][0]
            sends[out][where * height : (where + 1) * height, :] = result[at * height : (at + 1) * height]


def add_spills(n_chan, outs, steps, got, total):
    count = total.shape[0]
    early = lax.broadcasted_iota(jnp.int32, (count, LANES), 1) < SPILL
    me = lax.axis_index("chan")
    pieces = [
        (me ^ k, ref.at[at * count : (at + 1) * count])
        for ks, ref in zip(steps, got)
        for at, k in enumerate(ks)
    ]
    for chunk, value in pieces:
        at = pl.ds(pl.multiple_of(chunk * outs, LANES), outs)
        total[:, at] = value[:, :outs].astype(jnp.float32)
    for chunk, value in pieces:
        spill = value[:, outs:].astype(jnp.float32)
        after = jnp.minimum(chunk + 1, n_chan - 1) * outs
        after = pl.ds(pl.multiple_of(after, LANES), LANES)
        total[:, after] += jnp.where(early & (chunk < n_chan - 1), spill, 0.0)
        before = jnp.maximum(chunk * outs, LANES) - LANES
        before = pl.ds(pl.multiple_of(before, LANES), LANES)
        total[:, before] += jnp.where(early | (chunk == 0), 0.0, spill)


def tile_of(group, width, vectors):
    half = vectors // 2
    if group == 0:
        return jnp.where(width == 0, 0, half + 1), half - 1
    return jnp.where(width == 0, half - 1, 0), half + 1


def own_half(n_chan):
    return jnp.where(lax.axis_index("chan") < n_chan // 2, 0, 1)


def place_kernel(n_chan, n_tgroup, outs, group, steps, owners, *refs):
    got, (total, pairs) = refs[: -n_tgroup - 2], refs[-2:]
    sends = refs[-n_tgroup - 2 : -2]
    me = lax.axis_index("tgroup")
    if len(got) == 1:
        total[...] = got[0][...]
    else:
        add_spills(n_chan, outs, steps, got, total)

    for at in range(n_tgroup * SLOTS):
        pairs[at] = -1
    counts = jnp.int32(0)
    for q in range(PAIRS):
        owner = owners[q]
        slot = (counts >> (3 * owner)) & 7
        counts = counts + (jnp.int32(1) << (3 * owner))
        pairs[lax.rem(owner - me + n_tgroup, n_tgroup) * SLOTS + slot] = q

    base, per = tile_of(group, own_half(n_chan), total.shape[1] // LANES)

    def tiles(q):
        rows = pl.ds(pl.multiple_of(q * CB, CB), CB)
        return [
            total[rows, pl.ds(pl.multiple_of((base + j) * LANES, LANES), LANES)] for j in range(per)
        ]

    zero = jnp.zeros((CB, LANES), jnp.float32)
    leads = sum([tiles(p * K) for p in range(STRIPES)], [])
    for shift in range(n_tgroup):
        parts = list(leads)
        for s in range(SLOTS):
            q = pairs[shift * SLOTS + s]
            parts += [jnp.where(q >= 0, tile, 0.0) for tile in tiles(jnp.maximum(q, 0))]
        parts += [zero] * (len(parts) % 2)
        for at in range(0, len(parts), 2):
            value = jnp.concatenate(parts[at : at + 2], 0)
            sends[shift][at // 2] = value.astype(jnp.bfloat16)


def correlate_kernel(n_chan, factor, last, owners, *refs):
    lead, window_a, window_b, whole = refs[-4:]
    out = refs[-5]
    arrived, before = refs[:2], (refs[2] if len(refs) == 8 else None)
    windows = (window_a, window_b)
    span = lead.shape[2]
    samples = span - LANES
    cols = span // LANES
    high = STEP * CB
    ahead = FRONT // LANES - 1
    me = lax.axis_index("tgroup")
    first_count = jnp.int32(0)
    for q in range(K):
        first_count += jnp.where(owners[q] == me, 1, 0)

    for group in range(2):
        base, per = tile_of(group, own_half(n_chan), samples // LANES)
        for at in range(arrived[group].shape[0]):
            value = arrived[group][at].astype(jnp.float32)
            for part in range(2):
                block, j = (2 * at + part) // per, (2 * at + part) % per
                if block < BLOCKS:
                    lanes = pl.ds(pl.multiple_of((base + j) * LANES, LANES), LANES)
                    whole[block, :, lanes] = value[part * CB : (part + 1) * CB]

    def series(block):
        return jnp.concatenate([whole[block], jnp.zeros((CB, LANES), jnp.float32)], 1)

    for p in range(STRIPES):
        value = series(p)
        for a in range(CB):
            spread = jnp.broadcast_to(value[a : a + 1], (SHIFTS, span))
            turned = pltpu.roll(spread, 0, 1, stride=1, stride_axis=0)
            lead[p, a * SHIFTS : (a + 1) * SHIFTS, :] = turned.astype(jnp.bfloat16)

    def bounds(i):
        return max(0, ahead - i), min(cols, ahead + cols - i)

    for window in windows:
        for i in range(LAG_BLOCKS):
            first, end = bounds(i)
            rows = slice(i * high, (i + 1) * high)
            if first > 0:
                window[rows, : first * LANES] = jnp.zeros((high, first * LANES), jnp.bfloat16)
            if end < cols:
                window[rows, end * LANES :] = jnp.zeros((high, (cols - end) * LANES), jnp.bfloat16)

    group = lax.broadcasted_iota(jnp.int32, (CB, LANES), 1) // SHIFTS
    for s in range(SLOTS):
        window = windows[s % 2]
        value = series(STRIPES + s)
        turned = [pltpu.roll(value, span - (FRONT - MAXLAG + SHIFTS * n), 1) for n in range(STEP)]
        stacked = jnp.concatenate(turned, 0).astype(jnp.bfloat16)
        stacked = jnp.concatenate([stacked[:, samples:], stacked[:, :samples]], 1)
        for i in range(LAG_BLOCKS):
            first, end = bounds(i)
            window[i * high : (i + 1) * high, first * LANES : end * LANES] = stacked[
                :, (first + i - ahead) * LANES : (end + i - ahead) * LANES
            ]
        which = jnp.where(s < first_count, 0, 1)
        summed = lax.dot_general(window[...], lead[which], NT, preferred_element_type=jnp.float32)
        if before is not None:
            summed = summed + before[s]
        if not last:
            out[s] = summed
            continue
        summed = summed * factor
        for i in range(LAG_BLOCKS):
            width = min(LANES, LAGS - i * LANES)
            for h in range(CB // STEP):
                parts = [
                    summed[(i * STEP + n) * CB : (i * STEP + n + 1) * CB, h * LANES : (h + 1) * LANES]
                    for n in range(STEP)
                ]
                for a in range(STEP):
                    value = parts[a]
                    for n in range(STEP):
                        if n != a:
                            moved = pltpu.roll(parts[n], (SHIFTS * (n - a)) % LANES, 1)
                            value = jnp.where(group == n, moved, value)
                    out[s, h * STEP + a, :, i * LANES : i * LANES + width] = value[:, :width]


def correlate(n_chan, owners, arrived, before, factor, last, samples):
    high, wide = STEP * LAG_BLOCKS * CB, CB * SHIFTS
    if last:
        shape = jax.ShapeDtypeStruct((SLOTS, CB, CB, LAGS), jnp.float32)
    else:
        shape = jax.ShapeDtypeStruct((SLOTS, high, wide), jnp.float32)
    operands = (owners,) + arrived + (() if before is None else (before,))
    return pl.pallas_call(
        functools.partial(correlate_kernel, n_chan, factor, last),
        out_shape=shape,
        in_specs=[smem()] + [vmem()] * (len(operands) - 1),
        out_specs=vmem(),
        scratch_shapes=[
            pltpu.VMEM((STRIPES, wide, samples + LANES), jnp.bfloat16),
            pltpu.VMEM((high, samples + LANES), jnp.bfloat16),
            pltpu.VMEM((high, samples + LANES), jnp.bfloat16),
            pltpu.VMEM((BLOCKS, CB, samples), jnp.float32),
        ],
        compiler_params=params(40),
        name="correlate_last" if last else "correlate",
    )(*operands)


def local(raw_strain, whitening_taps, first_block, pair_owner):
    n_chan, n_tgroup = lax.axis_size("chan"), lax.axis_size("tgroup")
    rows, channels = raw_strain.shape
    outs = rows // 2
    samples = outs * n_chan
    count = PAIRS * CB
    owners = pair_owner[:, 0]

    firsts = lax.all_to_all(
        jnp.broadcast_to(first_block[None, :], (n_chan, STRIPES)),
        "chan",
        split_axis=0,
        concat_axis=0,
        tiled=True,
    )
    line = -(-(rows + 2 * outs + 4 * SPILL) // (2 * LANES)) * 2 * LANES
    weights = pl.pallas_call(
        weights_kernel,
        out_shape=jax.ShapeDtypeStruct((outs + 2 * SPILL, rows), jnp.bfloat16),
        in_specs=[pl.BlockSpec(memory_space=pl.ANY)],
        out_specs=vmem(),
        scratch_shapes=[
            pltpu.VMEM((1, TAPS), jnp.float32),
            pltpu.VMEM((8, line), jnp.float32),
            pltpu.SemaphoreType.DMA,
        ],
        compiler_params=params(40),
        name="fir_weights",
    )(whitening_taps.reshape(1, TAPS))

    relayed = n_chan == 8 and outs % LANES == 0
    groups = [[2], [3], [1, 5, 7], [4], [6], [0]] if relayed else [[k] for k in range(n_chan)]
    sends = pl.pallas_call(
        functools.partial(select_kernel, n_chan, groups),
        out_shape=[
            jax.ShapeDtypeStruct((len(group) * count, outs + 2 * SPILL), jnp.bfloat16)
            for group in groups
        ],
        in_specs=[smem(), pl.BlockSpec(memory_space=pl.ANY), vmem()],
        out_specs=[vmem()] * len(groups),
        scratch_shapes=[
            pltpu.VMEM((n_chan * STRIPES, rows, 2 * LANES), jnp.float32),
            pltpu.VMEM((n_chan * count, rows), jnp.bfloat16),
            pltpu.SemaphoreType.DMA((n_chan * STRIPES,)),
        ],
        compiler_params=params(40),
        name="select_filter",
    )(firsts, raw_strain, weights)

    def exchange(value, k):
        return lax.ppermute(value, "chan", [(c, c ^ k) for c in range(n_chan)])

    if relayed:
        got = [sends[5], exchange(sends[0], 2), exchange(sends[1], 3), exchange(sends[2], 1)]
        across = [
            jnp.concatenate([sends[3 + at], got[3][(1 + at) * count : (2 + at) * count]], 0)
            for at in range(2)
        ]
        across, got[1] = lax.optimization_barrier((across, got[1]))
        across = [exchange(value, 4 + 2 * at) for at, value in enumerate(across)]
        early, late = got, got + across
        early_steps, late_steps = [[0], [2], [3], [1]], [[0], [2], [3], [1], [4, 5], [6, 7]]
    else:
        got = [sends[0]] + [exchange(sends[k], k) for k in range(1, n_chan)]
        half = n_chan // 2
        early, late = got[:half], got
        early_steps, late_steps = [[k] for k in range(half)], [[k] for k in range(n_chan)]
    if outs % LANES:
        wide = jnp.stack(got).astype(jnp.float32)
        wide = jnp.take(wide, lax.axis_index("chan") ^ jnp.arange(n_chan), axis=0)
        none = jnp.zeros((n_chan, count, outs - SPILL), jnp.float32)
        zero = jnp.zeros((1, count, SPILL), jnp.float32)
        right = jnp.concatenate([zero, wide[:-1, :, outs : outs + SPILL]], 0)
        left = jnp.concatenate([wide[1:, :, outs + SPILL :], zero], 0)
        added = wide[:, :, :outs] + jnp.concatenate([right, none], 2) + jnp.concatenate([none, left], 2)
        early = late = [added.transpose(1, 0, 2).reshape(count, samples)]

    order = sorted(range(1, n_tgroup), key=lambda s: min(s, n_tgroup - s))
    arrived = [[] for _ in range(n_tgroup)]
    for group in range(2):
        use, steps = (early, early_steps) if group == 0 else (late, late_steps)
        vectors = samples // LANES // 2 + (1 if group else -1)
        packed = jax.ShapeDtypeStruct((-(-BLOCKS * vectors // 2), 2 * CB, LANES), jnp.bfloat16)
        sends = pl.pallas_call(
            functools.partial(place_kernel, n_chan, n_tgroup, outs, group, steps),
            out_shape=(packed,) * n_tgroup,
            in_specs=[smem()] + [vmem()] * len(use),
            out_specs=(vmem(),) * n_tgroup,
            scratch_shapes=[
                pltpu.VMEM((count, samples), jnp.float32),
                pltpu.SMEM((n_tgroup * SLOTS,), jnp.int32),
            ],
            compiler_params=params(40),
            name="place_first" if group == 0 else "place_second",
        )(owners, *use)
        arrived[0].append(sends[0])
        for at, shift in enumerate(order):
            route = [(g, (g + shift) % n_tgroup) for g in range(n_tgroup)]
            value = sends[shift]
            if group == 1:
                value, arrived[shift][0] = lax.optimization_barrier((value, arrived[shift][0]))
            arrived[shift].append(lax.ppermute(value, "tgroup", route))

    value = None
    factor = 1.0 / math.sqrt(samples)
    for at, shift in enumerate([0] + order):
        last = at == n_tgroup - 1
        value = correlate(n_chan, owners, tuple(arrived[shift]), value, factor, last, samples)
    return value


def solution(mesh):
    in_specs = (P(("tgroup", "chan"), None), P(), P("chan"), P("chan", None))
    out_specs = P(("tgroup", "chan"), None, None, None)
    return jax.shard_map(local, mesh=mesh, in_specs=in_specs, out_specs=out_specs, check_vma=False)
```

```python
import functools
import math

import jax
import jax.numpy as jnp
from jax import lax
from jax.experimental import pallas as pl
from jax.experimental.pallas import tpu as pltpu
from jax.sharding import PartitionSpec as P

MAXLAG = 500
LAGS = 2 * MAXLAG + 1
TAPS = 255
CB = 8
K = 8
STRIPES = 2
SLOTS = 5
PAIRS = STRIPES * K
BLOCKS = STRIPES + SLOTS
WIDE = K * CB
SPILL = 64
LANES = 128
SHIFTS = 32
STEP = LANES // SHIFTS
LAG_BLOCKS = -(-LAGS // LANES)
FRONT = -(-MAXLAG // LANES) * LANES
NT = (((1,), (1,)), ((), ()))


def params(megabytes):
    return pltpu.CompilerParams(vmem_limit_bytes=megabytes << 20)


def vmem():
    return pl.BlockSpec(memory_space=pltpu.VMEM)


def smem():
    return pl.BlockSpec(memory_space=pltpu.SMEM)


def weights_kernel(taps, weights, held, line, sem):
    copy = pltpu.make_async_copy(taps, held, sem)
    copy.start()
    rows, outs, width = weights.shape[1], weights.shape[0] - 2 * SPILL, line.shape[1]
    line[...] = jnp.zeros_like(line)
    copy.wait()
    line[0:1, :TAPS] = held[...]
    spread = jnp.broadcast_to(line[0:1, :], (outs + 2 * SPILL, width))
    value = pltpu.roll(spread, width - 4 * SPILL + 1, 1, stride=2, stride_axis=0)[:, :rows]
    value = value.astype(jnp.bfloat16)
    weights[:outs, :] = value[SPILL : SPILL + outs]
    weights[outs : outs + SPILL, :] = value[SPILL + outs :]
    weights[outs + SPILL :, :] = value[:SPILL]


def select_kernel(n_chan, groups, firsts, raw, weights, *refs):
    sends, (window, picked, sems) = refs[: len(groups)], refs[len(groups) :]
    rows, channels = raw.shape
    steps = [k for group in groups for k in group]
    stripes = len(steps) * STRIPES
    blocks_per = channels // n_chan // CB
    span = window.shape[2]
    me = lax.axis_index("chan")

    def place(p):
        c, k = me ^ steps[p // STRIPES], p % STRIPES
        start = (firsts[c, k] + c * blocks_per) * CB
        offset = lax.rem(start, LANES)
        base = pl.multiple_of(start - offset, LANES)
        return start, offset, base, (offset > LANES - WIDE) & (base < channels - LANES)

    def copy(p, tile):
        base = place(p)[2]
        if tile:
            base = pl.multiple_of(jnp.minimum(base + LANES, channels - LANES), LANES)
        return pltpu.make_async_copy(
            raw.at[:, pl.ds(base, LANES)],
            window.at[p, :, pl.ds(tile * LANES, LANES)],
            sems.at[p, tile],
        )

    for p in range(stripes):
        copy(p, 0).start()

        @pl.when(place(p)[3])
        def _(p=p):
            copy(p, 1).start()

    row = lax.broadcasted_iota(jnp.int32, (WIDE, span), 0)
    lane = lax.broadcasted_iota(jnp.int32, (WIDE, span), 1)
    batch = 2 * STRIPES
    for first in range(0, stripes, batch):
        for p in range(first, first + batch):
            start, offset, _, both = place(p)
            copy(p, 0).wait()

            @pl.when(both)
            def _(p=p):
                copy(p, 1).wait()

            @pl.when(jnp.logical_not(both))
            def _(p=p):
                window[p, :, LANES:] = jnp.zeros((rows, LANES), jnp.float32)

            hot = (lane == row + offset) & (row < channels - start)
            hot = jnp.where(hot, 1.0, 0.0).astype(jnp.bfloat16)
            block = window[p].astype(jnp.bfloat16)
            chosen = lax.dot_general(hot, block, NT, preferred_element_type=jnp.float32)
            picked[p * WIDE : (p + 1) * WIDE, :] = chosen.astype(jnp.bfloat16)
        part = slice(first * WIDE, (first + batch) * WIDE)
        result = lax.dot_general(
            picked[part, :], weights[...], NT, preferred_element_type=jnp.float32
        ).astype(jnp.bfloat16)
        height = STRIPES * WIDE
        for at in range(batch // STRIPES):
            k = steps[first // STRIPES + at]
            out, where = [(o, g.index(k)) for o, g in enumerate(groups) if k in g][0]
            sends[out][where * height : (where + 1) * height, :] = result[at * height : (at + 1) * height]


def add_spills(n_chan, outs, steps, got, total):
    count = total.shape[0]
    early = lax.broadcasted_iota(jnp.int32, (count, LANES), 1) < SPILL
    me = lax.axis_index("chan")
    pieces = [
        (me ^ k, ref.at[at * count : (at + 1) * count])
        for ks, ref in zip(steps, got)
        for at, k in enumerate(ks)
    ]
    for chunk, value in pieces:
        at = pl.ds(pl.multiple_of(chunk * outs, LANES), outs)
        total[:, at] = value[:, :outs].astype(jnp.float32)
    for chunk, value in pieces:
        spill = value[:, outs:].astype(jnp.float32)
        after = jnp.minimum(chunk + 1, n_chan - 1) * outs
        after = pl.ds(pl.multiple_of(after, LANES), LANES)
        total[:, after] += jnp.where(early & (chunk < n_chan - 1), spill, 0.0)
        before = jnp.maximum(chunk * outs, LANES) - LANES
        before = pl.ds(pl.multiple_of(before, LANES), LANES)
        total[:, before] += jnp.where(early | (chunk == 0), 0.0, spill)


def tile_of(group, width, vectors):
    half = vectors // 2
    if group == 0:
        return jnp.where(width == 0, 0, half + 1), half - 1
    return jnp.where(width == 0, half - 1, 0), half + 1


def own_half(n_chan):
    return jnp.where(lax.axis_index("chan") < n_chan // 2, 0, 1)


def place_kernel(n_chan, n_tgroup, outs, group, steps, owners, *refs):
    got, (total, pairs) = refs[: -n_tgroup - 2], refs[-2:]
    sends = refs[-n_tgroup - 2 : -2]
    me = lax.axis_index("tgroup")
    if len(got) == 1:
        total[...] = got[0][...]
    else:
        add_spills(n_chan, outs, steps, got, total)

    for at in range(n_tgroup * SLOTS):
        pairs[at] = -1
    counts = jnp.int32(0)
    for q in range(PAIRS):
        owner = owners[q]
        slot = (counts >> (3 * owner)) & 7
        counts = counts + (jnp.int32(1) << (3 * owner))
        pairs[lax.rem(owner - me + n_tgroup, n_tgroup) * SLOTS + slot] = q

    base, per = tile_of(group, own_half(n_chan), total.shape[1] // LANES)

    def tiles(q):
        rows = pl.ds(pl.multiple_of(q * CB, CB), CB)
        return [
            total[rows, pl.ds(pl.multiple_of((base + j) * LANES, LANES), LANES)] for j in range(per)
        ]

    zero = jnp.zeros((CB, LANES), jnp.float32)
    leads = sum([tiles(p * K) for p in range(STRIPES)], [])
    for shift in range(n_tgroup):
        parts = list(leads)
        for s in range(SLOTS):
            q = pairs[shift * SLOTS + s]
            parts += [jnp.where(q >= 0, tile, 0.0) for tile in tiles(jnp.maximum(q, 0))]
        parts += [zero] * (len(parts) % 2)
        for at in range(0, len(parts), 2):
            value = jnp.concatenate(parts[at : at + 2], 0)
            sends[shift][at // 2] = value.astype(jnp.bfloat16)


def correlate_kernel(n_chan, factor, last, owners, *refs):
    lead, window_a, window_b, whole = refs[-4:]
    out = refs[-5]
    arrived, before = refs[:2], (refs[2] if len(refs) == 8 else None)
    windows = (window_a, window_b)
    span = lead.shape[2]
    samples = span - LANES
    cols = span // LANES
    high = STEP * CB
    ahead = FRONT // LANES - 1
    me = lax.axis_index("tgroup")
    first_count = jnp.int32(0)
    for q in range(K):
        first_count += jnp.where(owners[q] == me, 1, 0)

    for group in range(2):
        base, per = tile_of(group, own_half(n_chan), samples // LANES)
        for at in range(arrived[group].shape[0]):
            value = arrived[group][at].astype(jnp.float32)
            for part in range(2):
                block, j = (2 * at + part) // per, (2 * at + part) % per
                if block < BLOCKS:
                    lanes = pl.ds(pl.multiple_of((base + j) * LANES, LANES), LANES)
                    whole[block, :, lanes] = value[part * CB : (part + 1) * CB]

    def series(block):
        return jnp.concatenate([whole[block], jnp.zeros((CB, LANES), jnp.float32)], 1)

    for p in range(STRIPES):
        value = series(p)
        for a in range(CB):
            spread = jnp.broadcast_to(value[a : a + 1], (SHIFTS, span))
            turned = pltpu.roll(spread, 0, 1, stride=1, stride_axis=0)
            lead[p, a * SHIFTS : (a + 1) * SHIFTS, :] = turned.astype(jnp.bfloat16)

    def bounds(i):
        return max(0, ahead - i), min(cols, ahead + cols - i)

    for window in windows:
        for i in range(LAG_BLOCKS):
            first, end = bounds(i)
            rows = slice(i * high, (i + 1) * high)
            if first > 0:
                window[rows, : first * LANES] = jnp.zeros((high, first * LANES), jnp.bfloat16)
            if end < cols:
                window[rows, end * LANES :] = jnp.zeros((high, (cols - end) * LANES), jnp.bfloat16)

    group = lax.broadcasted_iota(jnp.int32, (CB, LANES), 1) // SHIFTS
    for s in range(SLOTS):
        window = windows[s % 2]
        value = series(STRIPES + s)
        turned = [pltpu.roll(value, span - (FRONT - MAXLAG + SHIFTS * n), 1) for n in range(STEP)]
        stacked = jnp.concatenate(turned, 0).astype(jnp.bfloat16)
        stacked = jnp.concatenate([stacked[:, samples:], stacked[:, :samples]], 1)
        for i in range(LAG_BLOCKS):
            first, end = bounds(i)
            window[i * high : (i + 1) * high, first * LANES : end * LANES] = stacked[
                :, (first + i - ahead) * LANES : (end + i - ahead) * LANES
            ]
        which = jnp.where(s < first_count, 0, 1)
        summed = lax.dot_general(window[...], lead[which], NT, preferred_element_type=jnp.float32)
        if before is not None:
            summed = summed + before[s]
        if not last:
            out[s] = summed
            continue
        summed = summed * factor
        for i in range(LAG_BLOCKS):
            width = min(LANES, LAGS - i * LANES)
            for h in range(CB // STEP):
                parts = [
                    summed[(i * STEP + n) * CB : (i * STEP + n + 1) * CB, h * LANES : (h + 1) * LANES]
                    for n in range(STEP)
                ]
                for a in range(STEP):
                    value = parts[a]
                    for n in range(STEP):
                        if n != a:
                            moved = pltpu.roll(parts[n], (SHIFTS * (n - a)) % LANES, 1)
                            value = jnp.where(group == n, moved, value)
                    out[s, h * STEP + a, :, i * LANES : i * LANES + width] = value[:, :width]


def correlate(n_chan, owners, arrived, before, factor, last, samples):
    high, wide = STEP * LAG_BLOCKS * CB, CB * SHIFTS
    if last:
        shape = jax.ShapeDtypeStruct((SLOTS, CB, CB, LAGS), jnp.float32)
    else:
        shape = jax.ShapeDtypeStruct((SLOTS, high, wide), jnp.float32)
    operands = (owners,) + arrived + (() if before is None else (before,))
    return pl.pallas_call(
        functools.partial(correlate_kernel, n_chan, factor, last),
        out_shape=shape,
        in_specs=[smem()] + [vmem()] * (len(operands) - 1),
        out_specs=vmem(),
        scratch_shapes=[
            pltpu.VMEM((STRIPES, wide, samples + LANES), jnp.bfloat16),
            pltpu.VMEM((high, samples + LANES), jnp.bfloat16),
            pltpu.VMEM((high, samples + LANES), jnp.bfloat16),
            pltpu.VMEM((BLOCKS, CB, samples), jnp.float32),
        ],
        compiler_params=params(40),
        name="correlate_last" if last else "correlate",
    )(*operands)


def local(raw_strain, whitening_taps, first_block, pair_owner):
    n_chan, n_tgroup = lax.axis_size("chan"), lax.axis_size("tgroup")
    rows, channels = raw_strain.shape
    outs = rows // 2
    samples = outs * n_chan
    count = PAIRS * CB
    owners = pair_owner[:, 0]

    firsts = lax.all_to_all(
        jnp.broadcast_to(first_block[None, :], (n_chan, STRIPES)),
        "chan",
        split_axis=0,
        concat_axis=0,
        tiled=True,
    )
    line = -(-(rows + 2 * outs + 4 * SPILL) // (2 * LANES)) * 2 * LANES
    weights = pl.pallas_call(
        weights_kernel,
        out_shape=jax.ShapeDtypeStruct((outs + 2 * SPILL, rows), jnp.bfloat16),
        in_specs=[pl.BlockSpec(memory_space=pl.ANY)],
        out_specs=vmem(),
        scratch_shapes=[
            pltpu.VMEM((1, TAPS), jnp.float32),
            pltpu.VMEM((8, line), jnp.float32),
            pltpu.SemaphoreType.DMA,
        ],
        compiler_params=params(40),
        name="fir_weights",
    )(whitening_taps.reshape(1, TAPS))

    relayed = n_chan == 8 and outs % LANES == 0
    if relayed:
        parts = [[[2], [3]], [[1, 5, 7], [4], [6], [0]]]
    else:
        parts = [[[k] for k in range(n_chan)]]
    sends = []
    for groups in parts:
        steps = sum(len(group) for group in groups)
        sends += pl.pallas_call(
            functools.partial(select_kernel, n_chan, groups),
            out_shape=[
                jax.ShapeDtypeStruct((len(group) * count, outs + 2 * SPILL), jnp.bfloat16)
                for group in groups
            ],
            in_specs=[smem(), pl.BlockSpec(memory_space=pl.ANY), vmem()],
            out_specs=[vmem()] * len(groups),
            scratch_shapes=[
                pltpu.VMEM((steps * STRIPES, rows, 2 * LANES), jnp.float32),
                pltpu.VMEM((steps * count, rows), jnp.bfloat16),
                pltpu.SemaphoreType.DMA((steps * STRIPES, 2)),
            ],
            compiler_params=params(40),
            name="select_filter",
        )(firsts, raw_strain, weights)
        weights, sends = lax.optimization_barrier((weights, sends))

    def exchange(value, k):
        return lax.ppermute(value, "chan", [(c, c ^ k) for c in range(n_chan)])

    if relayed:
        near = exchange(sends[0], 2)
        handed, near = lax.optimization_barrier((sends[2], near))
        got = [sends[5], near, exchange(sends[1], 3), exchange(handed, 1)]
        across = [
            jnp.concatenate([sends[3 + at], got[3][(1 + at) * count : (2 + at) * count]], 0)
            for at in range(2)
        ]
        across, got[1] = lax.optimization_barrier((across, got[1]))
        across = [exchange(value, 4 + 2 * at) for at, value in enumerate(across)]
        early, late = got, got + across
        early_steps, late_steps = [[0], [2], [3], [1]], [[0], [2], [3], [1], [4, 5], [6, 7]]
    else:
        got = [sends[0]] + [exchange(sends[k], k) for k in range(1, n_chan)]
        half = n_chan // 2
        early, late = got[:half], got
        early_steps, late_steps = [[k] for k in range(half)], [[k] for k in range(n_chan)]
    if outs % LANES:
        wide = jnp.stack(got).astype(jnp.float32)
        wide = jnp.take(wide, lax.axis_index("chan") ^ jnp.arange(n_chan), axis=0)
        none = jnp.zeros((n_chan, count, outs - SPILL), jnp.float32)
        zero = jnp.zeros((1, count, SPILL), jnp.float32)
        right = jnp.concatenate([zero, wide[:-1, :, outs : outs + SPILL]], 0)
        left = jnp.concatenate([wide[1:, :, outs + SPILL :], zero], 0)
        added = wide[:, :, :outs] + jnp.concatenate([right, none], 2) + jnp.concatenate([none, left], 2)
        early = late = [added.transpose(1, 0, 2).reshape(count, samples)]

    order = sorted(range(1, n_tgroup), key=lambda s: min(s, n_tgroup - s))
    arrived = [[] for _ in range(n_tgroup)]
    for group in range(2):
        use, steps = (early, early_steps) if group == 0 else (late, late_steps)
        vectors = samples // LANES // 2 + (1 if group else -1)
        packed = jax.ShapeDtypeStruct((-(-BLOCKS * vectors // 2), 2 * CB, LANES), jnp.bfloat16)
        sends = pl.pallas_call(
            functools.partial(place_kernel, n_chan, n_tgroup, outs, group, steps),
            out_shape=(packed,) * n_tgroup,
            in_specs=[smem()] + [vmem()] * len(use),
            out_specs=(vmem(),) * n_tgroup,
            scratch_shapes=[
                pltpu.VMEM((count, samples), jnp.float32),
                pltpu.SMEM((n_tgroup * SLOTS,), jnp.int32),
            ],
            compiler_params=params(40),
            name="place_first" if group == 0 else "place_second",
        )(owners, *use)
        arrived[0].append(sends[0])
        for at, shift in enumerate(order):
            route = [(g, (g + shift) % n_tgroup) for g in range(n_tgroup)]
            value = sends[shift]
            if group == 1:
                value, arrived[shift][0] = lax.optimization_barrier((value, arrived[shift][0]))
            arrived[shift].append(lax.ppermute(value, "tgroup", route))

    value = None
    factor = 1.0 / math.sqrt(samples)
    for at, shift in enumerate([0] + order):
        last = at == n_tgroup - 1
        value = correlate(n_chan, owners, tuple(arrived[shift]), value, factor, last, samples)
    return value


def solution(mesh):
    in_specs = (P(("tgroup", "chan"), None), P(), P("chan"), P("chan", None))
    out_specs = P(("tgroup", "chan"), None, None, None)
    return jax.shard_map(local, mesh=mesh, in_specs=in_specs, out_specs=out_specs, check_vma=False)
```

```python
import functools
import math

import jax
import jax.numpy as jnp
from jax import lax
from jax.experimental import pallas as pl
from jax.experimental.pallas import tpu as pltpu
from jax.sharding import PartitionSpec as P

MAXLAG = 500
LAGS = 2 * MAXLAG + 1
TAPS = 255
CB = 8
K = 8
STRIPES = 2
SLOTS = 5
PAIRS = STRIPES * K
BLOCKS = STRIPES + SLOTS
WIDE = K * CB
SPILL = 64
LANES = 128
SHIFTS = 32
STEP = LANES // SHIFTS
LAG_BLOCKS = -(-LAGS // LANES)
FRONT = -(-MAXLAG // LANES) * LANES


def params(megabytes):
    return pltpu.CompilerParams(vmem_limit_bytes=megabytes << 20)


def vmem():
    return pl.BlockSpec(memory_space=pltpu.VMEM)


def smem():
    return pl.BlockSpec(memory_space=pltpu.SMEM)


def weights_kernel(taps, weights, held, line, sem):
    copy = pltpu.make_async_copy(taps, held, sem)
    copy.start()
    rows, outs, width = weights.shape[1], weights.shape[0] - 2 * SPILL, line.shape[1]
    line[...] = jnp.zeros_like(line)
    copy.wait()
    line[0:1, :TAPS] = held[...]
    spread = jnp.broadcast_to(line[0:1, :], (outs + 2 * SPILL, width))
    value = pltpu.roll(spread, width - 4 * SPILL + 1, 1, stride=2, stride_axis=0)[:, :rows]
    value = value.astype(jnp.bfloat16)
    weights[:outs, :] = value[SPILL : SPILL + outs]
    weights[outs : outs + SPILL, :] = value[SPILL + outs :]
    weights[outs + SPILL :, :] = value[:SPILL]


def select_kernel(n_chan, groups, firsts, raw, weights, *refs):
    sends, (window, sems) = refs[: len(groups)], refs[len(groups) :]
    rows, channels = raw.shape
    steps = [k for group in groups for k in group]
    stripes = n_chan * STRIPES
    blocks_per = channels // n_chan // CB
    span = window.shape[2]
    me = lax.axis_index("chan")

    def place(p):
        c, k = me ^ steps[p // STRIPES], p % STRIPES
        start = (firsts[c, k] + c * blocks_per) * CB
        base = jnp.minimum(start - lax.rem(start, LANES), channels - span)
        return start, pl.multiple_of(base, LANES)

    def copy(p):
        base = place(p)[1]
        return pltpu.make_async_copy(raw.at[:, pl.ds(base, span)], window.at[p], sems.at[p])

    for p in range(stripes):
        copy(p).start()

    row = lax.broadcasted_iota(jnp.int32, (span, STRIPES * WIDE), 0)
    column = lax.broadcasted_iota(jnp.int32, (span, STRIPES * WIDE), 1)
    height = STRIPES * WIDE
    for at, k in enumerate(steps):
        hots, blocks = [], []
        for i in range(STRIPES):
            p = at * STRIPES + i
            copy(p).wait()
            start, base = place(p)
            channel = column - i * WIDE
            hot = (row == channel + (start - base)) & (channel < channels - start)
            hot = hot & (channel >= 0) & (channel < WIDE)
            hots.append(jnp.where(hot, 1.0, 0.0).astype(jnp.bfloat16))
            blocks.append(window[p].astype(jnp.bfloat16))
        chosen = jnp.dot(
            jnp.concatenate(blocks, 1),
            jnp.concatenate(hots, 0),
            preferred_element_type=jnp.float32,
        )
        result = jnp.dot(
            weights[...], chosen.astype(jnp.bfloat16), preferred_element_type=jnp.float32
        )
        out, where = [(o, g.index(k)) for o, g in enumerate(groups) if k in g][0]
        sends[out][where * height : (where + 1) * height, :] = result.T.astype(jnp.bfloat16)


def add_spills(n_chan, outs, steps, got, total):
    count = total.shape[0]
    early = lax.broadcasted_iota(jnp.int32, (count, LANES), 1) < SPILL
    me = lax.axis_index("chan")
    pieces = [
        (me ^ k, ref.at[at * count : (at + 1) * count])
        for ks, ref in zip(steps, got)
        for at, k in enumerate(ks)
    ]
    for chunk, value in pieces:
        at = pl.ds(pl.multiple_of(chunk * outs, LANES), outs)
        total[:, at] = value[:, :outs].astype(jnp.float32)
    for chunk, value in pieces:
        spill = value[:, outs:].astype(jnp.float32)
        after = jnp.minimum(chunk + 1, n_chan - 1) * outs
        after = pl.ds(pl.multiple_of(after, LANES), LANES)
        total[:, after] += jnp.where(early & (chunk < n_chan - 1), spill, 0.0)
        before = jnp.maximum(chunk * outs, LANES) - LANES
        before = pl.ds(pl.multiple_of(before, LANES), LANES)
        total[:, before] += jnp.where(early | (chunk == 0), 0.0, spill)


def tile_of(group, width, vectors):
    half = vectors // 2
    if group == 0:
        return jnp.where(width == 0, 0, half + 1), half - 1
    return jnp.where(width == 0, half - 1, 0), half + 1


def own_half(n_chan):
    return jnp.where(lax.axis_index("chan") < n_chan // 2, 0, 1)


def place_kernel(n_chan, n_tgroup, outs, group, steps, owners, *refs):
    got, (total, pairs) = refs[: -n_tgroup - 2], refs[-2:]
    sends = refs[-n_tgroup - 2 : -2]
    me = lax.axis_index("tgroup")
    if len(got) == 1:
        total[...] = got[0][...]
    else:
        add_spills(n_chan, outs, steps, got, total)

    for at in range(n_tgroup * SLOTS):
        pairs[at] = -1
    counts = jnp.int32(0)
    for q in range(PAIRS):
        owner = owners[q]
        slot = (counts >> (3 * owner)) & 7
        counts = counts + (jnp.int32(1) << (3 * owner))
        pairs[lax.rem(owner - me + n_tgroup, n_tgroup) * SLOTS + slot] = q

    base, per = tile_of(group, own_half(n_chan), total.shape[1] // LANES)

    def tiles(q):
        rows = pl.ds(pl.multiple_of(q * CB, CB), CB)
        return [
            total[rows, pl.ds(pl.multiple_of((base + j) * LANES, LANES), LANES)] for j in range(per)
        ]

    zero = jnp.zeros((CB, LANES), jnp.float32)
    leads = sum([tiles(p * K) for p in range(STRIPES)], [])
    for shift in range(n_tgroup):
        parts = list(leads)
        for s in range(SLOTS):
            q = pairs[shift * SLOTS + s]
            parts += [jnp.where(q >= 0, tile, 0.0) for tile in tiles(jnp.maximum(q, 0))]
        parts += [zero] * (len(parts) % 2)
        for at in range(0, len(parts), 2):
            value = jnp.concatenate(parts[at : at + 2], 0)
            sends[shift][at // 2] = value.astype(jnp.bfloat16)


def correlate_kernel(n_chan, factor, last, owners, *refs):
    lead, window_a, window_b, whole = refs[-4:]
    out = refs[-5]
    arrived, before = refs[:2], (refs[2] if len(refs) == 8 else None)
    windows = (window_a, window_b)
    span = lead.shape[1]
    samples = span - LANES
    cols = span // LANES
    high = STEP * CB
    ahead = FRONT // LANES - 1
    me = lax.axis_index("tgroup")
    first_count = jnp.int32(0)
    for q in range(K):
        first_count += jnp.where(owners[q] == me, 1, 0)

    for group in range(2):
        base, per = tile_of(group, own_half(n_chan), samples // LANES)
        for at in range(arrived[group].shape[0]):
            value = arrived[group][at].astype(jnp.float32)
            for part in range(2):
                block, j = (2 * at + part) // per, (2 * at + part) % per
                if block < BLOCKS:
                    lanes = pl.ds(pl.multiple_of((base + j) * LANES, LANES), LANES)
                    whole[block, :, lanes] = value[part * CB : (part + 1) * CB]

    def series(block):
        return jnp.concatenate([whole[block], jnp.zeros((CB, LANES), jnp.float32)], 1)

    for p in range(STRIPES):
        value = series(p)
        for first in range(0, CB, STEP):
            turned = [
                pltpu.roll(
                    jnp.broadcast_to(value[a : a + 1], (SHIFTS, span)), 0, 1, stride=1, stride_axis=0
                )
                for a in range(first, first + STEP)
            ]
            turned = jnp.concatenate(turned, 0).T.astype(jnp.bfloat16)
            lead[p, :, first * SHIFTS : (first + STEP) * SHIFTS] = turned

    def bounds(i):
        return max(0, ahead - i), min(cols, ahead + cols - i)

    for window in windows:
        for i in range(LAG_BLOCKS):
            first, end = bounds(i)
            rows = slice(i * high, (i + 1) * high)
            if first > 0:
                window[rows, : first * LANES] = jnp.zeros((high, first * LANES), jnp.bfloat16)
            if end < cols:
                window[rows, end * LANES :] = jnp.zeros((high, (cols - end) * LANES), jnp.bfloat16)

    lane = lax.broadcasted_iota(jnp.int32, (CB, LANES), 1)
    left, even = lane < 2 * SHIFTS, (lane // SHIFTS) % 2 == 0

    def swap(one, two, keep, by):
        return (
            jnp.where(keep, one, pltpu.roll(two, by, 1)),
            jnp.where(keep, pltpu.roll(one, LANES - by, 1), two),
        )

    for s in range(SLOTS):
        window = windows[s % 2]
        value = series(STRIPES + s)
        turned = [pltpu.roll(value, span - (FRONT - MAXLAG + SHIFTS * n), 1) for n in range(STEP)]
        stacked = jnp.concatenate(turned, 0).astype(jnp.bfloat16)
        stacked = jnp.concatenate([stacked[:, samples:], stacked[:, :samples]], 1)
        for i in range(LAG_BLOCKS):
            first, end = bounds(i)
            window[i * high : (i + 1) * high, first * LANES : end * LANES] = stacked[
                :, (first + i - ahead) * LANES : (end + i - ahead) * LANES
            ]
        which = jnp.where(s < first_count, 0, 1)
        summed = jnp.dot(window[...], lead[which], preferred_element_type=jnp.float32)
        if before is not None:
            summed = summed + before[s]
        if not last:
            out[s] = summed
            continue
        summed = summed * factor
        for i in range(LAG_BLOCKS):
            width = min(LANES, LAGS - i * LANES)
            for h in range(CB // STEP):
                parts = [
                    summed[i * high + n * CB : i * high + (n + 1) * CB, h * LANES : (h + 1) * LANES]
                    for n in range(STEP)
                ]
                parts[0], parts[2] = swap(parts[0], parts[2], left, 2 * SHIFTS)
                parts[1], parts[3] = swap(parts[1], parts[3], left, 2 * SHIFTS)
                parts[0], parts[1] = swap(parts[0], parts[1], even, SHIFTS)
                parts[2], parts[3] = swap(parts[2], parts[3], even, SHIFTS)
                for a in range(STEP):
                    out[s, h * STEP + a, :, i * LANES : i * LANES + width] = parts[a][:, :width]


def correlate(n_chan, owners, arrived, before, factor, last, samples):
    high, wide = STEP * LAG_BLOCKS * CB, CB * SHIFTS
    if last:
        shape = jax.ShapeDtypeStruct((SLOTS, CB, CB, LAGS), jnp.float32)
    else:
        shape = jax.ShapeDtypeStruct((SLOTS, high, wide), jnp.float32)
    operands = (owners,) + arrived + (() if before is None else (before,))
    return pl.pallas_call(
        functools.partial(correlate_kernel, n_chan, factor, last),
        out_shape=shape,
        in_specs=[smem()] + [vmem()] * (len(operands) - 1),
        out_specs=vmem(),
        scratch_shapes=[
            pltpu.VMEM((STRIPES, samples + LANES, wide), jnp.bfloat16),
            pltpu.VMEM((high, samples + LANES), jnp.bfloat16),
            pltpu.VMEM((high, samples + LANES), jnp.bfloat16),
            pltpu.VMEM((BLOCKS, CB, samples), jnp.float32),
        ],
        compiler_params=params(40),
        name="correlate_last" if last else "correlate",
    )(*operands)


def local(raw_strain, whitening_taps, first_block, pair_owner):
    n_chan, n_tgroup = lax.axis_size("chan"), lax.axis_size("tgroup")
    rows, channels = raw_strain.shape
    outs = rows // 2
    samples = outs * n_chan
    count = PAIRS * CB
    owners = pair_owner[:, 0]

    firsts = lax.all_to_all(
        jnp.broadcast_to(first_block[None, :], (n_chan, STRIPES)),
        "chan",
        split_axis=0,
        concat_axis=0,
        tiled=True,
    )
    line = -(-(rows + 2 * outs + 4 * SPILL) // (2 * LANES)) * 2 * LANES
    weights = pl.pallas_call(
        weights_kernel,
        out_shape=jax.ShapeDtypeStruct((outs + 2 * SPILL, rows), jnp.bfloat16),
        in_specs=[pl.BlockSpec(memory_space=pl.ANY)],
        out_specs=vmem(),
        scratch_shapes=[
            pltpu.VMEM((1, TAPS), jnp.float32),
            pltpu.VMEM((8, line), jnp.float32),
            pltpu.SemaphoreType.DMA,
        ],
        compiler_params=params(40),
        name="fir_weights",
    )(whitening_taps.reshape(1, TAPS))

    relayed = n_chan == 8 and outs % LANES == 0
    groups = [[2], [3], [1, 5, 7], [4], [6], [0]] if relayed else [[k] for k in range(n_chan)]
    sends = pl.pallas_call(
        functools.partial(select_kernel, n_chan, groups),
        out_shape=[
            jax.ShapeDtypeStruct((len(group) * count, outs + 2 * SPILL), jnp.bfloat16)
            for group in groups
        ],
        in_specs=[smem(), pl.BlockSpec(memory_space=pl.ANY), vmem()],
        out_specs=[vmem()] * len(groups),
        scratch_shapes=[
            pltpu.VMEM((n_chan * STRIPES, rows, 2 * LANES), jnp.float32),
            pltpu.SemaphoreType.DMA((n_chan * STRIPES,)),
        ],
        compiler_params=params(40),
        name="select_filter",
    )(firsts, raw_strain, weights)

    def exchange(value, k):
        return lax.ppermute(value, "chan", [(c, c ^ k) for c in range(n_chan)])

    if relayed:
        got = [sends[5], exchange(sends[0], 2), exchange(sends[1], 3), exchange(sends[2], 1)]
        across = [
            jnp.concatenate([sends[3 + at], got[3][(1 + at) * count : (2 + at) * count]], 0)
            for at in range(2)
        ]
        across, got[1] = lax.optimization_barrier((across, got[1]))
        across = [exchange(value, 4 + 2 * at) for at, value in enumerate(across)]
        early, late = got, got + across
        early_steps, late_steps = [[0], [2], [3], [1]], [[0], [2], [3], [1], [4, 5], [6, 7]]
    else:
        got = [sends[0]] + [exchange(sends[k], k) for k in range(1, n_chan)]
        half = n_chan // 2
        early, late = got[:half], got
        early_steps, late_steps = [[k] for k in range(half)], [[k] for k in range(n_chan)]
    if outs % LANES:
        wide = jnp.stack(got).astype(jnp.float32)
        wide = jnp.take(wide, lax.axis_index("chan") ^ jnp.arange(n_chan), axis=0)
        none = jnp.zeros((n_chan, count, outs - SPILL), jnp.float32)
        zero = jnp.zeros((1, count, SPILL), jnp.float32)
        right = jnp.concatenate([zero, wide[:-1, :, outs : outs + SPILL]], 0)
        left = jnp.concatenate([wide[1:, :, outs + SPILL :], zero], 0)
        added = wide[:, :, :outs] + jnp.concatenate([right, none], 2) + jnp.concatenate([none, left], 2)
        early = late = [added.transpose(1, 0, 2).reshape(count, samples)]

    order = sorted(range(1, n_tgroup), key=lambda s: min(s, n_tgroup - s))
    arrived = [[] for _ in range(n_tgroup)]
    for group in range(2):
        use, steps = (early, early_steps) if group == 0 else (late, late_steps)
        vectors = samples // LANES // 2 + (1 if group else -1)
        packed = jax.ShapeDtypeStruct((-(-BLOCKS * vectors // 2), 2 * CB, LANES), jnp.bfloat16)
        sends = pl.pallas_call(
            functools.partial(place_kernel, n_chan, n_tgroup, outs, group, steps),
            out_shape=(packed,) * n_tgroup,
            in_specs=[smem()] + [vmem()] * len(use),
            out_specs=(vmem(),) * n_tgroup,
            scratch_shapes=[
                pltpu.VMEM((count, samples), jnp.float32),
                pltpu.SMEM((n_tgroup * SLOTS,), jnp.int32),
            ],
            compiler_params=params(40),
            name="place_first" if group == 0 else "place_second",
        )(owners, *use)
        arrived[0].append(sends[0])
        for at, shift in enumerate(order):
            route = [(g, (g + shift) % n_tgroup) for g in range(n_tgroup)]
            value = sends[shift]
            if group == 1:
                value, arrived[shift][0] = lax.optimization_barrier((value, arrived[shift][0]))
            arrived[shift].append(lax.ppermute(value, "tgroup", route))

    value = None
    factor = 1.0 / math.sqrt(samples)
    for at, shift in enumerate([0] + order):
        last = at == n_tgroup - 1
        value = correlate(n_chan, owners, tuple(arrived[shift]), value, factor, last, samples)
    return value


def solution(mesh):
    in_specs = (P(("tgroup", "chan"), None), P(), P("chan"), P("chan", None))
    out_specs = P(("tgroup", "chan"), None, None, None)
    return jax.shard_map(local, mesh=mesh, in_specs=in_specs, out_specs=out_specs, check_vma=False)
```

```python
import functools
import math

import jax
import jax.numpy as jnp
from jax import lax
from jax.experimental import pallas as pl
from jax.experimental.pallas import tpu as pltpu
from jax.sharding import PartitionSpec as P

MAXLAG = 500
LAGS = 2 * MAXLAG + 1
TAPS = 255
CB = 8
K = 8
STRIPES = 2
SLOTS = 5
PAIRS = STRIPES * K
BLOCKS = STRIPES + SLOTS
WIDE = K * CB
SPILL = 64
LANES = 128
SHIFTS = 32
STEP = LANES // SHIFTS
LAG_BLOCKS = -(-LAGS // LANES)
FRONT = -(-MAXLAG // LANES) * LANES
NT = (((1,), (1,)), ((), ()))


def params(megabytes):
    return pltpu.CompilerParams(vmem_limit_bytes=megabytes << 20)


def vmem():
    return pl.BlockSpec(memory_space=pltpu.VMEM)


def smem():
    return pl.BlockSpec(memory_space=pltpu.SMEM)


def weights_kernel(taps, weights, held, line, sem):
    copy = pltpu.make_async_copy(taps, held, sem)
    copy.start()
    rows, outs, width = weights.shape[1], weights.shape[0] - 2 * SPILL, line.shape[1]
    line[...] = jnp.zeros_like(line)
    copy.wait()
    line[0:1, :TAPS] = held[...]
    spread = jnp.broadcast_to(line[0:1, :], (outs + 2 * SPILL, width))
    value = pltpu.roll(spread, width - 4 * SPILL + 1, 1, stride=2, stride_axis=0)[:, :rows]
    value = value.astype(jnp.bfloat16)
    weights[:outs, :] = value[SPILL : SPILL + outs]
    weights[outs : outs + SPILL, :] = value[SPILL + outs :]
    weights[outs + SPILL :, :] = value[:SPILL]


def select_kernel(n_chan, groups, firsts, raw, weights, *refs):
    sends, (window, picked, sems) = refs[: len(groups)], refs[len(groups) :]
    rows, channels = raw.shape
    steps = [k for group in groups for k in group]
    stripes = n_chan * STRIPES
    blocks_per = channels // n_chan // CB
    me = lax.axis_index("chan")

    def place(p):
        c, k = me ^ steps[p // STRIPES], p % STRIPES
        start = (firsts[c, k] + c * blocks_per) * CB
        return start, start - lax.rem(start, LANES)

    def copy(p, tile):
        base = jnp.minimum(place(p)[1] + tile * LANES, channels - LANES)
        return pltpu.make_async_copy(
            raw.at[:, pl.ds(pl.multiple_of(base, LANES), LANES)], window.at[p, tile], sems.at[p, tile]
        )

    for p in range(stripes):
        for tile in range(2):
            copy(p, tile).start()

    lane = lax.broadcasted_iota(jnp.int32, (rows, LANES), 1)
    row = lax.broadcasted_iota(jnp.int32, (LANES, LANES), 0)
    column = lax.broadcasted_iota(jnp.int32, (LANES, LANES), 1)
    height = STRIPES * WIDE
    batch = 2
    for first in range(0, len(steps), batch):
        for at in range(first, first + batch):
            sides, limits = [], []
            for i in range(STRIPES):
                p = at * STRIPES + i
                start, base = place(p)
                shift = start - base - i * WIDE
                turn = lax.rem(2 * LANES - shift, LANES)
                for tile in range(2):
                    copy(p, tile).wait()
                turned = [pltpu.roll(window[p, tile], turn, 1) for tile in range(2)]
                sides.append(jnp.where(lane < LANES - shift, turned[0], turned[1]))
                limits.append(channels - start + i * WIDE)
            both = jnp.where(lane < WIDE, sides[0], sides[1]).astype(jnp.bfloat16)
            limit = jnp.where(row < WIDE, limits[0], limits[1])
            unit = jnp.where((row == column) & (row < limit), 1.0, 0.0).astype(jnp.bfloat16)
            chosen = lax.dot_general(unit, both, NT, preferred_element_type=jnp.float32)
            picked[at * height : (at + 1) * height, :] = chosen.astype(jnp.bfloat16)
        part = slice(first * height, (first + batch) * height)
        result = lax.dot_general(
            picked[part, :], weights[...], NT, preferred_element_type=jnp.float32
        ).astype(jnp.bfloat16)
        for at in range(batch):
            k = steps[first + at]
            out, where = [(o, g.index(k)) for o, g in enumerate(groups) if k in g][0]
            sends[out][where * height : (where + 1) * height, :] = result[at * height : (at + 1) * height]


def add_spills(n_chan, outs, steps, got, total):
    count = total.shape[0]
    early = lax.broadcasted_iota(jnp.int32, (count, LANES), 1) < SPILL
    me = lax.axis_index("chan")
    pieces = [
        (me ^ k, ref.at[at * count : (at + 1) * count])
        for ks, ref in zip(steps, got)
        for at, k in enumerate(ks)
    ]
    for chunk, value in pieces:
        at = pl.ds(pl.multiple_of(chunk * outs, LANES), outs)
        total[:, at] = value[:, :outs].astype(jnp.float32)
    for chunk, value in pieces:
        spill = value[:, outs:].astype(jnp.float32)
        after = jnp.minimum(chunk + 1, n_chan - 1) * outs
        after = pl.ds(pl.multiple_of(after, LANES), LANES)
        total[:, after] += jnp.where(early & (chunk < n_chan - 1), spill, 0.0)
        before = jnp.maximum(chunk * outs, LANES) - LANES
        before = pl.ds(pl.multiple_of(before, LANES), LANES)
        total[:, before] += jnp.where(early | (chunk == 0), 0.0, spill)


def tile_of(group, width, vectors):
    half = vectors // 2
    if group == 0:
        return jnp.where(width == 0, 0, half + 1), half - 1
    return jnp.where(width == 0, half - 1, 0), half + 1


def own_half(n_chan):
    return jnp.where(lax.axis_index("chan") < n_chan // 2, 0, 1)


def place_kernel(n_chan, n_tgroup, outs, group, steps, owners, *refs):
    got, (total, pairs) = refs[: -n_tgroup - 2], refs[-2:]
    sends = refs[-n_tgroup - 2 : -2]
    me = lax.axis_index("tgroup")
    if len(got) == 1:
        total[...] = got[0][...]
    else:
        add_spills(n_chan, outs, steps, got, total)

    for at in range(n_tgroup * SLOTS):
        pairs[at] = -1
    counts = jnp.int32(0)
    for q in range(PAIRS):
        owner = owners[q]
        slot = (counts >> (3 * owner)) & 7
        counts = counts + (jnp.int32(1) << (3 * owner))
        pairs[(owner ^ me) * SLOTS + slot] = q

    base, per = tile_of(group, own_half(n_chan), total.shape[1] // LANES)

    def tiles(q):
        rows = pl.ds(pl.multiple_of(q * CB, CB), CB)
        return [
            total[rows, pl.ds(pl.multiple_of((base + j) * LANES, LANES), LANES)] for j in range(per)
        ]

    zero = jnp.zeros((CB, LANES), jnp.float32)
    leads = sum([tiles(p * K) for p in range(STRIPES)], [])
    for shift in range(n_tgroup):
        parts = list(leads)
        for s in range(SLOTS):
            q = pairs[shift * SLOTS + s]
            parts += [jnp.where(q >= 0, tile, 0.0) for tile in tiles(jnp.maximum(q, 0))]
        parts += [zero] * (len(parts) % 2)
        for at in range(0, len(parts), 2):
            value = jnp.concatenate(parts[at : at + 2], 0)
            sends[shift][at // 2] = value.astype(jnp.bfloat16)


def correlate_kernel(n_chan, count, factor, last, owners, *refs):
    lead, window_a, window_b, whole = refs[-4:]
    out = refs[-5]
    arrived, before = refs[: 2 * count], (refs[2 * count] if len(refs) > 2 * count + 5 else None)
    windows = (window_a, window_b)
    span = lead.shape[2] // count
    samples = span - LANES
    cols = span // LANES
    high = STEP * CB
    ahead = FRONT // LANES - 1
    me = lax.axis_index("tgroup")
    first_count = jnp.int32(0)
    for q in range(K):
        first_count += jnp.where(owners[q] == me, 1, 0)

    for at_segment in range(count):
        for group in range(2):
            ref = arrived[2 * at_segment + group]
            base, per = tile_of(group, own_half(n_chan), samples // LANES)
            for at in range(ref.shape[0]):
                value = ref[at].astype(jnp.float32)
                for part in range(2):
                    block, j = (2 * at + part) // per, (2 * at + part) % per
                    if block < BLOCKS:
                        lanes = pl.ds(pl.multiple_of((base + j) * LANES, LANES), LANES)
                        whole[at_segment, block, :, lanes] = value[part * CB : (part + 1) * CB]

    def series(at_segment, block):
        return jnp.concatenate([whole[at_segment, block], jnp.zeros((CB, LANES), jnp.float32)], 1)

    for p in range(STRIPES):
        for g in range(count):
            value = series(g, p)
            for a in range(CB):
                spread = jnp.broadcast_to(value[a : a + 1], (SHIFTS, span))
                turned = pltpu.roll(spread, 0, 1, stride=1, stride_axis=0)
                rows = slice(a * SHIFTS, (a + 1) * SHIFTS)
                lead[p, rows, g * span : (g + 1) * span] = turned.astype(jnp.bfloat16)

    def bounds(i):
        return max(0, ahead - i), min(cols, ahead + cols - i)

    for window in windows:
        for g in range(count):
            for i in range(LAG_BLOCKS):
                first, end = bounds(i)
                rows = slice(i * high, (i + 1) * high)
                if first > 0:
                    window[rows, g * span : g * span + first * LANES] = jnp.zeros(
                        (high, first * LANES), jnp.bfloat16
                    )
                if end < cols:
                    window[rows, g * span + end * LANES : (g + 1) * span] = jnp.zeros(
                        (high, (cols - end) * LANES), jnp.bfloat16
                    )

    group = lax.broadcasted_iota(jnp.int32, (CB, LANES), 1) // SHIFTS
    for s in range(SLOTS):
        window = windows[s % 2]
        for g in range(count):
            value = series(g, STRIPES + s)
            turned = [
                pltpu.roll(value, span - (FRONT - MAXLAG + SHIFTS * n), 1) for n in range(STEP)
            ]
            stacked = jnp.concatenate(turned, 0).astype(jnp.bfloat16)
            stacked = jnp.concatenate([stacked[:, samples:], stacked[:, :samples]], 1)
            for i in range(LAG_BLOCKS):
                first, end = bounds(i)
                window[
                    i * high : (i + 1) * high, g * span + first * LANES : g * span + end * LANES
                ] = stacked[:, (first + i - ahead) * LANES : (end + i - ahead) * LANES]
        which = jnp.where(s < first_count, 0, 1)
        summed = lax.dot_general(window[...], lead[which], NT, preferred_element_type=jnp.float32)
        if before is not None:
            summed = summed + before[s]
        if not last:
            out[s] = summed
            continue
        summed = summed * factor
        for i in range(LAG_BLOCKS):
            width = min(LANES, LAGS - i * LANES)
            for h in range(CB // STEP):
                parts = [
                    summed[(i * STEP + n) * CB : (i * STEP + n + 1) * CB, h * LANES : (h + 1) * LANES]
                    for n in range(STEP)
                ]
                for a in range(STEP):
                    value = parts[a]
                    for n in range(STEP):
                        if n != a:
                            moved = pltpu.roll(parts[n], (SHIFTS * (n - a)) % LANES, 1)
                            value = jnp.where(group == n, moved, value)
                    out[s, h * STEP + a, :, i * LANES : i * LANES + width] = value[:, :width]


def correlate(n_chan, owners, arrived, before, factor, last, samples):
    high, wide, count = STEP * LAG_BLOCKS * CB, CB * SHIFTS, len(arrived) // 2
    if last:
        shape = jax.ShapeDtypeStruct((SLOTS, CB, CB, LAGS), jnp.float32)
    else:
        shape = jax.ShapeDtypeStruct((SLOTS, high, wide), jnp.float32)
    operands = (owners,) + arrived + (() if before is None else (before,))
    depth = count * (samples + LANES)
    return pl.pallas_call(
        functools.partial(correlate_kernel, n_chan, count, factor, last),
        out_shape=shape,
        in_specs=[smem()] + [vmem()] * (len(operands) - 1),
        out_specs=vmem(),
        scratch_shapes=[
            pltpu.VMEM((STRIPES, wide, depth), jnp.bfloat16),
            pltpu.VMEM((high, depth), jnp.bfloat16),
            pltpu.VMEM((high, depth), jnp.bfloat16),
            pltpu.VMEM((count, BLOCKS, CB, samples), jnp.float32),
        ],
        compiler_params=params(40),
        name="correlate_last" if last else "correlate",
    )(*operands)


def local(raw_strain, whitening_taps, first_block, pair_owner):
    n_chan, n_tgroup = lax.axis_size("chan"), lax.axis_size("tgroup")
    rows, channels = raw_strain.shape
    outs = rows // 2
    samples = outs * n_chan
    count = PAIRS * CB
    owners = pair_owner[:, 0]

    firsts = lax.all_to_all(
        jnp.broadcast_to(first_block[None, :], (n_chan, STRIPES)),
        "chan",
        split_axis=0,
        concat_axis=0,
        tiled=True,
    )
    line = -(-(rows + 2 * outs + 4 * SPILL) // (2 * LANES)) * 2 * LANES
    weights = pl.pallas_call(
        weights_kernel,
        out_shape=jax.ShapeDtypeStruct((outs + 2 * SPILL, rows), jnp.bfloat16),
        in_specs=[pl.BlockSpec(memory_space=pl.ANY)],
        out_specs=vmem(),
        scratch_shapes=[
            pltpu.VMEM((1, TAPS), jnp.float32),
            pltpu.VMEM((8, line), jnp.float32),
            pltpu.SemaphoreType.DMA,
        ],
        compiler_params=params(40),
        name="fir_weights",
    )(whitening_taps.reshape(1, TAPS))

    relayed = n_chan == 8 and outs % LANES == 0
    groups = [[2], [3], [1, 5, 7], [4], [6], [0]] if relayed else [[k] for k in range(n_chan)]
    sends = pl.pallas_call(
        functools.partial(select_kernel, n_chan, groups),
        out_shape=[
            jax.ShapeDtypeStruct((len(group) * count, outs + 2 * SPILL), jnp.bfloat16)
            for group in groups
        ],
        in_specs=[smem(), pl.BlockSpec(memory_space=pl.ANY), vmem()],
        out_specs=[vmem()] * len(groups),
        scratch_shapes=[
            pltpu.VMEM((n_chan * STRIPES, 2, rows, LANES), jnp.float32),
            pltpu.VMEM((n_chan * count, rows), jnp.bfloat16),
            pltpu.SemaphoreType.DMA((n_chan * STRIPES, 2)),
        ],
        compiler_params=params(40),
        name="select_filter",
    )(firsts, raw_strain, weights)

    def exchange(value, k):
        return lax.ppermute(value, "chan", [(c, c ^ k) for c in range(n_chan)])

    if relayed:
        got = [sends[5], exchange(sends[0], 2), exchange(sends[1], 3), exchange(sends[2], 1)]
        across = [
            jnp.concatenate([sends[3 + at], got[3][(1 + at) * count : (2 + at) * count]], 0)
            for at in range(2)
        ]
        across, got[1] = lax.optimization_barrier((across, got[1]))
        across = [exchange(value, 4 + 2 * at) for at, value in enumerate(across)]
        early, late = got, got + across
        early_steps, late_steps = [[0], [2], [3], [1]], [[0], [2], [3], [1], [4, 5], [6, 7]]
    else:
        got = [sends[0]] + [exchange(sends[k], k) for k in range(1, n_chan)]
        half = n_chan // 2
        early, late = got[:half], got
        early_steps, late_steps = [[k] for k in range(half)], [[k] for k in range(n_chan)]
    if outs % LANES:
        wide = jnp.stack(got).astype(jnp.float32)
        wide = jnp.take(wide, lax.axis_index("chan") ^ jnp.arange(n_chan), axis=0)
        none = jnp.zeros((n_chan, count, outs - SPILL), jnp.float32)
        zero = jnp.zeros((1, count, SPILL), jnp.float32)
        right = jnp.concatenate([zero, wide[:-1, :, outs : outs + SPILL]], 0)
        left = jnp.concatenate([wide[1:, :, outs + SPILL :], zero], 0)
        added = wide[:, :, :outs] + jnp.concatenate([right, none], 2) + jnp.concatenate([none, left], 2)
        early = late = [added.transpose(1, 0, 2).reshape(count, samples)]

    order = sorted(range(1, n_tgroup), key=lambda s: (s.bit_length(), -s))
    arrived = [[] for _ in range(n_tgroup)]
    for group in range(2):
        use, steps = (early, early_steps) if group == 0 else (late, late_steps)
        vectors = samples // LANES // 2 + (1 if group else -1)
        packed = jax.ShapeDtypeStruct((-(-BLOCKS * vectors // 2), 2 * CB, LANES), jnp.bfloat16)
        sends = pl.pallas_call(
            functools.partial(place_kernel, n_chan, n_tgroup, outs, group, steps),
            out_shape=(packed,) * n_tgroup,
            in_specs=[smem()] + [vmem()] * len(use),
            out_specs=(vmem(),) * n_tgroup,
            scratch_shapes=[
                pltpu.VMEM((count, samples), jnp.float32),
                pltpu.SMEM((n_tgroup * SLOTS,), jnp.int32),
            ],
            compiler_params=params(40),
            name="place_first" if group == 0 else "place_second",
        )(owners, *use)
        arrived[0].append(sends[0])
        for shift in order:
            route = [(g, g ^ shift) for g in range(n_tgroup)]
            value = sends[shift]
            if group == 1:
                value, arrived[shift][0] = lax.optimization_barrier((value, arrived[shift][0]))
            arrived[shift].append(lax.ppermute(value, "tgroup", route))

    value = None
    factor = 1.0 / math.sqrt(samples)
    turns = [[shift] for shift in [0] + order]
    for at, shifts in enumerate(turns):
        operands = tuple(sum([arrived[shift] for shift in shifts], []))
        value = correlate(n_chan, owners, operands, value, factor, at == len(turns) - 1, samples)
    return value


def solution(mesh):
    in_specs = (P(("tgroup", "chan"), None), P(), P("chan"), P("chan", None))
    out_specs = P(("tgroup", "chan"), None, None, None)
    return jax.shard_map(local, mesh=mesh, in_specs=in_specs, out_specs=out_specs, check_vma=False)
```

```python
import functools
import math

import jax
import jax.numpy as jnp
from jax import lax
from jax.experimental import pallas as pl
from jax.experimental.pallas import tpu as pltpu
from jax.sharding import PartitionSpec as P

MAXLAG = 500
LAGS = 2 * MAXLAG + 1
TAPS = 255
CB = 8
K = 8
STRIPES = 2
SLOTS = 5
PAIRS = STRIPES * K
BLOCKS = STRIPES + SLOTS
WIDE = K * CB
SPILL = 64
LANES = 128
SHIFTS = 32
STEP = LANES // SHIFTS
LAG_BLOCKS = -(-LAGS // LANES)
FRONT = -(-MAXLAG // LANES) * LANES
NT = (((1,), (1,)), ((), ()))


def params(megabytes):
    return pltpu.CompilerParams(vmem_limit_bytes=megabytes << 20)


def vmem():
    return pl.BlockSpec(memory_space=pltpu.VMEM)


def smem():
    return pl.BlockSpec(memory_space=pltpu.SMEM)


def weights_kernel(taps, weights, held, line, sem):
    copy = pltpu.make_async_copy(taps, held, sem)
    copy.start()
    rows, outs, width = weights.shape[0], weights.shape[1] - 2 * SPILL, line.shape[1]
    line[...] = jnp.zeros_like(line)
    copy.wait()
    line[0:1, :TAPS] = held[...]
    spread = jnp.broadcast_to(line[0:1, :], (outs + 2 * SPILL, width))
    value = pltpu.roll(spread, width - 4 * SPILL + 1, 1, stride=2, stride_axis=0)[:, :rows]
    value = jnp.concatenate([value[SPILL : SPILL + outs], value[SPILL + outs :], value[:SPILL]], 0)
    weights[...] = value.T.astype(jnp.bfloat16)


def select_kernel(n_chan, groups, firsts, raw, weights, *refs):
    sends, (window, picked, sems) = refs[: len(groups)], refs[len(groups) :]
    rows, channels = raw.shape
    steps = [k for group in groups for k in group]
    stripes = n_chan * STRIPES
    blocks_per = channels // n_chan // CB
    span = window.shape[2]
    me = lax.axis_index("chan")

    def place(p):
        c, k = me ^ steps[p // STRIPES], p % STRIPES
        start = (firsts[c, k] + c * blocks_per) * CB
        base = jnp.minimum(start - lax.rem(start, LANES), channels - span)
        return start, pl.multiple_of(base, LANES)

    def copy(p):
        base = place(p)[1]
        return pltpu.make_async_copy(raw.at[:, pl.ds(base, span)], window.at[p], sems.at[p])

    for p in range(stripes):
        copy(p).start()

    row = lax.broadcasted_iota(jnp.int32, (WIDE, span), 0)
    lane = lax.broadcasted_iota(jnp.int32, (WIDE, span), 1)
    batch = 2 * STRIPES
    for first in range(0, stripes, batch):
        for p in range(first, first + batch):
            copy(p).wait()
            start, base = place(p)
            hot = (lane == row + (start - base)) & (row < channels - start)
            hot = jnp.where(hot, 1.0, 0.0).astype(jnp.bfloat16)
            block = window[p].astype(jnp.bfloat16)
            chosen = lax.dot_general(hot, block, NT, preferred_element_type=jnp.float32)
            picked[p * WIDE : (p + 1) * WIDE, :] = chosen.astype(jnp.bfloat16)
        part = slice(first * WIDE, (first + batch) * WIDE)
        result = jnp.dot(
            picked[part, :], weights[...], preferred_element_type=jnp.float32
        ).astype(jnp.bfloat16)
        height = STRIPES * WIDE
        for at in range(batch // STRIPES):
            k = steps[first // STRIPES + at]
            out, where = [(o, g.index(k)) for o, g in enumerate(groups) if k in g][0]
            sends[out][where * height : (where + 1) * height, :] = result[at * height : (at + 1) * height]


def add_spills(n_chan, outs, steps, got, total):
    count = total.shape[0]
    early = lax.broadcasted_iota(jnp.int32, (count, LANES), 1) < SPILL
    me = lax.axis_index("chan")
    pieces = [
        (me ^ k, ref.at[at * count : (at + 1) * count])
        for ks, ref in zip(steps, got)
        for at, k in enumerate(ks)
    ]
    for chunk, value in pieces:
        at = pl.ds(pl.multiple_of(chunk * outs, LANES), outs)
        total[:, at] = value[:, :outs].astype(jnp.float32)
    for chunk, value in pieces:
        spill = value[:, outs:].astype(jnp.float32)
        after = jnp.minimum(chunk + 1, n_chan - 1) * outs
        after = pl.ds(pl.multiple_of(after, LANES), LANES)
        total[:, after] += jnp.where(early & (chunk < n_chan - 1), spill, 0.0)
        before = jnp.maximum(chunk * outs, LANES) - LANES
        before = pl.ds(pl.multiple_of(before, LANES), LANES)
        total[:, before] += jnp.where(early | (chunk == 0), 0.0, spill)


def tile_of(group, width, vectors):
    half = vectors // 2
    if group == 0:
        return jnp.where(width == 0, 0, half + 1), half - 1
    if group == 1:
        return jnp.where(width == 0, half - 1, 0), half + 1
    return 0, vectors


def tiles_in(group, vectors):
    return -(-BLOCKS * tile_of(group, 0, vectors)[1] // 2)


def own_half(n_chan):
    return jnp.where(lax.axis_index("chan") < n_chan // 2, 0, 1)


def place_kernel(n_chan, n_tgroup, outs, plan, steps, owners, *refs):
    got, (total, pairs) = refs[: -len(plan) - 2], refs[-2:]
    sends = refs[-len(plan) - 2 : -2]
    me = lax.axis_index("tgroup")
    if len(got) == 1:
        total[...] = got[0][...]
    else:
        add_spills(n_chan, outs, steps, got, total)

    for at in range(n_tgroup * SLOTS):
        pairs[at] = -1
    counts = jnp.int32(0)
    for q in range(PAIRS):
        owner = owners[q]
        slot = (counts >> (3 * owner)) & 7
        counts = counts + (jnp.int32(1) << (3 * owner))
        pairs[(owner ^ me) * SLOTS + slot] = q

    zero = jnp.zeros((CB, LANES), jnp.float32)
    for send, (shift, group) in zip(sends, plan):
        base, per = tile_of(group, own_half(n_chan), total.shape[1] // LANES)

        def tiles(q):
            rows = pl.ds(pl.multiple_of(q * CB, CB), CB)
            return [
                total[rows, pl.ds(pl.multiple_of((base + j) * LANES, LANES), LANES)]
                for j in range(per)
            ]

        parts = sum([tiles(p * K) for p in range(STRIPES)], [])
        for s in range(SLOTS):
            q = pairs[shift * SLOTS + s]
            parts += [jnp.where(q >= 0, tile, 0.0) for tile in tiles(jnp.maximum(q, 0))]
        parts += [zero] * (len(parts) % 2)
        for at in range(0, len(parts), 2):
            value = jnp.concatenate(parts[at : at + 2], 0)
            send[at // 2] = value.astype(jnp.bfloat16)


def correlate_kernel(n_chan, groups, factor, last, owners, *refs):
    lead, window_a, window_b, whole = refs[-4:]
    out = refs[-5]
    arrived = refs[: len(groups)]
    before = refs[len(groups)] if len(refs) > len(groups) + 5 else None
    windows = (window_a, window_b)
    span = lead.shape[2]
    samples = span - LANES
    cols = span // LANES
    high = STEP * CB
    ahead = FRONT // LANES - 1
    me = lax.axis_index("tgroup")
    first_count = jnp.int32(0)
    for q in range(K):
        first_count += jnp.where(owners[q] == me, 1, 0)

    for ref, group in zip(arrived, groups):
        base, per = tile_of(group, own_half(n_chan), samples // LANES)
        for at in range(ref.shape[0]):
            value = ref[at].astype(jnp.float32)
            for part in range(2):
                block, j = (2 * at + part) // per, (2 * at + part) % per
                if block < BLOCKS:
                    lanes = pl.ds(pl.multiple_of((base + j) * LANES, LANES), LANES)
                    whole[block, :, lanes] = value[part * CB : (part + 1) * CB]

    def series(block):
        return jnp.concatenate([whole[block], jnp.zeros((CB, LANES), jnp.float32)], 1)

    for p in range(STRIPES):
        value = series(p)
        for a in range(CB):
            spread = jnp.broadcast_to(value[a : a + 1], (SHIFTS, span))
            turned = pltpu.roll(spread, 0, 1, stride=1, stride_axis=0)
            lead[p, a * SHIFTS : (a + 1) * SHIFTS, :] = turned.astype(jnp.bfloat16)

    def bounds(i):
        return max(0, ahead - i), min(cols, ahead + cols - i)

    for window in windows:
        for i in range(LAG_BLOCKS):
            first, end = bounds(i)
            rows = slice(i * high, (i + 1) * high)
            if first > 0:
                window[rows, : first * LANES] = jnp.zeros((high, first * LANES), jnp.bfloat16)
            if end < cols:
                window[rows, end * LANES :] = jnp.zeros((high, (cols - end) * LANES), jnp.bfloat16)

    group = lax.broadcasted_iota(jnp.int32, (CB, LANES), 1) // SHIFTS
    for s in range(SLOTS):
        window = windows[s % 2]
        value = series(STRIPES + s)
        turned = [pltpu.roll(value, span - (FRONT - MAXLAG + SHIFTS * n), 1) for n in range(STEP)]
        stacked = jnp.concatenate(turned, 0).astype(jnp.bfloat16)
        stacked = jnp.concatenate([stacked[:, samples:], stacked[:, :samples]], 1)
        for i in range(LAG_BLOCKS):
            first, end = bounds(i)
            window[i * high : (i + 1) * high, first * LANES : end * LANES] = stacked[
                :, (first + i - ahead) * LANES : (end + i - ahead) * LANES
            ]
        which = jnp.where(s < first_count, 0, 1)
        summed = lax.dot_general(window[...], lead[which], NT, preferred_element_type=jnp.float32)
        if before is not None:
            summed = summed + before[s]
        if not last:
            out[s] = summed
            continue
        summed = summed * factor
        for i in range(LAG_BLOCKS):
            width = min(LANES, LAGS - i * LANES)
            for h in range(CB // STEP):
                parts = [
                    summed[(i * STEP + n) * CB : (i * STEP + n + 1) * CB, h * LANES : (h + 1) * LANES]
                    for n in range(STEP)
                ]
                for a in range(STEP):
                    value = parts[a]
                    for n in range(STEP):
                        if n != a:
                            moved = pltpu.roll(parts[n], (SHIFTS * (n - a)) % LANES, 1)
                            value = jnp.where(group == n, moved, value)
                    out[s, h * STEP + a, :, i * LANES : i * LANES + width] = value[:, :width]


def correlate(n_chan, owners, arrived, groups, before, factor, last, samples):
    high, wide = STEP * LAG_BLOCKS * CB, CB * SHIFTS
    if last:
        shape = jax.ShapeDtypeStruct((SLOTS, CB, CB, LAGS), jnp.float32)
    else:
        shape = jax.ShapeDtypeStruct((SLOTS, high, wide), jnp.float32)
    operands = (owners,) + arrived + (() if before is None else (before,))
    depth = samples + LANES
    return pl.pallas_call(
        functools.partial(correlate_kernel, n_chan, groups, factor, last),
        out_shape=shape,
        in_specs=[smem()] + [vmem()] * (len(operands) - 1),
        out_specs=vmem(),
        scratch_shapes=[
            pltpu.VMEM((STRIPES, wide, depth), jnp.bfloat16),
            pltpu.VMEM((high, depth), jnp.bfloat16),
            pltpu.VMEM((high, depth), jnp.bfloat16),
            pltpu.VMEM((BLOCKS, CB, samples), jnp.float32),
        ],
        compiler_params=params(40),
        name="correlate_last" if last else "correlate",
    )(*operands)


def local(raw_strain, whitening_taps, first_block, pair_owner):
    n_chan, n_tgroup = lax.axis_size("chan"), lax.axis_size("tgroup")
    rows, channels = raw_strain.shape
    outs = rows // 2
    samples = outs * n_chan
    count = PAIRS * CB
    owners = pair_owner[:, 0]

    firsts = lax.all_to_all(
        jnp.broadcast_to(first_block[None, :], (n_chan, STRIPES)),
        "chan",
        split_axis=0,
        concat_axis=0,
        tiled=True,
    )
    line = -(-(rows + 2 * outs + 4 * SPILL) // (2 * LANES)) * 2 * LANES
    weights = pl.pallas_call(
        weights_kernel,
        out_shape=jax.ShapeDtypeStruct((rows, outs + 2 * SPILL), jnp.bfloat16),
        in_specs=[pl.BlockSpec(memory_space=pl.ANY)],
        out_specs=vmem(),
        scratch_shapes=[
            pltpu.VMEM((1, TAPS), jnp.float32),
            pltpu.VMEM((8, line), jnp.float32),
            pltpu.SemaphoreType.DMA,
        ],
        compiler_params=params(40),
        name="fir_weights",
    )(whitening_taps.reshape(1, TAPS))

    groups = [[k] for k in range(n_chan)]
    sends = pl.pallas_call(
        functools.partial(select_kernel, n_chan, groups),
        out_shape=[
            jax.ShapeDtypeStruct((len(group) * count, outs + 2 * SPILL), jnp.bfloat16)
            for group in groups
        ],
        in_specs=[smem(), pl.BlockSpec(memory_space=pl.ANY), vmem()],
        out_specs=[vmem()] * len(groups),
        scratch_shapes=[
            pltpu.VMEM((n_chan * STRIPES, rows, 2 * LANES), jnp.float32),
            pltpu.VMEM((n_chan * count, rows), jnp.bfloat16),
            pltpu.SemaphoreType.DMA((n_chan * STRIPES,)),
        ],
        compiler_params=params(40),
        name="select_filter",
    )(firsts, raw_strain, weights)

    def exchange(value, k):
        return lax.ppermute(value, "chan", [(c, c ^ k) for c in range(n_chan)])

    half = n_chan // 2
    got = [sends[0]] + [exchange(sends[k], k) for k in range(1, n_chan)]
    steps = [[k] for k in range(n_chan)]
    early, late = got[:half], got

    if outs % LANES:
        wide = jnp.stack(got).astype(jnp.float32)
        wide = jnp.take(wide, lax.axis_index("chan") ^ jnp.arange(n_chan), axis=0)
        none = jnp.zeros((n_chan, count, outs - SPILL), jnp.float32)
        zero = jnp.zeros((1, count, SPILL), jnp.float32)
        right = jnp.concatenate([zero, wide[:-1, :, outs : outs + SPILL]], 0)
        left = jnp.concatenate([wide[1:, :, outs + SPILL :], zero], 0)
        added = wide[:, :, :outs] + jnp.concatenate([right, none], 2) + jnp.concatenate([none, left], 2)
        early = late = [added.transpose(1, 0, 2).reshape(count, samples)]

    order = sorted(range(1, n_tgroup), key=lambda s: (s.bit_length(), -s))
    vectors = samples // LANES
    factor = 1.0 / math.sqrt(samples)

    def place(plan, use, name):
        return pl.pallas_call(
            functools.partial(place_kernel, n_chan, n_tgroup, outs, plan, steps),
            out_shape=[
                jax.ShapeDtypeStruct((tiles_in(group, vectors), 2 * CB, LANES), jnp.bfloat16)
                for _, group in plan
            ],
            in_specs=[smem()] + [vmem()] * len(use),
            out_specs=[vmem()] * len(plan),
            scratch_shapes=[
                pltpu.VMEM((count, samples), jnp.float32),
                pltpu.SMEM((n_tgroup * SLOTS,), jnp.int32),
            ],
            compiler_params=params(40),
            name=name,
        )(owners, *use)

    def hand_over(value, shift):
        return lax.ppermute(value, "tgroup", [(g, g ^ shift) for g in range(n_tgroup)])

    if outs % LANES == 0:
        early, got[half] = lax.optimization_barrier((early, got[half]))
        late = list(early) + got[half:]
    far = order[1:]
    first = place([(shift, 0) for shift in far], early, "place_first")
    arrived = {shift: [hand_over(value, shift)] for shift, value in zip(far, first)}
    plan = [(0, 2), (1, 2)] + [(shift, 1) for shift in far]
    own, near, *second = place(plan, late, "place_second")
    arrived[0], arrived[1] = [own], [hand_over(near, 1)]
    for shift, value in zip(far, second):
        value, held = lax.optimization_barrier((value, arrived[shift][0]))
        arrived[shift] = [held, hand_over(value, shift)]

    value = None
    for at, shift in enumerate([0] + order):
        parts = (0, 1) if shift in far else (2,)
        last = at == n_tgroup - 1
        value = correlate(
            n_chan, owners, tuple(arrived[shift]), parts, value, factor, last, samples
        )
    return value


def solution(mesh):
    in_specs = (P(("tgroup", "chan"), None), P(), P("chan"), P("chan", None))
    out_specs = P(("tgroup", "chan"), None, None, None)
    return jax.shard_map(local, mesh=mesh, in_specs=in_specs, out_specs=out_specs, check_vma=False)
```

```python
import functools
import math

import jax
import jax.numpy as jnp
from jax import lax
from jax.experimental import pallas as pl
from jax.experimental.pallas import tpu as pltpu
from jax.sharding import PartitionSpec as P

MAXLAG = 500
LAGS = 2 * MAXLAG + 1
TAPS = 255
CB = 8
K = 8
STRIPES = 2
SLOTS = 5
PAIRS = STRIPES * K
BLOCKS = STRIPES + SLOTS
WIDE = K * CB
SPILL = 64
LANES = 128
SHIFTS = 32
STEP = LANES // SHIFTS
LAG_BLOCKS = -(-LAGS // LANES)
FRONT = -(-MAXLAG // LANES) * LANES
NT = (((1,), (1,)), ((), ()))


def params(megabytes):
    return pltpu.CompilerParams(vmem_limit_bytes=megabytes << 20)


def vmem():
    return pl.BlockSpec(memory_space=pltpu.VMEM)


def smem():
    return pl.BlockSpec(memory_space=pltpu.SMEM)


def weights_kernel(taps, weights, held, line, sem):
    copy = pltpu.make_async_copy(taps, held, sem)
    copy.start()
    rows, outs, width = weights.shape[0], weights.shape[1] - 2 * SPILL, line.shape[1]
    line[...] = jnp.zeros_like(line)
    copy.wait()
    line[0:1, :TAPS] = held[...]
    spread = jnp.broadcast_to(line[0:1, :], (outs + 2 * SPILL, width))
    value = pltpu.roll(spread, width - 4 * SPILL + 1, 1, stride=2, stride_axis=0)[:, :rows]
    value = jnp.concatenate([value[SPILL : SPILL + outs], value[SPILL + outs :], value[:SPILL]], 0)
    weights[...] = value.T.astype(jnp.bfloat16)


def select_kernel(n_chan, groups, firsts, raw, weights, *refs):
    sends, (window, picked, sems) = refs[: len(groups)], refs[len(groups) :]
    rows, channels = raw.shape
    steps = [k for group in groups for k in group]
    stripes = n_chan * STRIPES
    blocks_per = channels // n_chan // CB
    span = window.shape[2]
    me = lax.axis_index("chan")

    def place(p):
        k = steps[p // STRIPES]
        start = (firsts[k, p % STRIPES] + (me ^ k) * blocks_per) * CB
        base = jnp.minimum(start - lax.rem(start, LANES), channels - span)
        return start, pl.multiple_of(base, LANES)

    def copy(p):
        base = place(p)[1]
        return pltpu.make_async_copy(raw.at[:, pl.ds(base, span)], window.at[p], sems.at[p])

    for p in range(stripes):
        copy(p).start()

    row = lax.broadcasted_iota(jnp.int32, (WIDE, span), 0)
    lane = lax.broadcasted_iota(jnp.int32, (WIDE, span), 1)
    batch = 2 * STRIPES
    for first in range(0, stripes, batch):
        for p in range(first, first + batch):
            copy(p).wait()
            start, base = place(p)
            hot = (lane == row + (start - base)) & (row < channels - start)
            hot = jnp.where(hot, 1.0, 0.0).astype(jnp.bfloat16)
            block = window[p].astype(jnp.bfloat16)
            chosen = lax.dot_general(hot, block, NT, preferred_element_type=jnp.float32)
            picked[p * WIDE : (p + 1) * WIDE, :] = chosen.astype(jnp.bfloat16)
        part = slice(first * WIDE, (first + batch) * WIDE)
        result = jnp.dot(
            picked[part, :], weights[...], preferred_element_type=jnp.float32
        ).astype(jnp.bfloat16)
        height = STRIPES * WIDE
        for at in range(batch // STRIPES):
            k = steps[first // STRIPES + at]
            out, where = [(o, g.index(k)) for o, g in enumerate(groups) if k in g][0]
            sends[out][where * height : (where + 1) * height, :] = result[at * height : (at + 1) * height]


def add_spills(n_chan, outs, steps, got, total):
    count = total.shape[0]
    early = lax.broadcasted_iota(jnp.int32, (count, LANES), 1) < SPILL
    me = lax.axis_index("chan")
    pieces = [
        (me ^ k, ref.at[at * count : (at + 1) * count])
        for ks, ref in zip(steps, got)
        for at, k in enumerate(ks)
    ]
    for chunk, value in pieces:
        at = pl.ds(pl.multiple_of(chunk * outs, LANES), outs)
        total[:, at] = value[:, :outs].astype(jnp.float32)
    for chunk, value in pieces:
        spill = value[:, outs:].astype(jnp.float32)
        after = jnp.minimum(chunk + 1, n_chan - 1) * outs
        after = pl.ds(pl.multiple_of(after, LANES), LANES)
        total[:, after] += jnp.where(early & (chunk < n_chan - 1), spill, 0.0)
        before = jnp.maximum(chunk * outs, LANES) - LANES
        before = pl.ds(pl.multiple_of(before, LANES), LANES)
        total[:, before] += jnp.where(early | (chunk == 0), 0.0, spill)


def tile_of(group, width, vectors):
    half = vectors // 2
    if group == 0:
        return jnp.where(width == 0, 0, half + 1), half - 1
    if group == 1:
        return jnp.where(width == 0, half - 1, 0), half + 1
    return 0, vectors


def tiles_in(group, vectors):
    return -(-BLOCKS * tile_of(group, 0, vectors)[1] // 2)


def own_half(n_chan):
    return jnp.where(lax.axis_index("chan") < n_chan // 2, 0, 1)


def place_kernel(n_chan, n_tgroup, outs, plan, steps, owners, *refs):
    got, (total, pairs) = refs[: -len(plan) - 2], refs[-2:]
    sends = refs[-len(plan) - 2 : -2]
    me = lax.axis_index("tgroup")
    if len(got) == 1:
        total[...] = got[0][...]
    else:
        add_spills(n_chan, outs, steps, got, total)

    for at in range(n_tgroup * SLOTS):
        pairs[at] = -1
    counts = jnp.int32(0)
    for q in range(PAIRS):
        owner = owners[q]
        slot = (counts >> (3 * owner)) & 7
        counts = counts + (jnp.int32(1) << (3 * owner))
        pairs[(owner ^ me) * SLOTS + slot] = q

    zero = jnp.zeros((CB, LANES), jnp.float32)
    for send, (shift, group) in zip(sends, plan):
        base, per = tile_of(group, own_half(n_chan), total.shape[1] // LANES)

        def tiles(q):
            rows = pl.ds(pl.multiple_of(q * CB, CB), CB)
            return [
                total[rows, pl.ds(pl.multiple_of((base + j) * LANES, LANES), LANES)]
                for j in range(per)
            ]

        parts = sum([tiles(p * K) for p in range(STRIPES)], [])
        for s in range(SLOTS):
            q = pairs[shift * SLOTS + s]
            parts += [jnp.where(q >= 0, tile, 0.0) for tile in tiles(jnp.maximum(q, 0))]
        parts += [zero] * (len(parts) % 2)
        for at in range(0, len(parts), 2):
            value = jnp.concatenate(parts[at : at + 2], 0)
            send[at // 2] = value.astype(jnp.bfloat16)


def correlate_kernel(n_chan, groups, factor, last, owners, *refs):
    lead, window_a, window_b, whole = refs[-4:]
    out = refs[-5]
    arrived = refs[: len(groups)]
    before = refs[len(groups)] if len(refs) > len(groups) + 5 else None
    windows = (window_a, window_b)
    span = lead.shape[2]
    samples = span - LANES
    cols = span // LANES
    high = STEP * CB
    ahead = FRONT // LANES - 1
    me = lax.axis_index("tgroup")
    first_count = jnp.int32(0)
    for q in range(K):
        first_count += jnp.where(owners[q] == me, 1, 0)

    for ref, group in zip(arrived, groups):
        base, per = tile_of(group, own_half(n_chan), samples // LANES)
        for at in range(ref.shape[0]):
            value = ref[at].astype(jnp.float32)
            for part in range(2):
                block, j = (2 * at + part) // per, (2 * at + part) % per
                if block < BLOCKS:
                    lanes = pl.ds(pl.multiple_of((base + j) * LANES, LANES), LANES)
                    whole[block, :, lanes] = value[part * CB : (part + 1) * CB]

    def series(block):
        return jnp.concatenate([whole[block], jnp.zeros((CB, LANES), jnp.float32)], 1)

    for p in range(STRIPES):
        value = series(p)
        for a in range(CB):
            spread = jnp.broadcast_to(value[a : a + 1], (SHIFTS, span))
            turned = pltpu.roll(spread, 0, 1, stride=1, stride_axis=0)
            lead[p, a * SHIFTS : (a + 1) * SHIFTS, :] = turned.astype(jnp.bfloat16)

    def bounds(i):
        return max(0, ahead - i), min(cols, ahead + cols - i)

    for window in windows:
        for i in range(LAG_BLOCKS):
            first, end = bounds(i)
            rows = slice(i * high, (i + 1) * high)
            if first > 0:
                window[rows, : first * LANES] = jnp.zeros((high, first * LANES), jnp.bfloat16)
            if end < cols:
                window[rows, end * LANES :] = jnp.zeros((high, (cols - end) * LANES), jnp.bfloat16)

    group = lax.broadcasted_iota(jnp.int32, (CB, LANES), 1) // SHIFTS
    for s in range(SLOTS):
        window = windows[s % 2]
        value = series(STRIPES + s)
        turned = [pltpu.roll(value, span - (FRONT - MAXLAG + SHIFTS * n), 1) for n in range(STEP)]
        stacked = jnp.concatenate(turned, 0).astype(jnp.bfloat16)
        stacked = jnp.concatenate([stacked[:, samples:], stacked[:, :samples]], 1)
        for i in range(LAG_BLOCKS):
            first, end = bounds(i)
            window[i * high : (i + 1) * high, first * LANES : end * LANES] = stacked[
                :, (first + i - ahead) * LANES : (end + i - ahead) * LANES
            ]
        which = jnp.where(s < first_count, 0, 1)
        summed = lax.dot_general(window[...], lead[which], NT, preferred_element_type=jnp.float32)
        if before is not None:
            summed = summed + before[s]
        if not last:
            out[s] = summed
            continue
        summed = summed * factor
        for i in range(LAG_BLOCKS):
            width = min(LANES, LAGS - i * LANES)
            for h in range(CB // STEP):
                parts = [
                    summed[(i * STEP + n) * CB : (i * STEP + n + 1) * CB, h * LANES : (h + 1) * LANES]
                    for n in range(STEP)
                ]
                for a in range(STEP):
                    value = parts[a]
                    for n in range(STEP):
                        if n != a:
                            moved = pltpu.roll(parts[n], (SHIFTS * (n - a)) % LANES, 1)
                            value = jnp.where(group == n, moved, value)
                    out[s, h * STEP + a, :, i * LANES : i * LANES + width] = value[:, :width]


def correlate(n_chan, owners, arrived, groups, before, factor, last, samples):
    high, wide = STEP * LAG_BLOCKS * CB, CB * SHIFTS
    if last:
        shape = jax.ShapeDtypeStruct((SLOTS, CB, CB, LAGS), jnp.float32)
    else:
        shape = jax.ShapeDtypeStruct((SLOTS, high, wide), jnp.float32)
    operands = (owners,) + arrived + (() if before is None else (before,))
    depth = samples + LANES
    return pl.pallas_call(
        functools.partial(correlate_kernel, n_chan, groups, factor, last),
        out_shape=shape,
        in_specs=[smem()] + [vmem()] * (len(operands) - 1),
        out_specs=vmem(),
        scratch_shapes=[
            pltpu.VMEM((STRIPES, wide, depth), jnp.bfloat16),
            pltpu.VMEM((high, depth), jnp.bfloat16),
            pltpu.VMEM((high, depth), jnp.bfloat16),
            pltpu.VMEM((BLOCKS, CB, samples), jnp.float32),
        ],
        compiler_params=params(40),
        name="correlate_last" if last else "correlate",
    )(*operands)


def local(raw_strain, whitening_taps, first_block, pair_owner):
    n_chan, n_tgroup = lax.axis_size("chan"), lax.axis_size("tgroup")
    rows, channels = raw_strain.shape
    outs = rows // 2
    samples = outs * n_chan
    count = PAIRS * CB
    owners = pair_owner[:, 0]

    def exchange(value, k):
        return lax.ppermute(value, "chan", [(c, c ^ k) for c in range(n_chan)])

    firsts = first_block.reshape(1, STRIPES)
    while firsts.shape[0] < n_chan:
        firsts = jnp.concatenate([firsts, exchange(firsts, firsts.shape[0])], 0)
    line = -(-(rows + 2 * outs + 4 * SPILL) // (2 * LANES)) * 2 * LANES
    weights = pl.pallas_call(
        weights_kernel,
        out_shape=jax.ShapeDtypeStruct((rows, outs + 2 * SPILL), jnp.bfloat16),
        in_specs=[pl.BlockSpec(memory_space=pl.ANY)],
        out_specs=vmem(),
        scratch_shapes=[
            pltpu.VMEM((1, TAPS), jnp.float32),
            pltpu.VMEM((8, line), jnp.float32),
            pltpu.SemaphoreType.DMA,
        ],
        compiler_params=params(40),
        name="fir_weights",
    )(whitening_taps.reshape(1, TAPS))

    groups = [[k] for k in range(n_chan)]
    sends = pl.pallas_call(
        functools.partial(select_kernel, n_chan, groups),
        out_shape=[
            jax.ShapeDtypeStruct((len(group) * count, outs + 2 * SPILL), jnp.bfloat16)
            for group in groups
        ],
        in_specs=[smem(), pl.BlockSpec(memory_space=pl.ANY), vmem()],
        out_specs=[vmem()] * len(groups),
        scratch_shapes=[
            pltpu.VMEM((n_chan * STRIPES, rows, 2 * LANES), jnp.float32),
            pltpu.VMEM((n_chan * count, rows), jnp.bfloat16),
            pltpu.SemaphoreType.DMA((n_chan * STRIPES,)),
        ],
        compiler_params=params(40),
        name="select_filter",
    )(firsts, raw_strain, weights)

    half = n_chan // 2
    got = [sends[0]] + [exchange(sends[k], k) for k in range(1, n_chan)]
    steps = [[k] for k in range(n_chan)]
    early, late = got[:half], got

    if outs % LANES:
        wide = jnp.stack(got).astype(jnp.float32)
        wide = jnp.take(wide, lax.axis_index("chan") ^ jnp.arange(n_chan), axis=0)
        none = jnp.zeros((n_chan, count, outs - SPILL), jnp.float32)
        zero = jnp.zeros((1, count, SPILL), jnp.float32)
        right = jnp.concatenate([zero, wide[:-1, :, outs : outs + SPILL]], 0)
        left = jnp.concatenate([wide[1:, :, outs + SPILL :], zero], 0)
        added = wide[:, :, :outs] + jnp.concatenate([right, none], 2) + jnp.concatenate([none, left], 2)
        early = late = [added.transpose(1, 0, 2).reshape(count, samples)]

    order = sorted(range(1, n_tgroup), key=lambda s: (s.bit_length(), -s))
    vectors = samples // LANES
    factor = 1.0 / math.sqrt(samples)

    def place(plan, use, name):
        return pl.pallas_call(
            functools.partial(place_kernel, n_chan, n_tgroup, outs, plan, steps),
            out_shape=[
                jax.ShapeDtypeStruct((tiles_in(group, vectors), 2 * CB, LANES), jnp.bfloat16)
                for _, group in plan
            ],
            in_specs=[smem()] + [vmem()] * len(use),
            out_specs=[vmem()] * len(plan),
            scratch_shapes=[
                pltpu.VMEM((count, samples), jnp.float32),
                pltpu.SMEM((n_tgroup * SLOTS,), jnp.int32),
            ],
            compiler_params=params(40),
            name=name,
        )(owners, *use)

    def hand_over(value, shift):
        return lax.ppermute(value, "tgroup", [(g, g ^ shift) for g in range(n_tgroup)])

    if outs % LANES == 0:
        early, got[half] = lax.optimization_barrier((early, got[half]))
        late = list(early) + got[half:]
    far = order[1:]
    first = place([(shift, 0) for shift in far], early, "place_first")
    arrived = {shift: [hand_over(value, shift)] for shift, value in zip(far, first)}
    plan = [(0, 2), (1, 2)] + [(shift, 1) for shift in far]
    own, near, *second = place(plan, late, "place_second")
    arrived[1] = [hand_over(near, 1)]
    result = correlate(n_chan, owners, (own,), (2,), None, factor, n_tgroup == 1, samples)
    for shift, value in zip(far, second):
        value, held = lax.optimization_barrier((value, arrived[shift][0]))
        if shift == far[-1]:
            value, result = lax.optimization_barrier((value, result))
        arrived[shift] = [held, hand_over(value, shift)]

    for shift in order:
        parts = (0, 1) if shift in far else (2,)
        operands = (owners, tuple(arrived[shift]), parts, result)
        result = correlate(n_chan, *operands, factor, shift == order[-1], samples)
    return result


def solution(mesh):
    in_specs = (P(("tgroup", "chan"), None), P(), P("chan"), P("chan", None))
    out_specs = P(("tgroup", "chan"), None, None, None)
    return jax.shard_map(local, mesh=mesh, in_specs=in_specs, out_specs=out_specs, check_vma=False)
```

```python
import functools
import math

import jax
import jax.numpy as jnp
from jax import lax
from jax.experimental import pallas as pl
from jax.experimental.pallas import tpu as pltpu
from jax.sharding import PartitionSpec as P

MAXLAG = 500
LAGS = 2 * MAXLAG + 1
TAPS = 255
CB = 8
K = 8
STRIPES = 2
SLOTS = 5
PAIRS = STRIPES * K
BLOCKS = STRIPES + SLOTS
WIDE = K * CB
SPILL = 64
LANES = 128
SHIFTS = 32
STEP = LANES // SHIFTS
LAG_BLOCKS = -(-LAGS // LANES)
FRONT = -(-MAXLAG // LANES) * LANES
NT = (((1,), (1,)), ((), ()))


def params(megabytes):
    return pltpu.CompilerParams(vmem_limit_bytes=megabytes << 20)


def vmem():
    return pl.BlockSpec(memory_space=pltpu.VMEM)


def smem():
    return pl.BlockSpec(memory_space=pltpu.SMEM)


def weights_kernel(taps, weights, held, line, sem):
    copy = pltpu.make_async_copy(taps, held, sem)
    copy.start()
    rows, outs, width = weights.shape[0], weights.shape[1] - 2 * SPILL, line.shape[1]
    line[...] = jnp.zeros_like(line)
    copy.wait()
    line[0:1, :TAPS] = held[...]
    spread = jnp.broadcast_to(line[0:1, :], (outs + 2 * SPILL, width))
    value = pltpu.roll(spread, width - 4 * SPILL + 1, 1, stride=2, stride_axis=0)[:, :rows]
    value = jnp.concatenate([value[SPILL : SPILL + outs], value[SPILL + outs :], value[:SPILL]], 0)
    weights[...] = value.T.astype(jnp.bfloat16)


def select_kernel(n_chan, groups, firsts, raw, weights, *refs):
    sends, (window, picked, sems) = refs[: len(groups)], refs[len(groups) :]
    rows, channels = raw.shape
    steps = [k for group in groups for k in group]
    stripes = len(steps) * STRIPES
    blocks_per = channels // n_chan // CB
    span = window.shape[2]
    me = lax.axis_index("chan")

    def place(p):
        c, k = me ^ steps[p // STRIPES], p % STRIPES
        start = (firsts[c, k] + c * blocks_per) * CB
        base = jnp.minimum(start - lax.rem(start, LANES), channels - span)
        return start, pl.multiple_of(base, LANES)

    def copy(p):
        base = place(p)[1]
        return pltpu.make_async_copy(raw.at[:, pl.ds(base, span)], window.at[p], sems.at[p])

    for p in range(stripes):
        copy(p).start()

    row = lax.broadcasted_iota(jnp.int32, (WIDE, span), 0)
    lane = lax.broadcasted_iota(jnp.int32, (WIDE, span), 1)
    batch = 2 * STRIPES
    for first in range(0, stripes, batch):
        last = min(first + batch, stripes)
        for p in range(first, last):
            copy(p).wait()
            start, base = place(p)
            hot = (lane == row + (start - base)) & (row < channels - start)
            hot = jnp.where(hot, 1.0, 0.0).astype(jnp.bfloat16)
            block = window[p].astype(jnp.bfloat16)
            chosen = lax.dot_general(hot, block, NT, preferred_element_type=jnp.float32)
            picked[p * WIDE : (p + 1) * WIDE, :] = chosen.astype(jnp.bfloat16)
        part = slice(first * WIDE, last * WIDE)
        result = jnp.dot(
            picked[part, :], weights[...], preferred_element_type=jnp.float32
        ).astype(jnp.bfloat16)
        height = STRIPES * WIDE
        for at in range((last - first) // STRIPES):
            k = steps[first // STRIPES + at]
            out, where = [(o, g.index(k)) for o, g in enumerate(groups) if k in g][0]
            sends[out][where * height : (where + 1) * height, :] = result[at * height : (at + 1) * height]


def add_spills(n_chan, outs, steps, got, total):
    count = total.shape[0]
    early = lax.broadcasted_iota(jnp.int32, (count, LANES), 1) < SPILL
    me = lax.axis_index("chan")
    pieces = [
        (me ^ k, ref.at[at * count : (at + 1) * count])
        for ks, ref in zip(steps, got)
        for at, k in enumerate(ks)
    ]
    for chunk, value in pieces:
        at = pl.ds(pl.multiple_of(chunk * outs, LANES), outs)
        total[:, at] = value[:, :outs].astype(jnp.float32)
    for chunk, value in pieces:
        spill = value[:, outs:].astype(jnp.float32)
        after = jnp.minimum(chunk + 1, n_chan - 1) * outs
        after = pl.ds(pl.multiple_of(after, LANES), LANES)
        total[:, after] += jnp.where(early & (chunk < n_chan - 1), spill, 0.0)
        before = jnp.maximum(chunk * outs, LANES) - LANES
        before = pl.ds(pl.multiple_of(before, LANES), LANES)
        total[:, before] += jnp.where(early | (chunk == 0), 0.0, spill)


def tile_of(group, width, vectors):
    half = vectors // 2
    if group == 0:
        return jnp.where(width == 0, 0, half + 1), half - 1
    if group == 1:
        return jnp.where(width == 0, half - 1, 0), half + 1
    return 0, vectors


def tiles_in(group, vectors):
    return -(-BLOCKS * tile_of(group, 0, vectors)[1] // 2)


def own_half(n_chan):
    return jnp.where(lax.axis_index("chan") < n_chan // 2, 0, 1)


def place_kernel(n_chan, n_tgroup, outs, plan, steps, owners, *refs):
    got, (total, pairs) = refs[: -len(plan) - 2], refs[-2:]
    sends = refs[-len(plan) - 2 : -2]
    me = lax.axis_index("tgroup")
    if len(got) == 1:
        total[...] = got[0][...]
    else:
        add_spills(n_chan, outs, steps, got, total)

    for at in range(n_tgroup * SLOTS):
        pairs[at] = -1
    counts = jnp.int32(0)
    for q in range(PAIRS):
        owner = owners[q]
        slot = (counts >> (3 * owner)) & 7
        counts = counts + (jnp.int32(1) << (3 * owner))
        pairs[(owner ^ me) * SLOTS + slot] = q

    zero = jnp.zeros((CB, LANES), jnp.float32)
    for send, (shift, group) in zip(sends, plan):
        base, per = tile_of(group, own_half(n_chan), total.shape[1] // LANES)

        def tiles(q):
            rows = pl.ds(pl.multiple_of(q * CB, CB), CB)
            return [
                total[rows, pl.ds(pl.multiple_of((base + j) * LANES, LANES), LANES)]
                for j in range(per)
            ]

        parts = sum([tiles(p * K) for p in range(STRIPES)], [])
        for s in range(SLOTS):
            q = pairs[shift * SLOTS + s]
            parts += [jnp.where(q >= 0, tile, 0.0) for tile in tiles(jnp.maximum(q, 0))]
        parts += [zero] * (len(parts) % 2)
        for at in range(0, len(parts), 2):
            value = jnp.concatenate(parts[at : at + 2], 0)
            send[at // 2] = value.astype(jnp.bfloat16)


def correlate_kernel(n_chan, groups, factor, last, owners, *refs):
    lead, window_a, window_b, whole = refs[-4:]
    out = refs[-5]
    arrived = refs[: len(groups)]
    before = refs[len(groups)] if len(refs) > len(groups) + 5 else None
    windows = (window_a, window_b)
    span = lead.shape[2]
    samples = span - LANES
    cols = span // LANES
    high = STEP * CB
    ahead = FRONT // LANES - 1
    me = lax.axis_index("tgroup")
    first_count = jnp.int32(0)
    for q in range(K):
        first_count += jnp.where(owners[q] == me, 1, 0)

    for ref, group in zip(arrived, groups):
        base, per = tile_of(group, own_half(n_chan), samples // LANES)
        for at in range(ref.shape[0]):
            value = ref[at].astype(jnp.float32)
            for part in range(2):
                block, j = (2 * at + part) // per, (2 * at + part) % per
                if block < BLOCKS:
                    lanes = pl.ds(pl.multiple_of((base + j) * LANES, LANES), LANES)
                    whole[block, :, lanes] = value[part * CB : (part + 1) * CB]

    def series(block):
        return jnp.concatenate([whole[block], jnp.zeros((CB, LANES), jnp.float32)], 1)

    for p in range(STRIPES):
        value = series(p)
        for a in range(CB):
            spread = jnp.broadcast_to(value[a : a + 1], (SHIFTS, span))
            turned = pltpu.roll(spread, 0, 1, stride=1, stride_axis=0)
            lead[p, a * SHIFTS : (a + 1) * SHIFTS, :] = turned.astype(jnp.bfloat16)

    def bounds(i):
        return max(0, ahead - i), min(cols, ahead + cols - i)

    for window in windows:
        for i in range(LAG_BLOCKS):
            first, end = bounds(i)
            rows = slice(i * high, (i + 1) * high)
            if first > 0:
                window[rows, : first * LANES] = jnp.zeros((high, first * LANES), jnp.bfloat16)
            if end < cols:
                window[rows, end * LANES :] = jnp.zeros((high, (cols - end) * LANES), jnp.bfloat16)

    group = lax.broadcasted_iota(jnp.int32, (CB, LANES), 1) // SHIFTS
    for s in range(SLOTS):
        window = windows[s % 2]
        value = series(STRIPES + s)
        turned = [pltpu.roll(value, span - (FRONT - MAXLAG + SHIFTS * n), 1) for n in range(STEP)]
        stacked = jnp.concatenate(turned, 0).astype(jnp.bfloat16)
        stacked = jnp.concatenate([stacked[:, samples:], stacked[:, :samples]], 1)
        for i in range(LAG_BLOCKS):
            first, end = bounds(i)
            window[i * high : (i + 1) * high, first * LANES : end * LANES] = stacked[
                :, (first + i - ahead) * LANES : (end + i - ahead) * LANES
            ]
        which = jnp.where(s < first_count, 0, 1)
        summed = lax.dot_general(window[...], lead[which], NT, preferred_element_type=jnp.float32)
        if before is not None:
            summed = summed + before[s]
        if not last:
            out[s] = summed
            continue
        summed = summed * factor
        for i in range(LAG_BLOCKS):
            width = min(LANES, LAGS - i * LANES)
            for h in range(CB // STEP):
                parts = [
                    summed[(i * STEP + n) * CB : (i * STEP + n + 1) * CB, h * LANES : (h + 1) * LANES]
                    for n in range(STEP)
                ]
                for a in range(STEP):
                    value = parts[a]
                    for n in range(STEP):
                        if n != a:
                            moved = pltpu.roll(parts[n], (SHIFTS * (n - a)) % LANES, 1)
                            value = jnp.where(group == n, moved, value)
                    out[s, h * STEP + a, :, i * LANES : i * LANES + width] = value[:, :width]


def correlate(n_chan, owners, arrived, groups, before, factor, last, samples):
    high, wide = STEP * LAG_BLOCKS * CB, CB * SHIFTS
    if last:
        shape = jax.ShapeDtypeStruct((SLOTS, CB, CB, LAGS), jnp.float32)
    else:
        shape = jax.ShapeDtypeStruct((SLOTS, high, wide), jnp.float32)
    operands = (owners,) + arrived + (() if before is None else (before,))
    depth = samples + LANES
    return pl.pallas_call(
        functools.partial(correlate_kernel, n_chan, groups, factor, last),
        out_shape=shape,
        in_specs=[smem()] + [vmem()] * (len(operands) - 1),
        out_specs=vmem(),
        scratch_shapes=[
            pltpu.VMEM((STRIPES, wide, depth), jnp.bfloat16),
            pltpu.VMEM((high, depth), jnp.bfloat16),
            pltpu.VMEM((high, depth), jnp.bfloat16),
            pltpu.VMEM((BLOCKS, CB, samples), jnp.float32),
        ],
        compiler_params=params(40),
        name="correlate_last" if last else "correlate",
    )(*operands)


def local(raw_strain, whitening_taps, first_block, pair_owner):
    n_chan, n_tgroup = lax.axis_size("chan"), lax.axis_size("tgroup")
    rows, channels = raw_strain.shape
    outs = rows // 2
    samples = outs * n_chan
    count = PAIRS * CB
    owners = pair_owner[:, 0]

    firsts = lax.all_to_all(
        jnp.broadcast_to(first_block[None, :], (n_chan, STRIPES)),
        "chan",
        split_axis=0,
        concat_axis=0,
        tiled=True,
    )
    line = -(-(rows + 2 * outs + 4 * SPILL) // (2 * LANES)) * 2 * LANES
    weights = pl.pallas_call(
        weights_kernel,
        out_shape=jax.ShapeDtypeStruct((rows, outs + 2 * SPILL), jnp.bfloat16),
        in_specs=[pl.BlockSpec(memory_space=pl.ANY)],
        out_specs=vmem(),
        scratch_shapes=[
            pltpu.VMEM((1, TAPS), jnp.float32),
            pltpu.VMEM((8, line), jnp.float32),
            pltpu.SemaphoreType.DMA,
        ],
        compiler_params=params(40),
        name="fir_weights",
    )(whitening_taps.reshape(1, TAPS))

    split = n_chan == 8 and outs % LANES == 0
    pieces = {}
    for part in ([2, 3, 4], [1, 5, 6, 7, 0]) if split else (range(n_chan),):
        part = list(part)
        if pieces:
            weights, _ = lax.optimization_barrier((weights, list(pieces.values())))
        made = pl.pallas_call(
            functools.partial(select_kernel, n_chan, [[k] for k in part]),
            out_shape=[jax.ShapeDtypeStruct((count, outs + 2 * SPILL), jnp.bfloat16)] * len(part),
            in_specs=[smem(), pl.BlockSpec(memory_space=pl.ANY), vmem()],
            out_specs=[vmem()] * len(part),
            scratch_shapes=[
                pltpu.VMEM((len(part) * STRIPES, rows, 2 * LANES), jnp.float32),
                pltpu.VMEM((len(part) * count, rows), jnp.bfloat16),
                pltpu.SemaphoreType.DMA((len(part) * STRIPES,)),
            ],
            compiler_params=params(40),
            name="select_filter",
        )(firsts, raw_strain, weights)
        pieces.update(zip(part, made))
    def exchange(value, k):
        return lax.ppermute(value, "chan", [(c, c ^ k) for c in range(n_chan)])

    half = n_chan // 2
    moved = {}
    for k, value in pieces.items():
        if split and k in (1, 5):
            held = 2 if k == 1 else 3
            value, moved[held] = lax.optimization_barrier((value, moved[held]))
        if k:
            moved[k] = exchange(value, k)
    got = [pieces[0]] + [moved[k] for k in range(1, n_chan)]
    steps = [[k] for k in ([2, 3, 1, 0, 4, 5, 6, 7] if split else range(n_chan))]
    got = [got[k] for (k,) in steps]
    early, late = got[:half], got

    if outs % LANES:
        wide = jnp.stack(got).astype(jnp.float32)
        wide = jnp.take(wide, lax.axis_index("chan") ^ jnp.arange(n_chan), axis=0)
        none = jnp.zeros((n_chan, count, outs - SPILL), jnp.float32)
        zero = jnp.zeros((1, count, SPILL), jnp.float32)
        right = jnp.concatenate([zero, wide[:-1, :, outs : outs + SPILL]], 0)
        left = jnp.concatenate([wide[1:, :, outs + SPILL :], zero], 0)
        added = wide[:, :, :outs] + jnp.concatenate([right, none], 2) + jnp.concatenate([none, left], 2)
        early = late = [added.transpose(1, 0, 2).reshape(count, samples)]

    order = sorted(range(1, n_tgroup), key=lambda s: (s.bit_length(), -s))
    vectors = samples // LANES
    factor = 1.0 / math.sqrt(samples)

    def place(plan, use, name):
        return pl.pallas_call(
            functools.partial(place_kernel, n_chan, n_tgroup, outs, plan, steps),
            out_shape=[
                jax.ShapeDtypeStruct((tiles_in(group, vectors), 2 * CB, LANES), jnp.bfloat16)
                for _, group in plan
            ],
            in_specs=[smem()] + [vmem()] * len(use),
            out_specs=[vmem()] * len(plan),
            scratch_shapes=[
                pltpu.VMEM((count, samples), jnp.float32),
                pltpu.SMEM((n_tgroup * SLOTS,), jnp.int32),
            ],
            compiler_params=params(40),
            name=name,
        )(owners, *use)

    def hand_over(value, shift):
        return lax.ppermute(value, "tgroup", [(g, g ^ shift) for g in range(n_tgroup)])

    if outs % LANES == 0:
        held = early[:2] + got[half : half + 1] + early[2:]
        held = lax.optimization_barrier(held)
        early = held[:2] + held[3:]
        late = early + held[2:3] + got[half + 1 :]
    far = order[1:]
    first = place([(shift, 0) for shift in far], early, "place_first")
    arrived = {shift: [hand_over(value, shift)] for shift, value in zip(far, first)}
    plan = [(0, 2), (1, 2)] + [(shift, 1) for shift in far]
    own, near, *second = place(plan, late, "place_second")
    arrived[0], arrived[1] = [own], [hand_over(near, 1)]
    for shift, value in zip(far, second):
        value, held = lax.optimization_barrier((value, arrived[shift][0]))
        arrived[shift] = [held, hand_over(value, shift)]

    value = None
    for at, shift in enumerate([0] + order):
        parts = (0, 1) if shift in far else (2,)
        last = at == n_tgroup - 1
        value = correlate(
            n_chan, owners, tuple(arrived[shift]), parts, value, factor, last, samples
        )
    return value


def solution(mesh):
    in_specs = (P(("tgroup", "chan"), None), P(), P("chan"), P("chan", None))
    out_specs = P(("tgroup", "chan"), None, None, None)
    return jax.shard_map(local, mesh=mesh, in_specs=in_specs, out_specs=out_specs, check_vma=False)
```

```python
import functools
import math

import jax
import jax.numpy as jnp
from jax import lax
from jax.experimental import pallas as pl
from jax.experimental.pallas import tpu as pltpu
from jax.sharding import PartitionSpec as P

MAXLAG = 500
LAGS = 2 * MAXLAG + 1
TAPS = 255
CB = 8
K = 8
STRIPES = 2
SLOTS = 5
PAIRS = STRIPES * K
BLOCKS = STRIPES + SLOTS
WIDE = K * CB
SPILL = 64
LANES = 128
SHIFTS = 32
STEP = LANES // SHIFTS
LAG_BLOCKS = -(-LAGS // LANES)
FRONT = -(-MAXLAG // LANES) * LANES
NT = (((1,), (1,)), ((), ()))


def params(megabytes):
    return pltpu.CompilerParams(vmem_limit_bytes=megabytes << 20)


def vmem():
    return pl.BlockSpec(memory_space=pltpu.VMEM)


def smem():
    return pl.BlockSpec(memory_space=pltpu.SMEM)


def weights_kernel(taps, weights, held, line, sem):
    copy = pltpu.make_async_copy(taps, held, sem)
    copy.start()
    rows, outs, width = weights.shape[0], weights.shape[1] - 2 * SPILL, line.shape[1]
    line[...] = jnp.zeros_like(line)
    copy.wait()
    line[0:1, :TAPS] = held[...]
    spread = jnp.broadcast_to(line[0:1, :], (outs + 2 * SPILL, width))
    value = pltpu.roll(spread, width - 4 * SPILL + 1, 1, stride=2, stride_axis=0)[:, :rows]
    value = jnp.concatenate([value[SPILL : SPILL + outs], value[SPILL + outs :], value[:SPILL]], 0)
    weights[...] = value.T.astype(jnp.bfloat16)


def select_kernel(n_chan, groups, firsts, raw, weights, *refs):
    sends, (window, picked, sems) = refs[: len(groups)], refs[len(groups) :]
    rows, channels = raw.shape
    steps = [k for group in groups for k in group]
    stripes = n_chan * STRIPES
    blocks_per = channels // n_chan // CB
    span = window.shape[2]
    me = lax.axis_index("chan")

    def place(p):
        c, k = me ^ steps[p // STRIPES], p % STRIPES
        start = (firsts[c, k] + c * blocks_per) * CB
        base = jnp.minimum(start - lax.rem(start, LANES), channels - span)
        return start, pl.multiple_of(base, LANES)

    def copy(p):
        base = place(p)[1]
        return pltpu.make_async_copy(raw.at[:, pl.ds(base, span)], window.at[p], sems.at[p])

    for p in range(stripes):
        copy(p).start()

    row = lax.broadcasted_iota(jnp.int32, (WIDE, span), 0)
    lane = lax.broadcasted_iota(jnp.int32, (WIDE, span), 1)
    batch = 2 * STRIPES
    for first in range(0, stripes, batch):
        for p in range(first, first + batch):
            copy(p).wait()
            start, base = place(p)
            hot = (lane == row + (start - base)) & (row < channels - start)
            hot = jnp.where(hot, 1.0, 0.0).astype(jnp.bfloat16)
            block = window[p].astype(jnp.bfloat16)
            chosen = lax.dot_general(hot, block, NT, preferred_element_type=jnp.float32)
            picked[p * WIDE : (p + 1) * WIDE, :] = chosen.astype(jnp.bfloat16)
        part = slice(first * WIDE, (first + batch) * WIDE)
        result = jnp.dot(
            picked[part, :], weights[...], preferred_element_type=jnp.float32
        ).astype(jnp.bfloat16)
        height = STRIPES * WIDE
        for at in range(batch // STRIPES):
            k = steps[first // STRIPES + at]
            out, where = [(o, g.index(k)) for o, g in enumerate(groups) if k in g][0]
            sends[out][where * height : (where + 1) * height, :] = result[at * height : (at + 1) * height]


def add_spills(n_chan, outs, steps, got, total):
    count = total.shape[0]
    early = lax.broadcasted_iota(jnp.int32, (count, LANES), 1) < SPILL
    me = lax.axis_index("chan")
    pieces = [
        (me ^ k, ref.at[at * count : (at + 1) * count])
        for ks, ref in zip(steps, got)
        for at, k in enumerate(ks)
    ]
    for chunk, value in pieces:
        at = pl.ds(pl.multiple_of(chunk * outs, LANES), outs)
        total[:, at] = value[:, :outs].astype(jnp.float32)
    for chunk, value in pieces:
        spill = value[:, outs:].astype(jnp.float32)
        after = jnp.minimum(chunk + 1, n_chan - 1) * outs
        after = pl.ds(pl.multiple_of(after, LANES), LANES)
        total[:, after] += jnp.where(early & (chunk < n_chan - 1), spill, 0.0)
        before = jnp.maximum(chunk * outs, LANES) - LANES
        before = pl.ds(pl.multiple_of(before, LANES), LANES)
        total[:, before] += jnp.where(early | (chunk == 0), 0.0, spill)


def tile_of(group, width, vectors):
    half = vectors // 2
    if group == 0:
        return jnp.where(width == 0, 0, half + 1), half - 1
    if group == 1:
        return jnp.where(width == 0, half - 1, 0), half + 1
    return 0, vectors


def tiles_in(group, vectors):
    return -(-BLOCKS * tile_of(group, 0, vectors)[1] // 2)


def own_half(n_chan):
    return jnp.where(lax.axis_index("chan") < n_chan // 2, 0, 1)


def place_kernel(n_chan, n_tgroup, outs, plan, steps, owners, *refs):
    got, (total, pairs) = refs[: -len(plan) - 2], refs[-2:]
    sends = refs[-len(plan) - 2 : -2]
    me = lax.axis_index("tgroup")
    if len(got) == 1:
        total[...] = got[0][...]
    else:
        add_spills(n_chan, outs, steps, got, total)

    for at in range(n_tgroup * SLOTS):
        pairs[at] = -1
    counts = jnp.int32(0)
    for q in range(PAIRS):
        owner = owners[q]
        slot = (counts >> (3 * owner)) & 7
        counts = counts + (jnp.int32(1) << (3 * owner))
        pairs[(owner ^ me) * SLOTS + slot] = q

    zero = jnp.zeros((CB, LANES), jnp.float32)
    for send, (shift, group) in zip(sends, plan):
        base, per = tile_of(group, own_half(n_chan), total.shape[1] // LANES)

        def tiles(q):
            rows = pl.ds(pl.multiple_of(q * CB, CB), CB)
            return [
                total[rows, pl.ds(pl.multiple_of((base + j) * LANES, LANES), LANES)]
                for j in range(per)
            ]

        parts = sum([tiles(p * K) for p in range(STRIPES)], [])
        for s in range(SLOTS):
            q = pairs[shift * SLOTS + s]
            parts += [jnp.where(q >= 0, tile, 0.0) for tile in tiles(jnp.maximum(q, 0))]
        parts += [zero] * (len(parts) % 2)
        for at in range(0, len(parts), 2):
            value = jnp.concatenate(parts[at : at + 2], 0)
            send[at // 2] = value.astype(jnp.bfloat16)


def correlate_kernel(n_chan, groups, factor, last, owners, *refs):
    near, far, windows, whole, parts_sum = refs[-5:]
    out = refs[-6]
    arrived = refs[: len(groups)]
    before = refs[len(groups)] if len(refs) > len(groups) + 6 else None
    cut = near.shape[2]
    span = cut + far.shape[2]
    samples = span - LANES
    cols = span // LANES
    high = STEP * CB
    ahead = FRONT // LANES - 1
    me = lax.axis_index("tgroup")
    first_count = jnp.int32(0)
    for q in range(K):
        first_count += jnp.where(owners[q] == me, 1, 0)

    for ref, group in zip(arrived, groups):
        base, per = tile_of(group, own_half(n_chan), samples // LANES)
        for at in range(ref.shape[0]):
            value = ref[at].astype(jnp.float32)
            for part in range(2):
                block, j = (2 * at + part) // per, (2 * at + part) % per
                if block < BLOCKS:
                    lanes = pl.ds(pl.multiple_of((base + j) * LANES, LANES), LANES)
                    whole[block, :, lanes] = value[part * CB : (part + 1) * CB]

    def series(block):
        return jnp.concatenate([whole[block], jnp.zeros((CB, LANES), jnp.float32)], 1)

    for p in range(STRIPES):
        value = series(p)
        for a in range(CB):
            spread = jnp.broadcast_to(value[a : a + 1], (SHIFTS, span))
            turned = pltpu.roll(spread, 0, 1, stride=1, stride_axis=0)
            turned = turned.astype(jnp.bfloat16)
            near[p, a * SHIFTS : (a + 1) * SHIFTS, :] = turned[:, :cut]
            far[p, a * SHIFTS : (a + 1) * SHIFTS, :] = turned[:, cut:]

    def bounds(i):
        return max(0, ahead - i), min(cols, ahead + cols - i)

    def make_window(s):
        for i in range(LAG_BLOCKS):
            first, end = bounds(i)
            rows = slice(i * high, (i + 1) * high)
            if first > 0:
                windows[s, rows, : first * LANES] = jnp.zeros((high, first * LANES), jnp.bfloat16)
            if end < cols:
                windows[s, rows, end * LANES :] = jnp.zeros(
                    (high, (cols - end) * LANES), jnp.bfloat16
                )
        value = series(STRIPES + s)
        turned = [pltpu.roll(value, span - (FRONT - MAXLAG + SHIFTS * n), 1) for n in range(STEP)]
        stacked = jnp.concatenate(turned, 0).astype(jnp.bfloat16)
        stacked = jnp.concatenate([stacked[:, samples:], stacked[:, :samples]], 1)
        for i in range(LAG_BLOCKS):
            first, end = bounds(i)
            windows[s, i * high : (i + 1) * high, first * LANES : end * LANES] = stacked[
                :, (first + i - ahead) * LANES : (end + i - ahead) * LANES
            ]

    which = [jnp.where(s < first_count, 0, 1) for s in range(SLOTS)]
    for s in range(SLOTS):
        make_window(s)
        value = lax.dot_general(
            windows[s, :, :cut], near[which[s]], NT, preferred_element_type=jnp.float32
        )
        parts_sum[s] = value if before is None else value + before[s]

    group = lax.broadcasted_iota(jnp.int32, (CB, LANES), 1) // SHIFTS
    for s in range(SLOTS):
        summed = parts_sum[s] + lax.dot_general(
            windows[s, :, cut:], far[which[s]], NT, preferred_element_type=jnp.float32
        )
        if not last:
            out[s] = summed
            continue
        summed = summed * factor
        for i in range(LAG_BLOCKS):
            width = min(LANES, LAGS - i * LANES)
            for h in range(CB // STEP):
                parts = [
                    summed[(i * STEP + n) * CB : (i * STEP + n + 1) * CB, h * LANES : (h + 1) * LANES]
                    for n in range(STEP)
                ]
                for a in range(STEP):
                    value = parts[a]
                    for n in range(STEP):
                        if n != a:
                            moved = pltpu.roll(parts[n], (SHIFTS * (n - a)) % LANES, 1)
                            value = jnp.where(group == n, moved, value)
                    out[s, h * STEP + a, :, i * LANES : i * LANES + width] = value[:, :width]


def correlate(n_chan, owners, arrived, groups, before, factor, last, samples):
    high, wide = STEP * LAG_BLOCKS * CB, CB * SHIFTS
    if last:
        shape = jax.ShapeDtypeStruct((SLOTS, CB, CB, LAGS), jnp.float32)
    else:
        shape = jax.ShapeDtypeStruct((SLOTS, high, wide), jnp.float32)
    operands = (owners,) + arrived + (() if before is None else (before,))
    depth, cut = samples + LANES, samples // 2
    return pl.pallas_call(
        functools.partial(correlate_kernel, n_chan, groups, factor, last),
        out_shape=shape,
        in_specs=[smem()] + [vmem()] * (len(operands) - 1),
        out_specs=vmem(),
        scratch_shapes=[
            pltpu.VMEM((STRIPES, wide, cut), jnp.bfloat16),
            pltpu.VMEM((STRIPES, wide, depth - cut), jnp.bfloat16),
            pltpu.VMEM((SLOTS, high, depth), jnp.bfloat16),
            pltpu.VMEM((BLOCKS, CB, samples), jnp.float32),
            pltpu.VMEM((SLOTS, high, wide), jnp.float32),
        ],
        compiler_params=params(40),
        name="correlate_last" if last else "correlate",
    )(*operands)


def local(raw_strain, whitening_taps, first_block, pair_owner):
    n_chan, n_tgroup = lax.axis_size("chan"), lax.axis_size("tgroup")
    rows, channels = raw_strain.shape
    outs = rows // 2
    samples = outs * n_chan
    count = PAIRS * CB
    owners = pair_owner[:, 0]

    firsts = lax.all_to_all(
        jnp.broadcast_to(first_block[None, :], (n_chan, STRIPES)),
        "chan",
        split_axis=0,
        concat_axis=0,
        tiled=True,
    )
    line = -(-(rows + 2 * outs + 4 * SPILL) // (2 * LANES)) * 2 * LANES
    weights = pl.pallas_call(
        weights_kernel,
        out_shape=jax.ShapeDtypeStruct((rows, outs + 2 * SPILL), jnp.bfloat16),
        in_specs=[pl.BlockSpec(memory_space=pl.ANY)],
        out_specs=vmem(),
        scratch_shapes=[
            pltpu.VMEM((1, TAPS), jnp.float32),
            pltpu.VMEM((8, line), jnp.float32),
            pltpu.SemaphoreType.DMA,
        ],
        compiler_params=params(40),
        name="fir_weights",
    )(whitening_taps.reshape(1, TAPS))

    groups = [[k] for k in range(n_chan)]
    sends = pl.pallas_call(
        functools.partial(select_kernel, n_chan, groups),
        out_shape=[
            jax.ShapeDtypeStruct((len(group) * count, outs + 2 * SPILL), jnp.bfloat16)
            for group in groups
        ],
        in_specs=[smem(), pl.BlockSpec(memory_space=pl.ANY), vmem()],
        out_specs=[vmem()] * len(groups),
        scratch_shapes=[
            pltpu.VMEM((n_chan * STRIPES, rows, 2 * LANES), jnp.float32),
            pltpu.VMEM((n_chan * count, rows), jnp.bfloat16),
            pltpu.SemaphoreType.DMA((n_chan * STRIPES,)),
        ],
        compiler_params=params(40),
        name="select_filter",
    )(firsts, raw_strain, weights)

    def exchange(value, k):
        return lax.ppermute(value, "chan", [(c, c ^ k) for c in range(n_chan)])

    half = n_chan // 2
    got = [sends[0]] + [exchange(sends[k], k) for k in range(1, n_chan)]
    steps = [[k] for k in range(n_chan)]
    early, late = got[:half], got

    if outs % LANES:
        wide = jnp.stack(got).astype(jnp.float32)
        wide = jnp.take(wide, lax.axis_index("chan") ^ jnp.arange(n_chan), axis=0)
        none = jnp.zeros((n_chan, count, outs - SPILL), jnp.float32)
        zero = jnp.zeros((1, count, SPILL), jnp.float32)
        right = jnp.concatenate([zero, wide[:-1, :, outs : outs + SPILL]], 0)
        left = jnp.concatenate([wide[1:, :, outs + SPILL :], zero], 0)
        added = wide[:, :, :outs] + jnp.concatenate([right, none], 2) + jnp.concatenate([none, left], 2)
        early = late = [added.transpose(1, 0, 2).reshape(count, samples)]

    order = sorted(range(1, n_tgroup), key=lambda s: (s.bit_length(), -s))
    vectors = samples // LANES
    factor = 1.0 / math.sqrt(samples)

    def place(plan, use, name):
        return pl.pallas_call(
            functools.partial(place_kernel, n_chan, n_tgroup, outs, plan, steps),
            out_shape=[
                jax.ShapeDtypeStruct((tiles_in(group, vectors), 2 * CB, LANES), jnp.bfloat16)
                for _, group in plan
            ],
            in_specs=[smem()] + [vmem()] * len(use),
            out_specs=[vmem()] * len(plan),
            scratch_shapes=[
                pltpu.VMEM((count, samples), jnp.float32),
                pltpu.SMEM((n_tgroup * SLOTS,), jnp.int32),
            ],
            compiler_params=params(40),
            name=name,
        )(owners, *use)

    def hand_over(value, shift):
        return lax.ppermute(value, "tgroup", [(g, g ^ shift) for g in range(n_tgroup)])

    if outs % LANES == 0:
        early, got[half] = lax.optimization_barrier((early, got[half]))
        late = list(early) + got[half:]
    far = order[1:]
    first = place([(shift, 0) for shift in far], early, "place_first")
    arrived = {shift: [hand_over(value, shift)] for shift, value in zip(far, first)}
    plan = [(0, 2), (1, 2)] + [(shift, 1) for shift in far]
    own, near, *second = place(plan, late, "place_second")
    arrived[0], arrived[1] = [own], [hand_over(near, 1)]
    for shift, value in zip(far, second):
        value, held = lax.optimization_barrier((value, arrived[shift][0]))
        arrived[shift] = [held, hand_over(value, shift)]

    value = None
    for at, shift in enumerate([0] + order):
        parts = (0, 1) if shift in far else (2,)
        last = at == n_tgroup - 1
        value = correlate(
            n_chan, owners, tuple(arrived[shift]), parts, value, factor, last, samples
        )
    return value


def solution(mesh):
    in_specs = (P(("tgroup", "chan"), None), P(), P("chan"), P("chan", None))
    out_specs = P(("tgroup", "chan"), None, None, None)
    return jax.shard_map(local, mesh=mesh, in_specs=in_specs, out_specs=out_specs, check_vma=False)
```

```python
import functools
import math

import jax
import jax.numpy as jnp
from jax import lax
from jax.experimental import pallas as pl
from jax.experimental.pallas import tpu as pltpu
from jax.sharding import PartitionSpec as P

MAXLAG = 500
LAGS = 2 * MAXLAG + 1
TAPS = 255
CB = 8
K = 8
STRIPES = 2
SLOTS = 5
PAIRS = STRIPES * K
BLOCKS = STRIPES + SLOTS
WIDE = K * CB
SPILL = 64
LANES = 128
SHIFTS = 32
STEP = LANES // SHIFTS
LAG_BLOCKS = -(-LAGS // LANES)
FRONT = -(-MAXLAG // LANES) * LANES
NT = (((1,), (1,)), ((), ()))


def params(megabytes):
    return pltpu.CompilerParams(vmem_limit_bytes=megabytes << 20)


def vmem():
    return pl.BlockSpec(memory_space=pltpu.VMEM)


def smem():
    return pl.BlockSpec(memory_space=pltpu.SMEM)


def weights_kernel(taps, weights, held, line, sem):
    copy = pltpu.make_async_copy(taps, held, sem)
    copy.start()
    rows, outs, width = weights.shape[0], weights.shape[1] - 2 * SPILL, line.shape[1]
    line[...] = jnp.zeros_like(line)
    copy.wait()
    line[0:1, :TAPS] = held[...]
    spread = jnp.broadcast_to(line[0:1, :], (outs + 2 * SPILL, width))
    value = pltpu.roll(spread, width - 4 * SPILL + 1, 1, stride=2, stride_axis=0)[:, :rows]
    value = jnp.concatenate([value[SPILL : SPILL + outs], value[SPILL + outs :], value[:SPILL]], 0)
    weights[...] = value.T.astype(jnp.bfloat16)


def select_kernel(n_chan, groups, firsts, raw, weights, *refs):
    sends, (window, picked, sems) = refs[: len(groups)], refs[len(groups) :]
    rows, channels = raw.shape
    steps = [k for group in groups for k in group]
    stripes = n_chan * STRIPES
    blocks_per = channels // n_chan // CB
    span = window.shape[2]
    me = lax.axis_index("chan")

    def place(p):
        c, k = me ^ steps[p // STRIPES], p % STRIPES
        start = (firsts[c, k] + c * blocks_per) * CB
        offset = lax.rem(start, LANES)
        base = start - offset
        return start, offset, base, (offset > LANES - WIDE) & (base < channels - LANES)

    def copy(p, tile):
        base = place(p)[2]
        if tile:
            base = jnp.minimum(base + LANES, channels - LANES)
        return pltpu.make_async_copy(
            raw.at[:, pl.ds(pl.multiple_of(base, LANES), LANES)],
            window.at[p, :, pl.ds(tile * LANES, LANES)],
            sems.at[p, tile],
        )

    for p in range(stripes):
        copy(p, 0).start()

        @pl.when(place(p)[3])
        def _(p=p):
            copy(p, 1).start()

    for p in range(stripes):

        @pl.when(jnp.logical_not(place(p)[3]))
        def _(p=p):
            window[p, :, LANES:] = jnp.zeros((rows, LANES), jnp.float32)

    row = lax.broadcasted_iota(jnp.int32, (WIDE, span), 0)
    lane = lax.broadcasted_iota(jnp.int32, (WIDE, span), 1)
    batch = 2 * STRIPES
    for first in range(0, stripes, batch):
        for p in range(first, first + batch):
            copy(p, 0).wait()

            @pl.when(place(p)[3])
            def _(p=p):
                copy(p, 1).wait()

        for p in range(first, first + batch):
            start, offset, _, _ = place(p)
            hot = (lane == row + offset) & (row < channels - start)
            hot = jnp.where(hot, 1.0, 0.0).astype(jnp.bfloat16)
            block = window[p].astype(jnp.bfloat16)
            chosen = lax.dot_general(hot, block, NT, preferred_element_type=jnp.float32)
            picked[p * WIDE : (p + 1) * WIDE, :] = chosen.astype(jnp.bfloat16)
        part = slice(first * WIDE, (first + batch) * WIDE)
        result = jnp.dot(
            picked[part, :], weights[...], preferred_element_type=jnp.float32
        ).astype(jnp.bfloat16)
        height = STRIPES * WIDE
        for at in range(batch // STRIPES):
            k = steps[first // STRIPES + at]
            out, where = [(o, g.index(k)) for o, g in enumerate(groups) if k in g][0]
            sends[out][where * height : (where + 1) * height, :] = result[at * height : (at + 1) * height]


def add_spills(n_chan, outs, steps, got, total):
    count = total.shape[0]
    early = lax.broadcasted_iota(jnp.int32, (count, LANES), 1) < SPILL
    me = lax.axis_index("chan")
    pieces = [
        (me ^ k, ref.at[at * count : (at + 1) * count])
        for ks, ref in zip(steps, got)
        for at, k in enumerate(ks)
    ]
    for chunk, value in pieces:
        at = pl.ds(pl.multiple_of(chunk * outs, LANES), outs)
        total[:, at] = value[:, :outs].astype(jnp.float32)
    for chunk, value in pieces:
        spill = value[:, outs:].astype(jnp.float32)
        after = jnp.minimum(chunk + 1, n_chan - 1) * outs
        after = pl.ds(pl.multiple_of(after, LANES), LANES)
        total[:, after] += jnp.where(early & (chunk < n_chan - 1), spill, 0.0)
        before = jnp.maximum(chunk * outs, LANES) - LANES
        before = pl.ds(pl.multiple_of(before, LANES), LANES)
        total[:, before] += jnp.where(early | (chunk == 0), 0.0, spill)


def tile_of(group, width, vectors):
    half = vectors // 2
    if group == 0:
        return jnp.where(width == 0, 0, half + 1), half - 1
    if group == 1:
        return jnp.where(width == 0, half - 1, 0), half + 1
    return 0, vectors


def tiles_in(group, vectors):
    return -(-BLOCKS * tile_of(group, 0, vectors)[1] // 2)


def own_half(n_chan):
    return jnp.where(lax.axis_index("chan") < n_chan // 2, 0, 1)


def place_kernel(n_chan, n_tgroup, outs, plan, steps, owners, *refs):
    got, (total, pairs) = refs[: -len(plan) - 2], refs[-2:]
    sends = refs[-len(plan) - 2 : -2]
    me = lax.axis_index("tgroup")
    if len(got) == 1:
        total[...] = got[0][...]
    else:
        add_spills(n_chan, outs, steps, got, total)

    for at in range(n_tgroup * SLOTS):
        pairs[at] = -1
    counts = jnp.int32(0)
    for q in range(PAIRS):
        owner = owners[q]
        slot = (counts >> (3 * owner)) & 7
        counts = counts + (jnp.int32(1) << (3 * owner))
        pairs[(owner ^ me) * SLOTS + slot] = q

    zero = jnp.zeros((CB, LANES), jnp.float32)
    for send, (shift, group) in zip(sends, plan):
        base, per = tile_of(group, own_half(n_chan), total.shape[1] // LANES)

        def tiles(q):
            rows = pl.ds(pl.multiple_of(q * CB, CB), CB)
            return [
                total[rows, pl.ds(pl.multiple_of((base + j) * LANES, LANES), LANES)]
                for j in range(per)
            ]

        parts = sum([tiles(p * K) for p in range(STRIPES)], [])
        for s in range(SLOTS):
            q = pairs[shift * SLOTS + s]
            parts += [jnp.where(q >= 0, tile, 0.0) for tile in tiles(jnp.maximum(q, 0))]
        parts += [zero] * (len(parts) % 2)
        for at in range(0, len(parts), 2):
            value = jnp.concatenate(parts[at : at + 2], 0)
            send[at // 2] = value.astype(jnp.bfloat16)


def correlate_kernel(n_chan, groups, factor, last, owners, *refs):
    near, far, windows, whole, parts_sum = refs[-5:]
    out = refs[-6]
    arrived = refs[: len(groups)]
    before = refs[len(groups)] if len(refs) > len(groups) + 6 else None
    cut = near.shape[2]
    span = cut + far.shape[2]
    samples = span - LANES
    cols = span // LANES
    high = STEP * CB
    ahead = FRONT // LANES - 1
    me = lax.axis_index("tgroup")
    first_count = jnp.int32(0)
    for q in range(K):
        first_count += jnp.where(owners[q] == me, 1, 0)

    for ref, group in zip(arrived, groups):
        base, per = tile_of(group, own_half(n_chan), samples // LANES)
        for at in range(ref.shape[0]):
            value = ref[at].astype(jnp.float32)
            for part in range(2):
                block, j = (2 * at + part) // per, (2 * at + part) % per
                if block < BLOCKS:
                    lanes = pl.ds(pl.multiple_of((base + j) * LANES, LANES), LANES)
                    whole[block, :, lanes] = value[part * CB : (part + 1) * CB]

    def series(block):
        return jnp.concatenate([whole[block], jnp.zeros((CB, LANES), jnp.float32)], 1)

    for p in range(STRIPES):
        value = series(p)
        for a in range(CB):
            spread = jnp.broadcast_to(value[a : a + 1], (SHIFTS, span))
            turned = pltpu.roll(spread, 0, 1, stride=1, stride_axis=0)
            turned = turned.astype(jnp.bfloat16)
            near[p, a * SHIFTS : (a + 1) * SHIFTS, :] = turned[:, :cut]
            far[p, a * SHIFTS : (a + 1) * SHIFTS, :] = turned[:, cut:]

    def bounds(i):
        return max(0, ahead - i), min(cols, ahead + cols - i)

    def make_window(s):
        for i in range(LAG_BLOCKS):
            first, end = bounds(i)
            rows = slice(i * high, (i + 1) * high)
            if first > 0:
                windows[s, rows, : first * LANES] = jnp.zeros((high, first * LANES), jnp.bfloat16)
            if end < cols:
                windows[s, rows, end * LANES :] = jnp.zeros(
                    (high, (cols - end) * LANES), jnp.bfloat16
                )
        value = series(STRIPES + s)
        turned = [pltpu.roll(value, span - (FRONT - MAXLAG + SHIFTS * n), 1) for n in range(STEP)]
        stacked = jnp.concatenate(turned, 0).astype(jnp.bfloat16)
        stacked = jnp.concatenate([stacked[:, samples:], stacked[:, :samples]], 1)
        for i in range(LAG_BLOCKS):
            first, end = bounds(i)
            windows[s, i * high : (i + 1) * high, first * LANES : end * LANES] = stacked[
                :, (first + i - ahead) * LANES : (end + i - ahead) * LANES
            ]

    which = [jnp.where(s < first_count, 0, 1) for s in range(SLOTS)]
    for s in range(SLOTS):
        make_window(s)
        value = lax.dot_general(
            windows[s, :, :cut], near[which[s]], NT, preferred_element_type=jnp.float32
        )
        parts_sum[s] = value if before is None else value + before[s]

    group = lax.broadcasted_iota(jnp.int32, (CB, LANES), 1) // SHIFTS
    for s in range(SLOTS):
        summed = parts_sum[s] + lax.dot_general(
            windows[s, :, cut:], far[which[s]], NT, preferred_element_type=jnp.float32
        )
        if not last:
            out[s] = summed
            continue
        summed = summed * factor
        for i in range(LAG_BLOCKS):
            width = min(LANES, LAGS - i * LANES)
            for h in range(CB // STEP):
                parts = [
                    summed[(i * STEP + n) * CB : (i * STEP + n + 1) * CB, h * LANES : (h + 1) * LANES]
                    for n in range(STEP)
                ]
                for a in range(STEP):
                    value = parts[a]
                    for n in range(STEP):
                        if n != a:
                            moved = pltpu.roll(parts[n], (SHIFTS * (n - a)) % LANES, 1)
                            value = jnp.where(group == n, moved, value)
                    out[s, h * STEP + a, :, i * LANES : i * LANES + width] = value[:, :width]


def correlate(n_chan, owners, arrived, groups, before, factor, last, samples):
    high, wide = STEP * LAG_BLOCKS * CB, CB * SHIFTS
    if last:
        shape = jax.ShapeDtypeStruct((SLOTS, CB, CB, LAGS), jnp.float32)
    else:
        shape = jax.ShapeDtypeStruct((SLOTS, high, wide), jnp.float32)
    operands = (owners,) + arrived + (() if before is None else (before,))
    depth, cut = samples + LANES, samples // 2
    return pl.pallas_call(
        functools.partial(correlate_kernel, n_chan, groups, factor, last),
        out_shape=shape,
        in_specs=[smem()] + [vmem()] * (len(operands) - 1),
        out_specs=vmem(),
        scratch_shapes=[
            pltpu.VMEM((STRIPES, wide, cut), jnp.bfloat16),
            pltpu.VMEM((STRIPES, wide, depth - cut), jnp.bfloat16),
            pltpu.VMEM((SLOTS, high, depth), jnp.bfloat16),
            pltpu.VMEM((BLOCKS, CB, samples), jnp.float32),
            pltpu.VMEM((SLOTS, high, wide), jnp.float32),
        ],
        compiler_params=params(40),
        name="correlate_last" if last else "correlate",
    )(*operands)


def local(raw_strain, whitening_taps, first_block, pair_owner):
    n_chan, n_tgroup = lax.axis_size("chan"), lax.axis_size("tgroup")
    rows, channels = raw_strain.shape
    outs = rows // 2
    samples = outs * n_chan
    count = PAIRS * CB
    owners = pair_owner[:, 0]

    firsts = lax.all_to_all(
        jnp.broadcast_to(first_block[None, :], (n_chan, STRIPES)),
        "chan",
        split_axis=0,
        concat_axis=0,
        tiled=True,
    )
    line = -(-(rows + 2 * outs + 4 * SPILL) // (2 * LANES)) * 2 * LANES
    weights = pl.pallas_call(
        weights_kernel,
        out_shape=jax.ShapeDtypeStruct((rows, outs + 2 * SPILL), jnp.bfloat16),
        in_specs=[pl.BlockSpec(memory_space=pl.ANY)],
        out_specs=vmem(),
        scratch_shapes=[
            pltpu.VMEM((1, TAPS), jnp.float32),
            pltpu.VMEM((8, line), jnp.float32),
            pltpu.SemaphoreType.DMA,
        ],
        compiler_params=params(40),
        name="fir_weights",
    )(whitening_taps.reshape(1, TAPS))

    groups = [[k] for k in range(n_chan)]
    sends = pl.pallas_call(
        functools.partial(select_kernel, n_chan, groups),
        out_shape=[
            jax.ShapeDtypeStruct((len(group) * count, outs + 2 * SPILL), jnp.bfloat16)
            for group in groups
        ],
        in_specs=[smem(), pl.BlockSpec(memory_space=pl.ANY), vmem()],
        out_specs=[vmem()] * len(groups),
        scratch_shapes=[
            pltpu.VMEM((n_chan * STRIPES, rows, 2 * LANES), jnp.float32),
            pltpu.VMEM((n_chan * count, rows), jnp.bfloat16),
            pltpu.SemaphoreType.DMA((n_chan * STRIPES, 2)),
        ],
        compiler_params=params(40),
        name="select_filter",
    )(firsts, raw_strain, weights)

    def exchange(value, k):
        return lax.ppermute(value, "chan", [(c, c ^ k) for c in range(n_chan)])

    half = n_chan // 2
    got = [sends[0]] + [exchange(sends[k], k) for k in range(1, n_chan)]
    steps = [[k] for k in range(n_chan)]
    early, late = got[:half], got

    if outs % LANES:
        wide = jnp.stack(got).astype(jnp.float32)
        wide = jnp.take(wide, lax.axis_index("chan") ^ jnp.arange(n_chan), axis=0)
        none = jnp.zeros((n_chan, count, outs - SPILL), jnp.float32)
        zero = jnp.zeros((1, count, SPILL), jnp.float32)
        right = jnp.concatenate([zero, wide[:-1, :, outs : outs + SPILL]], 0)
        left = jnp.concatenate([wide[1:, :, outs + SPILL :], zero], 0)
        added = wide[:, :, :outs] + jnp.concatenate([right, none], 2) + jnp.concatenate([none, left], 2)
        early = late = [added.transpose(1, 0, 2).reshape(count, samples)]

    order = sorted(range(1, n_tgroup), key=lambda s: (s.bit_length(), -s))
    vectors = samples // LANES
    factor = 1.0 / math.sqrt(samples)

    def place(plan, use, name):
        return pl.pallas_call(
            functools.partial(place_kernel, n_chan, n_tgroup, outs, plan, steps),
            out_shape=[
                jax.ShapeDtypeStruct((tiles_in(group, vectors), 2 * CB, LANES), jnp.bfloat16)
                for _, group in plan
            ],
            in_specs=[smem()] + [vmem()] * len(use),
            out_specs=[vmem()] * len(plan),
            scratch_shapes=[
                pltpu.VMEM((count, samples), jnp.float32),
                pltpu.SMEM((n_tgroup * SLOTS,), jnp.int32),
            ],
            compiler_params=params(40),
            name=name,
        )(owners, *use)

    def hand_over(value, shift):
        return lax.ppermute(value, "tgroup", [(g, g ^ shift) for g in range(n_tgroup)])

    if outs % LANES == 0:
        early, got[half] = lax.optimization_barrier((early, got[half]))
        late = list(early) + got[half:]
    far = order[1:]
    first = place([(shift, 0) for shift in far], early, "place_first")
    arrived = {shift: [hand_over(value, shift)] for shift, value in zip(far, first)}
    plan = [(0, 2), (1, 2)] + [(shift, 1) for shift in far]
    own, near, *second = place(plan, late, "place_second")
    arrived[0], arrived[1] = [own], [hand_over(near, 1)]
    for shift, value in zip(far, second):
        value, held = lax.optimization_barrier((value, arrived[shift][0]))
        arrived[shift] = [held, hand_over(value, shift)]

    value = None
    for at, shift in enumerate([0] + order):
        parts = (0, 1) if shift in far else (2,)
        last = at == n_tgroup - 1
        value = correlate(
            n_chan, owners, tuple(arrived[shift]), parts, value, factor, last, samples
        )
    return value


def solution(mesh):
    in_specs = (P(("tgroup", "chan"), None), P(), P("chan"), P("chan", None))
    out_specs = P(("tgroup", "chan"), None, None, None)
    return jax.shard_map(local, mesh=mesh, in_specs=in_specs, out_specs=out_specs, check_vma=False)
```

```python
import functools
import math

import jax
import jax.numpy as jnp
from jax import lax
from jax.experimental import pallas as pl
from jax.experimental.pallas import tpu as pltpu
from jax.sharding import PartitionSpec as P

MAXLAG = 500
LAGS = 2 * MAXLAG + 1
TAPS = 255
CB = 8
K = 8
STRIPES = 2
SLOTS = 5
PAIRS = STRIPES * K
BLOCKS = STRIPES + SLOTS
WIDE = K * CB
SPILL = 64
LANES = 128
SHIFTS = 32
STEP = LANES // SHIFTS
LAG_BLOCKS = -(-LAGS // LANES)
FRONT = -(-MAXLAG // LANES) * LANES
NT = (((1,), (1,)), ((), ()))


def params(megabytes):
    return pltpu.CompilerParams(vmem_limit_bytes=megabytes << 20)


def vmem():
    return pl.BlockSpec(memory_space=pltpu.VMEM)


def smem():
    return pl.BlockSpec(memory_space=pltpu.SMEM)


def weights_kernel(taps, weights, held, line, sem):
    copy = pltpu.make_async_copy(taps, held, sem)
    copy.start()
    rows, outs, width = weights.shape[0], weights.shape[1] - 2 * SPILL, line.shape[1]
    line[...] = jnp.zeros_like(line)
    copy.wait()
    line[0:1, :TAPS] = held[...]
    spread = jnp.broadcast_to(line[0:1, :], (outs + 2 * SPILL, width))
    value = pltpu.roll(spread, width - 4 * SPILL + 1, 1, stride=2, stride_axis=0)[:, :rows]
    value = jnp.concatenate([value[SPILL : SPILL + outs], value[SPILL + outs :], value[:SPILL]], 0)
    weights[...] = value.T.astype(jnp.bfloat16)


def select_kernel(n_chan, groups, firsts, raw, weights, *refs):
    sends, (window, picked, sems) = refs[: len(groups)], refs[len(groups) :]
    rows, channels = raw.shape
    steps = [k for group in groups for k in group]
    stripes = n_chan * STRIPES
    blocks_per = channels // n_chan // CB
    span = window.shape[2]
    me = lax.axis_index("chan")

    def place(p):
        c, k = me ^ steps[p // STRIPES], p % STRIPES
        start = (firsts[c, k] + c * blocks_per) * CB
        offset = lax.rem(start, LANES)
        base = start - offset
        return start, offset, base, (offset > LANES - WIDE) & (base < channels - LANES)

    def copy(p, tile):
        base = place(p)[2]
        if tile:
            base = jnp.minimum(base + LANES, channels - LANES)
        return pltpu.make_async_copy(
            raw.at[:, pl.ds(pl.multiple_of(base, LANES), LANES)],
            window.at[p, :, pl.ds(tile * LANES, LANES)],
            sems.at[p, tile],
        )

    for p in range(stripes):
        copy(p, 0).start()

        @pl.when(place(p)[3])
        def _(p=p):
            copy(p, 1).start()

    for p in range(stripes):

        @pl.when(jnp.logical_not(place(p)[3]))
        def _(p=p):
            window[p, :, LANES:] = jnp.zeros((rows, LANES), jnp.float32)

    row = lax.broadcasted_iota(jnp.int32, (WIDE, span), 0)
    lane = lax.broadcasted_iota(jnp.int32, (WIDE, span), 1)
    batch = 2 * STRIPES
    for first in range(0, stripes, batch):
        for p in range(first, first + batch):
            copy(p, 0).wait()

            @pl.when(place(p)[3])
            def _(p=p):
                copy(p, 1).wait()

        for p in range(first, first + batch):
            start, offset, _, _ = place(p)
            hot = (lane == row + offset) & (row < channels - start)
            hot = jnp.where(hot, 1.0, 0.0).astype(jnp.bfloat16)
            block = window[p].astype(jnp.bfloat16)
            chosen = lax.dot_general(hot, block, NT, preferred_element_type=jnp.float32)
            picked[p * WIDE : (p + 1) * WIDE, :] = chosen.astype(jnp.bfloat16)
        part = slice(first * WIDE, (first + batch) * WIDE)
        result = jnp.dot(
            picked[part, :], weights[...], preferred_element_type=jnp.float32
        ).astype(jnp.bfloat16)
        height = STRIPES * WIDE
        for at in range(batch // STRIPES):
            k = steps[first // STRIPES + at]
            out, where = [(o, g.index(k)) for o, g in enumerate(groups) if k in g][0]
            sends[out][where * height : (where + 1) * height, :] = result[at * height : (at + 1) * height]


def add_spills(n_chan, outs, steps, got, total):
    count = total.shape[0]
    early = lax.broadcasted_iota(jnp.int32, (count, LANES), 1) < SPILL
    me = lax.axis_index("chan")
    pieces = [
        (me ^ k, ref.at[at * count : (at + 1) * count])
        for ks, ref in zip(steps, got)
        for at, k in enumerate(ks)
    ]
    for chunk, value in pieces:
        at = pl.ds(pl.multiple_of(chunk * outs, LANES), outs)
        total[:, at] = value[:, :outs].astype(jnp.float32)
    for chunk, value in pieces:
        spill = value[:, outs:].astype(jnp.float32)
        after = jnp.minimum(chunk + 1, n_chan - 1) * outs
        after = pl.ds(pl.multiple_of(after, LANES), LANES)
        total[:, after] += jnp.where(early & (chunk < n_chan - 1), spill, 0.0)
        before = jnp.maximum(chunk * outs, LANES) - LANES
        before = pl.ds(pl.multiple_of(before, LANES), LANES)
        total[:, before] += jnp.where(early | (chunk == 0), 0.0, spill)


def tile_of(group, width, vectors):
    half = vectors // 2
    if group == 0:
        return jnp.where(width == 0, 0, half + 1), half - 1
    if group == 1:
        return jnp.where(width == 0, half - 1, 0), half + 1
    return 0, vectors


def tiles_in(group, vectors):
    return -(-BLOCKS * tile_of(group, 0, vectors)[1] // 2)


def own_half(n_chan):
    return jnp.where(lax.axis_index("chan") < n_chan // 2, 0, 1)


def place_kernel(n_chan, n_tgroup, outs, plan, steps, owners, *refs):
    got, (total, pairs) = refs[: -len(plan) - 2], refs[-2:]
    sends = refs[-len(plan) - 2 : -2]
    me = lax.axis_index("tgroup")
    if len(got) == 1:
        total[...] = got[0][...]
    else:
        add_spills(n_chan, outs, steps, got, total)

    for at in range(n_tgroup * SLOTS):
        pairs[at] = -1
    counts = jnp.int32(0)
    for q in range(PAIRS):
        owner = owners[q]
        slot = (counts >> (3 * owner)) & 7
        counts = counts + (jnp.int32(1) << (3 * owner))
        pairs[(owner ^ me) * SLOTS + slot] = q

    zero = jnp.zeros((CB, LANES), jnp.float32)
    for send, (shift, group) in zip(sends, plan):
        base, per = tile_of(group, own_half(n_chan), total.shape[1] // LANES)

        def tiles(q):
            rows = pl.ds(pl.multiple_of(q * CB, CB), CB)
            return [
                total[rows, pl.ds(pl.multiple_of((base + j) * LANES, LANES), LANES)]
                for j in range(per)
            ]

        parts = sum([tiles(p * K) for p in range(STRIPES)], [])
        for s in range(SLOTS):
            q = pairs[shift * SLOTS + s]
            parts += [jnp.where(q >= 0, tile, 0.0) for tile in tiles(jnp.maximum(q, 0))]
        parts += [zero] * (len(parts) % 2)
        for at in range(0, len(parts), 2):
            value = jnp.concatenate(parts[at : at + 2], 0)
            send[at // 2] = value.astype(jnp.bfloat16)


def correlate_kernel(n_chan, groups, factor, last, owners, *refs):
    if last:
        *refs, final, sems = refs
    near, far, windows, whole, parts_sum = refs[-5:]
    out = refs[-6]
    arrived = refs[: len(groups)]
    before = refs[len(groups)] if len(refs) > len(groups) + 6 else None
    cut = near.shape[2]
    span = cut + far.shape[2]
    samples = span - LANES
    cols = span // LANES
    high = STEP * CB
    ahead = FRONT // LANES - 1
    me = lax.axis_index("tgroup")
    first_count = jnp.int32(0)
    for q in range(K):
        first_count += jnp.where(owners[q] == me, 1, 0)

    for ref, group in zip(arrived, groups):
        base, per = tile_of(group, own_half(n_chan), samples // LANES)
        for at in range(ref.shape[0]):
            value = ref[at].astype(jnp.float32)
            for part in range(2):
                block, j = (2 * at + part) // per, (2 * at + part) % per
                if block < BLOCKS:
                    lanes = pl.ds(pl.multiple_of((base + j) * LANES, LANES), LANES)
                    whole[block, :, lanes] = value[part * CB : (part + 1) * CB]

    def series(block):
        return jnp.concatenate([whole[block], jnp.zeros((CB, LANES), jnp.float32)], 1)

    for p in range(STRIPES):
        value = series(p)
        for a in range(CB):
            spread = jnp.broadcast_to(value[a : a + 1], (SHIFTS, span))
            turned = pltpu.roll(spread, 0, 1, stride=1, stride_axis=0)
            turned = turned.astype(jnp.bfloat16)
            near[p, a * SHIFTS : (a + 1) * SHIFTS, :] = turned[:, :cut]
            far[p, a * SHIFTS : (a + 1) * SHIFTS, :] = turned[:, cut:]

    def bounds(i):
        return max(0, ahead - i), min(cols, ahead + cols - i)

    def make_window(s):
        for i in range(LAG_BLOCKS):
            first, end = bounds(i)
            rows = slice(i * high, (i + 1) * high)
            if first > 0:
                windows[s, rows, : first * LANES] = jnp.zeros((high, first * LANES), jnp.bfloat16)
            if end < cols:
                windows[s, rows, end * LANES :] = jnp.zeros(
                    (high, (cols - end) * LANES), jnp.bfloat16
                )
        value = series(STRIPES + s)
        turned = [pltpu.roll(value, span - (FRONT - MAXLAG + SHIFTS * n), 1) for n in range(STEP)]
        stacked = jnp.concatenate(turned, 0).astype(jnp.bfloat16)
        stacked = jnp.concatenate([stacked[:, samples:], stacked[:, :samples]], 1)
        for i in range(LAG_BLOCKS):
            first, end = bounds(i)
            windows[s, i * high : (i + 1) * high, first * LANES : end * LANES] = stacked[
                :, (first + i - ahead) * LANES : (end + i - ahead) * LANES
            ]

    which = [jnp.where(s < first_count, 0, 1) for s in range(SLOTS)]
    for s in range(SLOTS):
        make_window(s)
        value = lax.dot_general(
            windows[s, :, :cut], near[which[s]], NT, preferred_element_type=jnp.float32
        )
        parts_sum[s] = value if before is None else value + before[s]

    def leave(part):
        slots = pl.ds(0, SLOTS // 2 + 1) if part == 0 else pl.ds(SLOTS // 2 + 1, SLOTS // 2)
        return pltpu.make_async_copy(final.at[slots], out.at[slots], sems.at[part])

    group = lax.broadcasted_iota(jnp.int32, (CB, LANES), 1) // SHIFTS
    for s in range(SLOTS):
        summed = parts_sum[s] + lax.dot_general(
            windows[s, :, cut:], far[which[s]], NT, preferred_element_type=jnp.float32
        )
        if not last:
            out[s] = summed
            continue
        summed = summed * factor
        for i in range(LAG_BLOCKS):
            width = min(LANES, LAGS - i * LANES)
            for h in range(CB // STEP):
                parts = [
                    summed[(i * STEP + n) * CB : (i * STEP + n + 1) * CB, h * LANES : (h + 1) * LANES]
                    for n in range(STEP)
                ]
                for a in range(STEP):
                    value = parts[a]
                    for n in range(STEP):
                        if n != a:
                            moved = pltpu.roll(parts[n], (SHIFTS * (n - a)) % LANES, 1)
                            value = jnp.where(group == n, moved, value)
                    final[s, h * STEP + a, :, i * LANES : i * LANES + width] = value[:, :width]
        if s == SLOTS // 2:
            leave(0).start()
    if last:
        leave(1).start()
        leave(0).wait()
        leave(1).wait()


def correlate(n_chan, owners, arrived, groups, before, factor, last, samples):
    high, wide = STEP * LAG_BLOCKS * CB, CB * SHIFTS
    if last:
        shape = jax.ShapeDtypeStruct((SLOTS, CB, CB, LAGS), jnp.float32)
    else:
        shape = jax.ShapeDtypeStruct((SLOTS, high, wide), jnp.float32)
    operands = (owners,) + arrived + (() if before is None else (before,))
    depth, cut = samples + LANES, samples // 2
    return pl.pallas_call(
        functools.partial(correlate_kernel, n_chan, groups, factor, last),
        out_shape=shape,
        in_specs=[smem()] + [vmem()] * (len(operands) - 1),
        out_specs=pl.BlockSpec(memory_space=pl.ANY) if last else vmem(),
        scratch_shapes=[
            pltpu.VMEM((STRIPES, wide, cut), jnp.bfloat16),
            pltpu.VMEM((STRIPES, wide, depth - cut), jnp.bfloat16),
            pltpu.VMEM((SLOTS, high, depth), jnp.bfloat16),
            pltpu.VMEM((BLOCKS, CB, samples), jnp.float32),
            pltpu.VMEM((SLOTS, high, wide), jnp.float32),
        ]
        + [pltpu.VMEM(shape.shape, jnp.float32), pltpu.SemaphoreType.DMA((2,))] * last,
        compiler_params=params(40),
        name="correlate_last" if last else "correlate",
    )(*operands)


def local(raw_strain, whitening_taps, first_block, pair_owner):
    n_chan, n_tgroup = lax.axis_size("chan"), lax.axis_size("tgroup")
    rows, channels = raw_strain.shape
    outs = rows // 2
    samples = outs * n_chan
    count = PAIRS * CB
    owners = pair_owner[:, 0]

    firsts = lax.all_to_all(
        jnp.broadcast_to(first_block[None, :], (n_chan, STRIPES)),
        "chan",
        split_axis=0,
        concat_axis=0,
        tiled=True,
    )
    line = -(-(rows + 2 * outs + 4 * SPILL) // (2 * LANES)) * 2 * LANES
    weights = pl.pallas_call(
        weights_kernel,
        out_shape=jax.ShapeDtypeStruct((rows, outs + 2 * SPILL), jnp.bfloat16),
        in_specs=[pl.BlockSpec(memory_space=pl.ANY)],
        out_specs=vmem(),
        scratch_shapes=[
            pltpu.VMEM((1, TAPS), jnp.float32),
            pltpu.VMEM((8, line), jnp.float32),
            pltpu.SemaphoreType.DMA,
        ],
        compiler_params=params(40),
        name="fir_weights",
    )(whitening_taps.reshape(1, TAPS))

    groups = [[k] for k in range(n_chan)]
    sends = pl.pallas_call(
        functools.partial(select_kernel, n_chan, groups),
        out_shape=[
            jax.ShapeDtypeStruct((len(group) * count, outs + 2 * SPILL), jnp.bfloat16)
            for group in groups
        ],
        in_specs=[smem(), pl.BlockSpec(memory_space=pl.ANY), vmem()],
        out_specs=[vmem()] * len(groups),
        scratch_shapes=[
            pltpu.VMEM((n_chan * STRIPES, rows, 2 * LANES), jnp.float32),
            pltpu.VMEM((n_chan * count, rows), jnp.bfloat16),
            pltpu.SemaphoreType.DMA((n_chan * STRIPES, 2)),
        ],
        compiler_params=params(40),
        name="select_filter",
    )(firsts, raw_strain, weights)

    def exchange(value, k):
        return lax.ppermute(value, "chan", [(c, c ^ k) for c in range(n_chan)])

    half = n_chan // 2
    got = [sends[0]] + [exchange(sends[k], k) for k in range(1, n_chan)]
    steps = [[k] for k in range(n_chan)]
    early, late = got[:half], got

    if outs % LANES:
        wide = jnp.stack(got).astype(jnp.float32)
        wide = jnp.take(wide, lax.axis_index("chan") ^ jnp.arange(n_chan), axis=0)
        none = jnp.zeros((n_chan, count, outs - SPILL), jnp.float32)
        zero = jnp.zeros((1, count, SPILL), jnp.float32)
        right = jnp.concatenate([zero, wide[:-1, :, outs : outs + SPILL]], 0)
        left = jnp.concatenate([wide[1:, :, outs + SPILL :], zero], 0)
        added = wide[:, :, :outs] + jnp.concatenate([right, none], 2) + jnp.concatenate([none, left], 2)
        early = late = [added.transpose(1, 0, 2).reshape(count, samples)]

    order = sorted(range(1, n_tgroup), key=lambda s: (s.bit_length(), -s))
    vectors = samples // LANES
    factor = 1.0 / math.sqrt(samples)

    def place(plan, use, name):
        return pl.pallas_call(
            functools.partial(place_kernel, n_chan, n_tgroup, outs, plan, steps),
            out_shape=[
                jax.ShapeDtypeStruct((tiles_in(group, vectors), 2 * CB, LANES), jnp.bfloat16)
                for _, group in plan
            ],
            in_specs=[smem()] + [vmem()] * len(use),
            out_specs=[vmem()] * len(plan),
            scratch_shapes=[
                pltpu.VMEM((count, samples), jnp.float32),
                pltpu.SMEM((n_tgroup * SLOTS,), jnp.int32),
            ],
            compiler_params=params(40),
            name=name,
        )(owners, *use)

    def hand_over(value, shift):
        return lax.ppermute(value, "tgroup", [(g, g ^ shift) for g in range(n_tgroup)])

    if outs % LANES == 0:
        early, got[half] = lax.optimization_barrier((early, got[half]))
        late = list(early) + got[half:]
    far = order[1:]
    first = place([(shift, 0) for shift in far], early, "place_first")
    arrived = {shift: [hand_over(value, shift)] for shift, value in zip(far, first)}
    plan = [(0, 2), (1, 2)] + [(shift, 1) for shift in far]
    own, near, *second = place(plan, late, "place_second")
    arrived[0], arrived[1] = [own], [hand_over(near, 1)]
    for shift, value in zip(far, second):
        value, held = lax.optimization_barrier((value, arrived[shift][0]))
        arrived[shift] = [held, hand_over(value, shift)]

    value = None
    for at, shift in enumerate([0] + order):
        parts = (0, 1) if shift in far else (2,)
        last = at == n_tgroup - 1
        value = correlate(
            n_chan, owners, tuple(arrived[shift]), parts, value, factor, last, samples
        )
    return value


def solution(mesh):
    in_specs = (P(("tgroup", "chan"), None), P(), P("chan"), P("chan", None))
    out_specs = P(("tgroup", "chan"), None, None, None)
    return jax.shard_map(local, mesh=mesh, in_specs=in_specs, out_specs=out_specs, check_vma=False)
```

```python
import functools
import math

import jax
import jax.numpy as jnp
from jax import lax
from jax.experimental import pallas as pl
from jax.experimental.pallas import tpu as pltpu
from jax.sharding import PartitionSpec as P

MAXLAG = 500
LAGS = 2 * MAXLAG + 1
TAPS = 255
CB = 8
K = 8
STRIPES = 2
SLOTS = 5
PAIRS = STRIPES * K
BLOCKS = STRIPES + SLOTS
WIDE = K * CB
SPILL = 64
LANES = 128
SHIFTS = 32
STEP = LANES // SHIFTS
LAG_BLOCKS = -(-LAGS // LANES)
FRONT = -(-MAXLAG // LANES) * LANES
NT = (((1,), (1,)), ((), ()))


def params(megabytes):
    return pltpu.CompilerParams(vmem_limit_bytes=megabytes << 20)


def vmem():
    return pl.BlockSpec(memory_space=pltpu.VMEM)


def smem():
    return pl.BlockSpec(memory_space=pltpu.SMEM)


def weights_kernel(taps, weights, held, line, sem):
    copy = pltpu.make_async_copy(taps, held, sem)
    copy.start()
    rows, outs, width = weights.shape[0], weights.shape[1] - 2 * SPILL, line.shape[1]
    line[...] = jnp.zeros_like(line)
    copy.wait()
    line[0:1, :TAPS] = held[...]
    spread = jnp.broadcast_to(line[0:1, :], (outs + 2 * SPILL, width))
    value = pltpu.roll(spread, width - 4 * SPILL + 1, 1, stride=2, stride_axis=0)[:, :rows]
    value = jnp.concatenate([value[SPILL : SPILL + outs], value[SPILL + outs :], value[:SPILL]], 0)
    weights[...] = value.T.astype(jnp.bfloat16)


def select_kernel(n_chan, groups, firsts, raw, weights, *refs):
    sends, (window, picked, sems) = refs[: len(groups)], refs[len(groups) :]
    rows, channels = raw.shape
    outs = rows // 2
    steps = [k for group in groups for k in group]
    stripes = n_chan * STRIPES
    blocks_per = channels // n_chan // CB
    span = window.shape[2]
    me = lax.axis_index("chan")

    def place(p):
        c, k = me ^ steps[p // STRIPES], p % STRIPES
        start = (firsts[c, k] + c * blocks_per) * CB
        offset = lax.rem(start, LANES)
        base = start - offset
        return start, offset, base, (offset > LANES - WIDE) & (base < channels - LANES)

    def copy(p, tile):
        base = place(p)[2]
        if tile:
            base = jnp.minimum(base + LANES, channels - LANES)
        return pltpu.make_async_copy(
            raw.at[:, pl.ds(pl.multiple_of(base, LANES), LANES)],
            window.at[p, :, pl.ds(tile * LANES, LANES)],
            sems.at[p, tile],
        )

    for p in range(stripes):
        copy(p, 0).start()

        @pl.when(place(p)[3])
        def _(p=p):
            copy(p, 1).start()

    for p in range(stripes):

        @pl.when(jnp.logical_not(place(p)[3]))
        def _(p=p):
            window[p, :, LANES:] = jnp.zeros((rows, LANES), jnp.float32)

    row = lax.broadcasted_iota(jnp.int32, (WIDE, span), 0)
    lane = lax.broadcasted_iota(jnp.int32, (WIDE, span), 1)
    batch = 2 * STRIPES
    for first in range(0, stripes, batch):
        for p in range(first, first + batch):
            copy(p, 0).wait()

            @pl.when(place(p)[3])
            def _(p=p):
                copy(p, 1).wait()

        for p in range(first, first + batch):
            start, offset, _, _ = place(p)
            hot = (lane == row + offset) & (row < channels - start)
            hot = jnp.where(hot, 1.0, 0.0).astype(jnp.bfloat16)
            block = window[p].astype(jnp.bfloat16)
            chosen = lax.dot_general(hot, block, NT, preferred_element_type=jnp.float32)
            picked[p * WIDE : (p + 1) * WIDE, :] = chosen.astype(jnp.bfloat16)
        part = slice(first * WIDE, (first + batch) * WIDE)
        taken = picked[part, :]
        inner = jnp.dot(taken, weights[:, :outs], preferred_element_type=jnp.float32)
        if rows > 4 * SPILL:
            taken = jnp.concatenate([taken[:, : 2 * SPILL], taken[:, rows - 2 * SPILL :]], 1)
            edge = jnp.concatenate(
                [weights[: 2 * SPILL, outs:], weights[rows - 2 * SPILL :, outs:]], 0
            )
        else:
            edge = weights[:, outs:]
        outer = jnp.dot(taken, edge, preferred_element_type=jnp.float32)
        result = jnp.concatenate([inner, outer], 1).astype(jnp.bfloat16)
        height = STRIPES * WIDE
        for at in range(batch // STRIPES):
            k = steps[first // STRIPES + at]
            out, where = [(o, g.index(k)) for o, g in enumerate(groups) if k in g][0]
            sends[out][where * height : (where + 1) * height, :] = result[at * height : (at + 1) * height]


def add_spills(n_chan, outs, steps, got, total):
    count = total.shape[0]
    early = lax.broadcasted_iota(jnp.int32, (count, LANES), 1) < SPILL
    me = lax.axis_index("chan")
    pieces = [
        (me ^ k, ref.at[at * count : (at + 1) * count])
        for ks, ref in zip(steps, got)
        for at, k in enumerate(ks)
    ]
    for chunk, value in pieces:
        at = pl.ds(pl.multiple_of(chunk * outs, LANES), outs)
        total[:, at] = value[:, :outs].astype(jnp.float32)
    for chunk, value in pieces:
        spill = value[:, outs:].astype(jnp.float32)
        after = jnp.minimum(chunk + 1, n_chan - 1) * outs
        after = pl.ds(pl.multiple_of(after, LANES), LANES)
        total[:, after] += jnp.where(early & (chunk < n_chan - 1), spill, 0.0)
        before = jnp.maximum(chunk * outs, LANES) - LANES
        before = pl.ds(pl.multiple_of(before, LANES), LANES)
        total[:, before] += jnp.where(early | (chunk == 0), 0.0, spill)


def tile_of(group, width, vectors):
    half = vectors // 2
    if group == 0:
        return jnp.where(width == 0, 0, half + 1), half - 1
    if group == 1:
        return jnp.where(width == 0, half - 1, 0), half + 1
    return 0, vectors


def tiles_in(group, vectors):
    return -(-BLOCKS * tile_of(group, 0, vectors)[1] // 2)


def own_half(n_chan):
    return jnp.where(lax.axis_index("chan") < n_chan // 2, 0, 1)


def place_kernel(n_chan, n_tgroup, outs, plan, steps, owners, *refs):
    got, (total, pairs) = refs[: -len(plan) - 2], refs[-2:]
    sends = refs[-len(plan) - 2 : -2]
    me = lax.axis_index("tgroup")
    if len(got) == 1:
        total[...] = got[0][...]
    else:
        add_spills(n_chan, outs, steps, got, total)

    for at in range(n_tgroup * SLOTS):
        pairs[at] = -1
    counts = jnp.int32(0)
    for q in range(PAIRS):
        owner = owners[q]
        slot = (counts >> (3 * owner)) & 7
        counts = counts + (jnp.int32(1) << (3 * owner))
        pairs[(owner ^ me) * SLOTS + slot] = q

    zero = jnp.zeros((CB, LANES), jnp.float32)
    for send, (shift, group) in zip(sends, plan):
        base, per = tile_of(group, own_half(n_chan), total.shape[1] // LANES)

        def tiles(q):
            rows = pl.ds(pl.multiple_of(q * CB, CB), CB)
            return [
                total[rows, pl.ds(pl.multiple_of((base + j) * LANES, LANES), LANES)]
                for j in range(per)
            ]

        parts = sum([tiles(p * K) for p in range(STRIPES)], [])
        for s in range(SLOTS):
            q = pairs[shift * SLOTS + s]
            parts += [jnp.where(q >= 0, tile, 0.0) for tile in tiles(jnp.maximum(q, 0))]
        parts += [zero] * (len(parts) % 2)
        for at in range(0, len(parts), 2):
            value = jnp.concatenate(parts[at : at + 2], 0)
            send[at // 2] = value.astype(jnp.bfloat16)


def correlate_kernel(n_chan, groups, factor, last, owners, *refs):
    if last:
        *refs, final, sems = refs
    near, far, windows, whole, parts_sum = refs[-5:]
    out = refs[-6]
    arrived = refs[: len(groups)]
    before = refs[len(groups)] if len(refs) > len(groups) + 6 else None
    cut = near.shape[2]
    span = cut + far.shape[2]
    samples = span - LANES
    cols = span // LANES
    high = STEP * CB
    ahead = FRONT // LANES - 1
    me = lax.axis_index("tgroup")
    first_count = jnp.int32(0)
    for q in range(K):
        first_count += jnp.where(owners[q] == me, 1, 0)

    for ref, group in zip(arrived, groups):
        base, per = tile_of(group, own_half(n_chan), samples // LANES)
        for at in range(ref.shape[0]):
            value = ref[at].astype(jnp.float32)
            for part in range(2):
                block, j = (2 * at + part) // per, (2 * at + part) % per
                if block < BLOCKS:
                    lanes = pl.ds(pl.multiple_of((base + j) * LANES, LANES), LANES)
                    whole[block, :, lanes] = value[part * CB : (part + 1) * CB]

    def series(block):
        return jnp.concatenate([whole[block], jnp.zeros((CB, LANES), jnp.float32)], 1)

    for p in range(STRIPES):
        value = series(p)
        for a in range(CB):
            spread = jnp.broadcast_to(value[a : a + 1], (SHIFTS, span))
            turned = pltpu.roll(spread, 0, 1, stride=1, stride_axis=0)
            turned = turned.astype(jnp.bfloat16)
            near[p, a * SHIFTS : (a + 1) * SHIFTS, :] = turned[:, :cut]
            far[p, a * SHIFTS : (a + 1) * SHIFTS, :] = turned[:, cut:]

    def bounds(i):
        return max(0, ahead - i), min(cols, ahead + cols - i)

    def make_window(s):
        for i in range(LAG_BLOCKS):
            first, end = bounds(i)
            rows = slice(i * high, (i + 1) * high)
            if first > 0:
                windows[s, rows, : first * LANES] = jnp.zeros((high, first * LANES), jnp.bfloat16)
            if end < cols:
                windows[s, rows, end * LANES :] = jnp.zeros(
                    (high, (cols - end) * LANES), jnp.bfloat16
                )
        value = series(STRIPES + s)
        turned = [pltpu.roll(value, span - (FRONT - MAXLAG + SHIFTS * n), 1) for n in range(STEP)]
        stacked = jnp.concatenate(turned, 0).astype(jnp.bfloat16)
        stacked = jnp.concatenate([stacked[:, samples:], stacked[:, :samples]], 1)
        for i in range(LAG_BLOCKS):
            first, end = bounds(i)
            windows[s, i * high : (i + 1) * high, first * LANES : end * LANES] = stacked[
                :, (first + i - ahead) * LANES : (end + i - ahead) * LANES
            ]

    which = [jnp.where(s < first_count, 0, 1) for s in range(SLOTS)]
    for s in range(SLOTS):
        make_window(s)
        value = lax.dot_general(
            windows[s, :, :cut], near[which[s]], NT, preferred_element_type=jnp.float32
        )
        parts_sum[s] = value if before is None else value + before[s]

    def leave(part):
        slots = pl.ds(0, SLOTS // 2 + 1) if part == 0 else pl.ds(SLOTS // 2 + 1, SLOTS // 2)
        return pltpu.make_async_copy(final.at[slots], out.at[slots], sems.at[part])

    group = lax.broadcasted_iota(jnp.int32, (CB, LANES), 1) // SHIFTS
    for s in range(SLOTS):
        summed = parts_sum[s] + lax.dot_general(
            windows[s, :, cut:], far[which[s]], NT, preferred_element_type=jnp.float32
        )
        if not last:
            out[s] = summed
            continue
        summed = summed * factor
        for i in range(LAG_BLOCKS):
            width = min(LANES, LAGS - i * LANES)
            for h in range(CB // STEP):
                parts = [
                    summed[(i * STEP + n) * CB : (i * STEP + n + 1) * CB, h * LANES : (h + 1) * LANES]
                    for n in range(STEP)
                ]
                for a in range(STEP):
                    value = parts[a]
                    for n in range(STEP):
                        if n != a:
                            moved = pltpu.roll(parts[n], (SHIFTS * (n - a)) % LANES, 1)
                            value = jnp.where(group == n, moved, value)
                    final[s, h * STEP + a, :, i * LANES : i * LANES + width] = value[:, :width]
        if s == SLOTS // 2:
            leave(0).start()
    if last:
        leave(1).start()
        leave(0).wait()
        leave(1).wait()


def correlate(n_chan, owners, arrived, groups, before, factor, last, samples):
    high, wide = STEP * LAG_BLOCKS * CB, CB * SHIFTS
    if last:
        shape = jax.ShapeDtypeStruct((SLOTS, CB, CB, LAGS), jnp.float32)
    else:
        shape = jax.ShapeDtypeStruct((SLOTS, high, wide), jnp.float32)
    operands = (owners,) + arrived + (() if before is None else (before,))
    depth, cut = samples + LANES, samples // 2
    return pl.pallas_call(
        functools.partial(correlate_kernel, n_chan, groups, factor, last),
        out_shape=shape,
        in_specs=[smem()] + [vmem()] * (len(operands) - 1),
        out_specs=pl.BlockSpec(memory_space=pl.ANY) if last else vmem(),
        scratch_shapes=[
            pltpu.VMEM((STRIPES, wide, cut), jnp.bfloat16),
            pltpu.VMEM((STRIPES, wide, depth - cut), jnp.bfloat16),
            pltpu.VMEM((SLOTS, high, depth), jnp.bfloat16),
            pltpu.VMEM((BLOCKS, CB, samples), jnp.float32),
            pltpu.VMEM((SLOTS, high, wide), jnp.float32),
        ]
        + [pltpu.VMEM(shape.shape, jnp.float32), pltpu.SemaphoreType.DMA((2,))] * last,
        compiler_params=params(40),
        name="correlate_last" if last else "correlate",
    )(*operands)


def local(raw_strain, whitening_taps, first_block, pair_owner):
    n_chan, n_tgroup = lax.axis_size("chan"), lax.axis_size("tgroup")
    rows, channels = raw_strain.shape
    outs = rows // 2
    samples = outs * n_chan
    count = PAIRS * CB
    owners = pair_owner[:, 0]

    firsts = lax.all_to_all(
        jnp.broadcast_to(first_block[None, :], (n_chan, STRIPES)),
        "chan",
        split_axis=0,
        concat_axis=0,
        tiled=True,
    )
    line = -(-(rows + 2 * outs + 4 * SPILL) // (2 * LANES)) * 2 * LANES
    weights = pl.pallas_call(
        weights_kernel,
        out_shape=jax.ShapeDtypeStruct((rows, outs + 2 * SPILL), jnp.bfloat16),
        in_specs=[pl.BlockSpec(memory_space=pl.ANY)],
        out_specs=vmem(),
        scratch_shapes=[
            pltpu.VMEM((1, TAPS), jnp.float32),
            pltpu.VMEM((8, line), jnp.float32),
            pltpu.SemaphoreType.DMA,
        ],
        compiler_params=params(40),
        name="fir_weights",
    )(whitening_taps.reshape(1, TAPS))

    groups = [[k] for k in range(n_chan)]
    sends = pl.pallas_call(
        functools.partial(select_kernel, n_chan, groups),
        out_shape=[
            jax.ShapeDtypeStruct((len(group) * count, outs + 2 * SPILL), jnp.bfloat16)
            for group in groups
        ],
        in_specs=[smem(), pl.BlockSpec(memory_space=pl.ANY), vmem()],
        out_specs=[vmem()] * len(groups),
        scratch_shapes=[
            pltpu.VMEM((n_chan * STRIPES, rows, 2 * LANES), jnp.float32),
            pltpu.VMEM((n_chan * count, rows), jnp.bfloat16),
            pltpu.SemaphoreType.DMA((n_chan * STRIPES, 2)),
        ],
        compiler_params=params(40),
        name="select_filter",
    )(firsts, raw_strain, weights)

    def exchange(value, k):
        return lax.ppermute(value, "chan", [(c, c ^ k) for c in range(n_chan)])

    half = n_chan // 2
    got = [sends[0]] + [exchange(sends[k], k) for k in range(1, n_chan)]
    steps = [[k] for k in range(n_chan)]
    early, late = got[:half], got

    if outs % LANES:
        wide = jnp.stack(got).astype(jnp.float32)
        wide = jnp.take(wide, lax.axis_index("chan") ^ jnp.arange(n_chan), axis=0)
        none = jnp.zeros((n_chan, count, outs - SPILL), jnp.float32)
        zero = jnp.zeros((1, count, SPILL), jnp.float32)
        right = jnp.concatenate([zero, wide[:-1, :, outs : outs + SPILL]], 0)
        left = jnp.concatenate([wide[1:, :, outs + SPILL :], zero], 0)
        added = wide[:, :, :outs] + jnp.concatenate([right, none], 2) + jnp.concatenate([none, left], 2)
        early = late = [added.transpose(1, 0, 2).reshape(count, samples)]

    order = sorted(range(1, n_tgroup), key=lambda s: (s.bit_length(), -s))
    vectors = samples // LANES
    factor = 1.0 / math.sqrt(samples)

    def place(plan, use, name):
        return pl.pallas_call(
            functools.partial(place_kernel, n_chan, n_tgroup, outs, plan, steps),
            out_shape=[
                jax.ShapeDtypeStruct((tiles_in(group, vectors), 2 * CB, LANES), jnp.bfloat16)
                for _, group in plan
            ],
            in_specs=[smem()] + [vmem()] * len(use),
            out_specs=[vmem()] * len(plan),
            scratch_shapes=[
                pltpu.VMEM((count, samples), jnp.float32),
                pltpu.SMEM((n_tgroup * SLOTS,), jnp.int32),
            ],
            compiler_params=params(40),
            name=name,
        )(owners, *use)

    def hand_over(value, shift):
        return lax.ppermute(value, "tgroup", [(g, g ^ shift) for g in range(n_tgroup)])

    if outs % LANES == 0:
        early, got[half] = lax.optimization_barrier((early, got[half]))
        late = list(early) + got[half:]
    far = order[1:]
    first = place([(shift, 0) for shift in far], early, "place_first")
    arrived = {shift: [hand_over(value, shift)] for shift, value in zip(far, first)}
    plan = [(0, 2), (1, 2)] + [(shift, 1) for shift in far]
    own, near, *second = place(plan, late, "place_second")
    arrived[0], arrived[1] = [own], [hand_over(near, 1)]
    for shift, value in zip(far, second):
        value, held = lax.optimization_barrier((value, arrived[shift][0]))
        arrived[shift] = [held, hand_over(value, shift)]

    value = None
    for at, shift in enumerate([0] + order):
        parts = (0, 1) if shift in far else (2,)
        last = at == n_tgroup - 1
        value = correlate(
            n_chan, owners, tuple(arrived[shift]), parts, value, factor, last, samples
        )
    return value


def solution(mesh):
    in_specs = (P(("tgroup", "chan"), None), P(), P("chan"), P("chan", None))
    out_specs = P(("tgroup", "chan"), None, None, None)
    return jax.shard_map(local, mesh=mesh, in_specs=in_specs, out_specs=out_specs, check_vma=False)
```

```python
import functools
import math

import jax
import jax.numpy as jnp
from jax import lax
from jax.experimental import pallas as pl
from jax.experimental.pallas import tpu as pltpu
from jax.sharding import PartitionSpec as P

MAXLAG = 500
LAGS = 2 * MAXLAG + 1
TAPS = 255
CB = 8
K = 8
STRIPES = 2
SLOTS = 5
PAIRS = STRIPES * K
BLOCKS = STRIPES + SLOTS
WIDE = K * CB
SPILL = 64
LANES = 128
SHIFTS = 32
STEP = LANES // SHIFTS
LAG_BLOCKS = -(-LAGS // LANES)
FRONT = -(-MAXLAG // LANES) * LANES
NT = (((1,), (1,)), ((), ()))


def params(megabytes):
    return pltpu.CompilerParams(vmem_limit_bytes=megabytes << 20)


def vmem():
    return pl.BlockSpec(memory_space=pltpu.VMEM)


def smem():
    return pl.BlockSpec(memory_space=pltpu.SMEM)


def weights_kernel(taps, weights, held, line, sem):
    copy = pltpu.make_async_copy(taps, held, sem)
    copy.start()
    rows, outs, width = weights.shape[0], weights.shape[1] - 2 * SPILL, line.shape[1]
    line[...] = jnp.zeros_like(line)
    copy.wait()
    line[0:1, :TAPS] = held[...]
    spread = jnp.broadcast_to(line[0:1, :], (outs + 2 * SPILL, width))
    value = pltpu.roll(spread, width - 4 * SPILL + 1, 1, stride=2, stride_axis=0)[:, :rows]
    value = jnp.concatenate([value[SPILL : SPILL + outs], value[SPILL + outs :], value[:SPILL]], 0)
    weights[...] = value.T.astype(jnp.bfloat16)


def select_kernel(n_chan, groups, firsts, raw, weights, *refs):
    sends, (window, picked, sems) = refs[: len(groups)], refs[len(groups) :]
    rows, channels = raw.shape
    steps = [k for group in groups for k in group]
    stripes = n_chan * STRIPES
    blocks_per = channels // n_chan // CB
    span = window.shape[2]
    me = lax.axis_index("chan")

    def place(p):
        c, k = me ^ steps[p // STRIPES], p % STRIPES
        start = (firsts[c, k] + c * blocks_per) * CB
        base = jnp.minimum(start & -LANES, channels - span)
        return start, pl.multiple_of(base, LANES)

    def copy(p):
        base = place(p)[1]
        return pltpu.make_async_copy(raw.at[:, pl.ds(base, span)], window.at[p], sems.at[p])

    for p in range(stripes):
        copy(p).start()

    row = lax.broadcasted_iota(jnp.int32, (WIDE, span), 0)
    lane = lax.broadcasted_iota(jnp.int32, (WIDE, span), 1)
    batch = 2 * STRIPES
    for first in range(0, stripes, batch):
        for p in range(first, first + batch):
            copy(p).wait()
        for p in range(first, first + batch):
            start, base = place(p)
            hot = (lane == row + (start - base)) & (row < channels - start)
            hot = jnp.where(hot, 1.0, 0.0).astype(jnp.bfloat16)
            block = window[p].astype(jnp.bfloat16)
            chosen = lax.dot_general(hot, block, NT, preferred_element_type=jnp.float32)
            picked[p * WIDE : (p + 1) * WIDE, :] = chosen.astype(jnp.bfloat16)
        part = slice(first * WIDE, (first + batch) * WIDE)
        result = jnp.dot(
            picked[part, :], weights[...], preferred_element_type=jnp.float32
        ).astype(jnp.bfloat16)
        height = STRIPES * WIDE
        for at in range(batch // STRIPES):
            k = steps[first // STRIPES + at]
            out, where = [(o, g.index(k)) for o, g in enumerate(groups) if k in g][0]
            sends[out][where * height : (where + 1) * height, :] = result[at * height : (at + 1) * height]


def add_spills(n_chan, outs, steps, got, total):
    count = total.shape[0]
    early = lax.broadcasted_iota(jnp.int32, (count, LANES), 1) < SPILL
    me = lax.axis_index("chan")
    pieces = [
        (me ^ k, ref.at[at * count : (at + 1) * count])
        for ks, ref in zip(steps, got)
        for at, k in enumerate(ks)
    ]
    for chunk, value in pieces:
        at = pl.ds(pl.multiple_of(chunk * outs, LANES), outs)
        total[:, at] = value[:, :outs].astype(jnp.float32)
    for chunk, value in pieces:
        spill = value[:, outs:].astype(jnp.float32)
        after = jnp.minimum(chunk + 1, n_chan - 1) * outs
        after = pl.ds(pl.multiple_of(after, LANES), LANES)
        total[:, after] += jnp.where(early & (chunk < n_chan - 1), spill, 0.0)
        before = jnp.maximum(chunk * outs, LANES) - LANES
        before = pl.ds(pl.multiple_of(before, LANES), LANES)
        total[:, before] += jnp.where(early | (chunk == 0), 0.0, spill)


def tile_of(group, width, vectors):
    half = vectors // 2
    if group == 0:
        return jnp.where(width == 0, 0, half + 1), half - 1
    if group == 1:
        return jnp.where(width == 0, half - 1, 0), half + 1
    return 0, vectors


def tiles_in(group, vectors):
    return -(-BLOCKS * tile_of(group, 0, vectors)[1] // 2)


def own_half(n_chan):
    return jnp.where(lax.axis_index("chan") < n_chan // 2, 0, 1)


def place_kernel(n_chan, n_tgroup, outs, plan, steps, owners, *refs):
    got, (total, pairs) = refs[: -len(plan) - 2], refs[-2:]
    sends = refs[-len(plan) - 2 : -2]
    me = lax.axis_index("tgroup")
    if len(got) == 1:
        total[...] = got[0][...]
    else:
        add_spills(n_chan, outs, steps, got, total)

    for at in range(n_tgroup * SLOTS):
        pairs[at] = -1
    counts = jnp.int32(0)
    for q in range(PAIRS):
        owner = owners[q]
        slot = (counts >> (3 * owner)) & 7
        counts = counts + (jnp.int32(1) << (3 * owner))
        pairs[(owner ^ me) * SLOTS + slot] = q

    zero = jnp.zeros((CB, LANES), jnp.float32)
    for send, (shift, group) in zip(sends, plan):
        base, per = tile_of(group, own_half(n_chan), total.shape[1] // LANES)

        def tiles(q):
            rows = pl.ds(pl.multiple_of(q * CB, CB), CB)
            return [
                total[rows, pl.ds(pl.multiple_of((base + j) * LANES, LANES), LANES)]
                for j in range(per)
            ]

        parts = sum([tiles(p * K) for p in range(STRIPES)], [])
        for s in range(SLOTS):
            q = pairs[shift * SLOTS + s]
            parts += [jnp.where(q >= 0, tile, 0.0) for tile in tiles(jnp.maximum(q, 0))]
        parts += [zero] * (len(parts) % 2)
        for at in range(0, len(parts), 2):
            value = jnp.concatenate(parts[at : at + 2], 0)
            send[at // 2] = value.astype(jnp.bfloat16)


def correlate_kernel(n_chan, groups, factor, last, owners, *refs):
    if last:
        *refs, final, sems = refs
    near, far, windows, whole, parts_sum = refs[-5:]
    out = refs[-6]
    arrived = refs[: len(groups)]
    before = refs[len(groups)] if len(refs) > len(groups) + 6 else None
    cut = near.shape[2]
    span = cut + far.shape[2]
    samples = span - LANES
    cols = span // LANES
    high = STEP * CB
    ahead = FRONT // LANES - 1
    me = lax.axis_index("tgroup")
    first_count = jnp.int32(0)
    for q in range(K):
        first_count += jnp.where(owners[q] == me, 1, 0)

    for ref, group in zip(arrived, groups):
        base, per = tile_of(group, own_half(n_chan), samples // LANES)
        for at in range(ref.shape[0]):
            value = ref[at].astype(jnp.float32)
            for part in range(2):
                block, j = (2 * at + part) // per, (2 * at + part) % per
                if block < BLOCKS:
                    lanes = pl.ds(pl.multiple_of((base + j) * LANES, LANES), LANES)
                    whole[block, :, lanes] = value[part * CB : (part + 1) * CB]

    def series(block):
        return jnp.concatenate([whole[block], jnp.zeros((CB, LANES), jnp.float32)], 1)

    for p in range(STRIPES):
        value = series(p)
        for a in range(CB):
            spread = jnp.broadcast_to(value[a : a + 1], (SHIFTS, span))
            turned = pltpu.roll(spread, 0, 1, stride=1, stride_axis=0)
            turned = turned.astype(jnp.bfloat16)
            near[p, a * SHIFTS : (a + 1) * SHIFTS, :] = turned[:, :cut]
            far[p, a * SHIFTS : (a + 1) * SHIFTS, :] = turned[:, cut:]

    def bounds(i):
        return max(0, ahead - i), min(cols, ahead + cols - i)

    def make_window(s):
        for i in range(LAG_BLOCKS):
            first, end = bounds(i)
            rows = slice(i * high, (i + 1) * high)
            if first > 0:
                windows[s, rows, : first * LANES] = jnp.zeros((high, first * LANES), jnp.bfloat16)
            if end < cols:
                windows[s, rows, end * LANES :] = jnp.zeros(
                    (high, (cols - end) * LANES), jnp.bfloat16
                )
        value = series(STRIPES + s)
        turned = [pltpu.roll(value, span - (FRONT - MAXLAG + SHIFTS * n), 1) for n in range(STEP)]
        stacked = jnp.concatenate(turned, 0).astype(jnp.bfloat16)
        stacked = jnp.concatenate([stacked[:, samples:], stacked[:, :samples]], 1)
        for i in range(LAG_BLOCKS):
            first, end = bounds(i)
            windows[s, i * high : (i + 1) * high, first * LANES : end * LANES] = stacked[
                :, (first + i - ahead) * LANES : (end + i - ahead) * LANES
            ]

    which = [jnp.where(s < first_count, 0, 1) for s in range(SLOTS)]
    for s in range(SLOTS):
        make_window(s)
        value = lax.dot_general(
            windows[s, :, :cut], near[which[s]], NT, preferred_element_type=jnp.float32
        )
        parts_sum[s] = value if before is None else value + before[s]

    def leave(part):
        slots = pl.ds(0, SLOTS // 2 + 1) if part == 0 else pl.ds(SLOTS // 2 + 1, SLOTS // 2)
        return pltpu.make_async_copy(final.at[slots], out.at[slots], sems.at[part])

    group = lax.broadcasted_iota(jnp.int32, (CB, LANES), 1) // SHIFTS
    for s in range(SLOTS):
        summed = parts_sum[s] + lax.dot_general(
            windows[s, :, cut:], far[which[s]], NT, preferred_element_type=jnp.float32
        )
        if not last:
            out[s] = summed
            continue
        summed = summed * factor
        for i in range(LAG_BLOCKS):
            width = min(LANES, LAGS - i * LANES)
            for h in range(CB // STEP):
                parts = [
                    summed[(i * STEP + n) * CB : (i * STEP + n + 1) * CB, h * LANES : (h + 1) * LANES]
                    for n in range(STEP)
                ]
                for a in range(STEP):
                    value = parts[a]
                    for n in range(STEP):
                        if n != a:
                            moved = pltpu.roll(parts[n], (SHIFTS * (n - a)) % LANES, 1)
                            value = jnp.where(group == n, moved, value)
                    final[s, h * STEP + a, :, i * LANES : i * LANES + width] = value[:, :width]
        if s == SLOTS // 2:
            leave(0).start()
    if last:
        leave(1).start()
        leave(0).wait()
        leave(1).wait()


def correlate(n_chan, owners, arrived, groups, before, factor, last, samples):
    high, wide = STEP * LAG_BLOCKS * CB, CB * SHIFTS
    if last:
        shape = jax.ShapeDtypeStruct((SLOTS, CB, CB, LAGS), jnp.float32)
    else:
        shape = jax.ShapeDtypeStruct((SLOTS, high, wide), jnp.float32)
    operands = (owners,) + arrived + (() if before is None else (before,))
    depth, cut = samples + LANES, samples // 2
    return pl.pallas_call(
        functools.partial(correlate_kernel, n_chan, groups, factor, last),
        out_shape=shape,
        in_specs=[smem()] + [vmem()] * (len(operands) - 1),
        out_specs=pl.BlockSpec(memory_space=pl.ANY) if last else vmem(),
        scratch_shapes=[
            pltpu.VMEM((STRIPES, wide, cut), jnp.bfloat16),
            pltpu.VMEM((STRIPES, wide, depth - cut), jnp.bfloat16),
            pltpu.VMEM((SLOTS, high, depth), jnp.bfloat16),
            pltpu.VMEM((BLOCKS, CB, samples), jnp.float32),
            pltpu.VMEM((SLOTS, high, wide), jnp.float32),
        ]
        + [pltpu.VMEM(shape.shape, jnp.float32), pltpu.SemaphoreType.DMA((2,))] * last,
        compiler_params=params(40),
        name="correlate_last" if last else "correlate",
    )(*operands)


def local(raw_strain, whitening_taps, first_block, pair_owner):
    n_chan, n_tgroup = lax.axis_size("chan"), lax.axis_size("tgroup")
    rows, channels = raw_strain.shape
    outs = rows // 2
    samples = outs * n_chan
    count = PAIRS * CB
    owners = pair_owner[:, 0]

    firsts = lax.all_to_all(
        jnp.broadcast_to(first_block[None, :], (n_chan, STRIPES)),
        "chan",
        split_axis=0,
        concat_axis=0,
        tiled=True,
    )
    line = -(-(rows + 2 * outs + 4 * SPILL) // (2 * LANES)) * 2 * LANES
    weights = pl.pallas_call(
        weights_kernel,
        out_shape=jax.ShapeDtypeStruct((rows, outs + 2 * SPILL), jnp.bfloat16),
        in_specs=[pl.BlockSpec(memory_space=pl.ANY)],
        out_specs=vmem(),
        scratch_shapes=[
            pltpu.VMEM((1, TAPS), jnp.float32),
            pltpu.VMEM((8, line), jnp.float32),
            pltpu.SemaphoreType.DMA,
        ],
        compiler_params=params(40),
        name="fir_weights",
    )(whitening_taps.reshape(1, TAPS))

    groups = [[k] for k in range(n_chan)]
    sends = pl.pallas_call(
        functools.partial(select_kernel, n_chan, groups),
        out_shape=[
            jax.ShapeDtypeStruct((len(group) * count, outs + 2 * SPILL), jnp.bfloat16)
            for group in groups
        ],
        in_specs=[smem(), pl.BlockSpec(memory_space=pl.ANY), vmem()],
        out_specs=[vmem()] * len(groups),
        scratch_shapes=[
            pltpu.VMEM((n_chan * STRIPES, rows, 2 * LANES), jnp.float32),
            pltpu.VMEM((n_chan * count, rows), jnp.bfloat16),
            pltpu.SemaphoreType.DMA((n_chan * STRIPES,)),
        ],
        compiler_params=params(40),
        name="select_filter",
    )(firsts, raw_strain, weights)

    def exchange(value, k):
        return lax.ppermute(value, "chan", [(c, c ^ k) for c in range(n_chan)])

    half = n_chan // 2
    got = [sends[0]] + [exchange(sends[k], k) for k in range(1, n_chan)]
    steps = [[k] for k in range(n_chan)]
    early, late = got[:half], got

    if outs % LANES:
        wide = jnp.stack(got).astype(jnp.float32)
        wide = jnp.take(wide, lax.axis_index("chan") ^ jnp.arange(n_chan), axis=0)
        none = jnp.zeros((n_chan, count, outs - SPILL), jnp.float32)
        zero = jnp.zeros((1, count, SPILL), jnp.float32)
        right = jnp.concatenate([zero, wide[:-1, :, outs : outs + SPILL]], 0)
        left = jnp.concatenate([wide[1:, :, outs + SPILL :], zero], 0)
        added = wide[:, :, :outs] + jnp.concatenate([right, none], 2) + jnp.concatenate([none, left], 2)
        early = late = [added.transpose(1, 0, 2).reshape(count, samples)]

    order = sorted(range(1, n_tgroup), key=lambda s: (s.bit_length(), -s))
    vectors = samples // LANES
    factor = 1.0 / math.sqrt(samples)

    def place(plan, use, name):
        return pl.pallas_call(
            functools.partial(place_kernel, n_chan, n_tgroup, outs, plan, steps),
            out_shape=[
                jax.ShapeDtypeStruct((tiles_in(group, vectors), 2 * CB, LANES), jnp.bfloat16)
                for _, group in plan
            ],
            in_specs=[smem()] + [vmem()] * len(use),
            out_specs=[vmem()] * len(plan),
            scratch_shapes=[
                pltpu.VMEM((count, samples), jnp.float32),
                pltpu.SMEM((n_tgroup * SLOTS,), jnp.int32),
            ],
            compiler_params=params(40),
            name=name,
        )(owners, *use)

    def hand_over(value, shift):
        return lax.ppermute(value, "tgroup", [(g, g ^ shift) for g in range(n_tgroup)])

    if outs % LANES == 0:
        early, got[half] = lax.optimization_barrier((early, got[half]))
        late = list(early) + got[half:]
    far = order[1:]
    first = place([(shift, 0) for shift in far], early, "place_first")
    arrived = {shift: [hand_over(value, shift)] for shift, value in zip(far, first)}
    plan = [(0, 2), (1, 2)] + [(shift, 1) for shift in far]
    own, near, *second = place(plan, late, "place_second")
    arrived[0], arrived[1] = [own], [hand_over(near, 1)]
    for shift, value in zip(far, second):
        value, held = lax.optimization_barrier((value, arrived[shift][0]))
        arrived[shift] = [held, hand_over(value, shift)]

    value = None
    for at, shift in enumerate([0] + order):
        parts = (0, 1) if shift in far else (2,)
        last = at == n_tgroup - 1
        value = correlate(
            n_chan, owners, tuple(arrived[shift]), parts, value, factor, last, samples
        )
    return value


def solution(mesh):
    in_specs = (P(("tgroup", "chan"), None), P(), P("chan"), P("chan", None))
    out_specs = P(("tgroup", "chan"), None, None, None)
    return jax.shard_map(local, mesh=mesh, in_specs=in_specs, out_specs=out_specs, check_vma=False)
```

```python
import functools
import math

import jax
import jax.numpy as jnp
from jax import lax
from jax.experimental import pallas as pl
from jax.experimental.pallas import tpu as pltpu
from jax.sharding import PartitionSpec as P

MAXLAG = 500
LAGS = 2 * MAXLAG + 1
TAPS = 255
CB = 8
K = 8
STRIPES = 2
SLOTS = 5
PAIRS = STRIPES * K
BLOCKS = STRIPES + SLOTS
WIDE = K * CB
SPILL = 64
LANES = 128
SHIFTS = 32
STEP = LANES // SHIFTS
LAG_BLOCKS = -(-LAGS // LANES)
FRONT = -(-MAXLAG // LANES) * LANES
NT = (((1,), (1,)), ((), ()))


def params(megabytes):
    return pltpu.CompilerParams(vmem_limit_bytes=megabytes << 20)


def vmem():
    return pl.BlockSpec(memory_space=pltpu.VMEM)


def smem():
    return pl.BlockSpec(memory_space=pltpu.SMEM)


def weights_kernel(taps, weights, held, line, sem):
    copy = pltpu.make_async_copy(taps, held, sem)
    copy.start()
    rows, outs, width = weights.shape[0], weights.shape[1] - 2 * SPILL, line.shape[1]
    line[...] = jnp.zeros_like(line)
    copy.wait()
    line[0:1, :TAPS] = held[...]
    spread = jnp.broadcast_to(line[0:1, :], (outs + 2 * SPILL, width))
    value = pltpu.roll(spread, width - 4 * SPILL + 1, 1, stride=2, stride_axis=0)[:, :rows]
    value = jnp.concatenate([value[SPILL : SPILL + outs], value[SPILL + outs :], value[:SPILL]], 0)
    weights[...] = value.T.astype(jnp.bfloat16)


def select_kernel(n_chan, groups, firsts, raw, weights, *refs):
    sends, (window, picked, sems) = refs[: len(groups)], refs[len(groups) :]
    rows, channels = raw.shape
    steps = [k for group in groups for k in group]
    stripes = n_chan * STRIPES
    blocks_per = channels // n_chan // CB
    span = window.shape[2]
    me = lax.axis_index("chan")

    def place(p):
        c, k = me ^ steps[p // STRIPES], p % STRIPES
        start = (firsts[c, k] + c * blocks_per) * CB
        offset = lax.rem(start, LANES)
        base = start - offset
        return start, offset, base, (offset > LANES - WIDE) & (base < channels - LANES)

    def copy(p, tile):
        base = place(p)[2]
        if tile:
            base = jnp.minimum(base + LANES, channels - LANES)
        return pltpu.make_async_copy(
            raw.at[:, pl.ds(pl.multiple_of(base, LANES), LANES)],
            window.at[p, :, pl.ds(tile * LANES, LANES)],
            sems.at[p, tile],
        )

    for p in range(stripes):
        copy(p, 0).start()

        @pl.when(place(p)[3])
        def _(p=p):
            copy(p, 1).start()

    for p in range(stripes):

        @pl.when(jnp.logical_not(place(p)[3]))
        def _(p=p):
            window[p, :, LANES:] = jnp.zeros((rows, LANES), jnp.float32)

    row = lax.broadcasted_iota(jnp.int32, (WIDE, span), 0)
    lane = lax.broadcasted_iota(jnp.int32, (WIDE, span), 1)
    batch = 4 * STRIPES
    for first in range(0, stripes, batch):
        for p in range(first, first + batch):
            copy(p, 0).wait()

            @pl.when(place(p)[3])
            def _(p=p):
                copy(p, 1).wait()

        for p in range(first, first + batch):
            start, offset, _, _ = place(p)
            hot = (lane == row + offset) & (row < channels - start)
            hot = jnp.where(hot, 1.0, 0.0).astype(jnp.bfloat16)
            block = window[p].astype(jnp.bfloat16)
            chosen = lax.dot_general(hot, block, NT, preferred_element_type=jnp.float32)
            picked[p * WIDE : (p + 1) * WIDE, :] = chosen.astype(jnp.bfloat16)
        part = slice(first * WIDE, (first + batch) * WIDE)
        result = jnp.dot(
            picked[part, :], weights[...], preferred_element_type=jnp.float32
        ).astype(jnp.bfloat16)
        height = STRIPES * WIDE
        for at in range(batch // STRIPES):
            k = steps[first // STRIPES + at]
            out, where = [(o, g.index(k)) for o, g in enumerate(groups) if k in g][0]
            sends[out][where * height : (where + 1) * height, :] = result[at * height : (at + 1) * height]


def add_spills(n_chan, outs, steps, got, total):
    count = total.shape[0]
    early = lax.broadcasted_iota(jnp.int32, (count, LANES), 1) < SPILL
    me = lax.axis_index("chan")
    pieces = [
        (me ^ k, ref.at[at * count : (at + 1) * count])
        for ks, ref in zip(steps, got)
        for at, k in enumerate(ks)
    ]
    for chunk, value in pieces:
        at = pl.ds(pl.multiple_of(chunk * outs, LANES), outs)
        total[:, at] = value[:, :outs].astype(jnp.float32)
    for chunk, value in pieces:
        spill = value[:, outs:].astype(jnp.float32)
        after = jnp.minimum(chunk + 1, n_chan - 1) * outs
        after = pl.ds(pl.multiple_of(after, LANES), LANES)
        total[:, after] += jnp.where(early & (chunk < n_chan - 1), spill, 0.0)
        before = jnp.maximum(chunk * outs, LANES) - LANES
        before = pl.ds(pl.multiple_of(before, LANES), LANES)
        total[:, before] += jnp.where(early | (chunk == 0), 0.0, spill)


def tile_of(group, width, vectors):
    half = vectors // 2
    if group == 0:
        return jnp.where(width == 0, 0, half + 1), half - 1
    if group == 1:
        return jnp.where(width == 0, half - 1, 0), half + 1
    return 0, vectors


def tiles_in(group, vectors):
    return -(-BLOCKS * tile_of(group, 0, vectors)[1] // 2)


def own_half(n_chan):
    return jnp.where(lax.axis_index("chan") < n_chan // 2, 0, 1)


def place_kernel(n_chan, n_tgroup, outs, plan, steps, owners, *refs):
    got, (total, pairs) = refs[: -len(plan) - 2], refs[-2:]
    sends = refs[-len(plan) - 2 : -2]
    me = lax.axis_index("tgroup")
    if len(got) == 1:
        total[...] = got[0][...]
    else:
        add_spills(n_chan, outs, steps, got, total)

    for at in range(n_tgroup * SLOTS):
        pairs[at] = -1
    counts = jnp.int32(0)
    for q in range(PAIRS):
        owner = owners[q]
        slot = (counts >> (3 * owner)) & 7
        counts = counts + (jnp.int32(1) << (3 * owner))
        pairs[(owner ^ me) * SLOTS + slot] = q

    zero = jnp.zeros((CB, LANES), jnp.float32)
    for send, (shift, group) in zip(sends, plan):
        base, per = tile_of(group, own_half(n_chan), total.shape[1] // LANES)

        def tiles(q):
            rows = pl.ds(pl.multiple_of(q * CB, CB), CB)
            return [
                total[rows, pl.ds(pl.multiple_of((base + j) * LANES, LANES), LANES)]
                for j in range(per)
            ]

        parts = sum([tiles(p * K) for p in range(STRIPES)], [])
        for s in range(SLOTS):
            q = pairs[shift * SLOTS + s]
            parts += [jnp.where(q >= 0, tile, 0.0) for tile in tiles(jnp.maximum(q, 0))]
        parts += [zero] * (len(parts) % 2)
        for at in range(0, len(parts), 2):
            value = jnp.concatenate(parts[at : at + 2], 0)
            send[at // 2] = value.astype(jnp.bfloat16)


def correlate_kernel(n_chan, groups, factor, last, owners, *refs):
    if last:
        *refs, final, sems = refs
    near, far, windows, whole, parts_sum = refs[-5:]
    out = refs[-6]
    arrived = refs[: len(groups)]
    before = refs[len(groups)] if len(refs) > len(groups) + 6 else None
    cut = near.shape[2]
    span = cut + far.shape[2]
    samples = span - LANES
    cols = span // LANES
    high = STEP * CB
    ahead = FRONT // LANES - 1
    me = lax.axis_index("tgroup")
    first_count = jnp.int32(0)
    for q in range(K):
        first_count += jnp.where(owners[q] == me, 1, 0)

    for ref, group in zip(arrived, groups):
        base, per = tile_of(group, own_half(n_chan), samples // LANES)
        for at in range(ref.shape[0]):
            value = ref[at].astype(jnp.float32)
            for part in range(2):
                block, j = (2 * at + part) // per, (2 * at + part) % per
                if block < BLOCKS:
                    lanes = pl.ds(pl.multiple_of((base + j) * LANES, LANES), LANES)
                    whole[block, :, lanes] = value[part * CB : (part + 1) * CB]

    def series(block):
        return jnp.concatenate([whole[block], jnp.zeros((CB, LANES), jnp.float32)], 1)

    for p in range(STRIPES):
        value = series(p)
        for a in range(CB):
            spread = jnp.broadcast_to(value[a : a + 1], (SHIFTS, span))
            turned = pltpu.roll(spread, 0, 1, stride=1, stride_axis=0)
            turned = turned.astype(jnp.bfloat16)
            near[p, a * SHIFTS : (a + 1) * SHIFTS, :] = turned[:, :cut]
            far[p, a * SHIFTS : (a + 1) * SHIFTS, :] = turned[:, cut:]

    def bounds(i):
        return max(0, ahead - i), min(cols, ahead + cols - i)

    def make_window(s):
        for i in range(LAG_BLOCKS):
            first, end = bounds(i)
            rows = slice(i * high, (i + 1) * high)
            if first > 0:
                windows[s, rows, : first * LANES] = jnp.zeros((high, first * LANES), jnp.bfloat16)
            if end < cols:
                windows[s, rows, end * LANES :] = jnp.zeros(
                    (high, (cols - end) * LANES), jnp.bfloat16
                )
        value = series(STRIPES + s)
        turned = [pltpu.roll(value, span - (FRONT - MAXLAG + SHIFTS * n), 1) for n in range(STEP)]
        stacked = jnp.concatenate(turned, 0).astype(jnp.bfloat16)
        stacked = jnp.concatenate([stacked[:, samples:], stacked[:, :samples]], 1)
        for i in range(LAG_BLOCKS):
            first, end = bounds(i)
            windows[s, i * high : (i + 1) * high, first * LANES : end * LANES] = stacked[
                :, (first + i - ahead) * LANES : (end + i - ahead) * LANES
            ]

    which = [jnp.where(s < first_count, 0, 1) for s in range(SLOTS)]
    for s in range(SLOTS):
        make_window(s)
        value = lax.dot_general(
            windows[s, :, :cut], near[which[s]], NT, preferred_element_type=jnp.float32
        )
        parts_sum[s] = value if before is None else value + before[s]

    def leave(part):
        slots = pl.ds(0, SLOTS // 2 + 1) if part == 0 else pl.ds(SLOTS // 2 + 1, SLOTS // 2)
        return pltpu.make_async_copy(final.at[slots], out.at[slots], sems.at[part])

    group = lax.broadcasted_iota(jnp.int32, (CB, LANES), 1) // SHIFTS
    for s in range(SLOTS):
        summed = parts_sum[s] + lax.dot_general(
            windows[s, :, cut:], far[which[s]], NT, preferred_element_type=jnp.float32
        )
        if not last:
            out[s] = summed
            continue
        summed = summed * factor
        for i in range(LAG_BLOCKS):
            width = min(LANES, LAGS - i * LANES)
            for h in range(CB // STEP):
                parts = [
                    summed[(i * STEP + n) * CB : (i * STEP + n + 1) * CB, h * LANES : (h + 1) * LANES]
                    for n in range(STEP)
                ]
                for a in range(STEP):
                    value = parts[a]
                    for n in range(STEP):
                        if n != a:
                            moved = pltpu.roll(parts[n], (SHIFTS * (n - a)) % LANES, 1)
                            value = jnp.where(group == n, moved, value)
                    final[s, h * STEP + a, :, i * LANES : i * LANES + width] = value[:, :width]
        if s == SLOTS // 2:
            leave(0).start()
    if last:
        leave(1).start()
        leave(0).wait()
        leave(1).wait()


def correlate(n_chan, owners, arrived, groups, before, factor, last, samples):
    high, wide = STEP * LAG_BLOCKS * CB, CB * SHIFTS
    if last:
        shape = jax.ShapeDtypeStruct((SLOTS, CB, CB, LAGS), jnp.float32)
    else:
        shape = jax.ShapeDtypeStruct((SLOTS, high, wide), jnp.float32)
    operands = (owners,) + arrived + (() if before is None else (before,))
    depth, cut = samples + LANES, samples // 2
    return pl.pallas_call(
        functools.partial(correlate_kernel, n_chan, groups, factor, last),
        out_shape=shape,
        in_specs=[smem()] + [vmem()] * (len(operands) - 1),
        out_specs=pl.BlockSpec(memory_space=pl.ANY) if last else vmem(),
        scratch_shapes=[
            pltpu.VMEM((STRIPES, wide, cut), jnp.bfloat16),
            pltpu.VMEM((STRIPES, wide, depth - cut), jnp.bfloat16),
            pltpu.VMEM((SLOTS, high, depth), jnp.bfloat16),
            pltpu.VMEM((BLOCKS, CB, samples), jnp.float32),
            pltpu.VMEM((SLOTS, high, wide), jnp.float32),
        ]
        + [pltpu.VMEM(shape.shape, jnp.float32), pltpu.SemaphoreType.DMA((2,))] * last,
        compiler_params=params(40),
        name="correlate_last" if last else "correlate",
    )(*operands)


def local(raw_strain, whitening_taps, first_block, pair_owner):
    n_chan, n_tgroup = lax.axis_size("chan"), lax.axis_size("tgroup")
    rows, channels = raw_strain.shape
    outs = rows // 2
    samples = outs * n_chan
    count = PAIRS * CB
    owners = pair_owner[:, 0]

    firsts = lax.all_to_all(
        jnp.broadcast_to(first_block[None, :], (n_chan, STRIPES)),
        "chan",
        split_axis=0,
        concat_axis=0,
        tiled=True,
    )
    line = -(-(rows + 2 * outs + 4 * SPILL) // (2 * LANES)) * 2 * LANES
    weights = pl.pallas_call(
        weights_kernel,
        out_shape=jax.ShapeDtypeStruct((rows, outs + 2 * SPILL), jnp.bfloat16),
        in_specs=[pl.BlockSpec(memory_space=pl.ANY)],
        out_specs=vmem(),
        scratch_shapes=[
            pltpu.VMEM((1, TAPS), jnp.float32),
            pltpu.VMEM((8, line), jnp.float32),
            pltpu.SemaphoreType.DMA,
        ],
        compiler_params=params(40),
        name="fir_weights",
    )(whitening_taps.reshape(1, TAPS))

    groups = [[k] for k in range(n_chan)]
    sends = pl.pallas_call(
        functools.partial(select_kernel, n_chan, groups),
        out_shape=[
            jax.ShapeDtypeStruct((len(group) * count, outs + 2 * SPILL), jnp.bfloat16)
            for group in groups
        ],
        in_specs=[smem(), pl.BlockSpec(memory_space=pl.ANY), vmem()],
        out_specs=[vmem()] * len(groups),
        scratch_shapes=[
            pltpu.VMEM((n_chan * STRIPES, rows, 2 * LANES), jnp.float32),
            pltpu.VMEM((n_chan * count, rows), jnp.bfloat16),
            pltpu.SemaphoreType.DMA((n_chan * STRIPES, 2)),
        ],
        compiler_params=params(40),
        name="select_filter",
    )(firsts, raw_strain, weights)

    def exchange(value, k):
        return lax.ppermute(value, "chan", [(c, c ^ k) for c in range(n_chan)])

    half = n_chan // 2
    got = [sends[0]] + [exchange(sends[k], k) for k in range(1, n_chan)]
    steps = [[k] for k in range(n_chan)]
    early, late = got[:half], got

    if outs % LANES:
        wide = jnp.stack(got).astype(jnp.float32)
        wide = jnp.take(wide, lax.axis_index("chan") ^ jnp.arange(n_chan), axis=0)
        none = jnp.zeros((n_chan, count, outs - SPILL), jnp.float32)
        zero = jnp.zeros((1, count, SPILL), jnp.float32)
        right = jnp.concatenate([zero, wide[:-1, :, outs : outs + SPILL]], 0)
        left = jnp.concatenate([wide[1:, :, outs + SPILL :], zero], 0)
        added = wide[:, :, :outs] + jnp.concatenate([right, none], 2) + jnp.concatenate([none, left], 2)
        early = late = [added.transpose(1, 0, 2).reshape(count, samples)]

    order = sorted(range(1, n_tgroup), key=lambda s: (s.bit_length(), -s))
    vectors = samples // LANES
    factor = 1.0 / math.sqrt(samples)

    def place(plan, use, name):
        return pl.pallas_call(
            functools.partial(place_kernel, n_chan, n_tgroup, outs, plan, steps),
            out_shape=[
                jax.ShapeDtypeStruct((tiles_in(group, vectors), 2 * CB, LANES), jnp.bfloat16)
                for _, group in plan
            ],
            in_specs=[smem()] + [vmem()] * len(use),
            out_specs=[vmem()] * len(plan),
            scratch_shapes=[
                pltpu.VMEM((count, samples), jnp.float32),
                pltpu.SMEM((n_tgroup * SLOTS,), jnp.int32),
            ],
            compiler_params=params(40),
            name=name,
        )(owners, *use)

    def hand_over(value, shift):
        return lax.ppermute(value, "tgroup", [(g, g ^ shift) for g in range(n_tgroup)])

    if outs % LANES == 0:
        early, got[half] = lax.optimization_barrier((early, got[half]))
        late = list(early) + got[half:]
    far = order[1:]
    first = place([(shift, 0) for shift in far], early, "place_first")
    arrived = {shift: [hand_over(value, shift)] for shift, value in zip(far, first)}
    plan = [(0, 2), (1, 2)] + [(shift, 1) for shift in far]
    own, near, *second = place(plan, late, "place_second")
    arrived[0], arrived[1] = [own], [hand_over(near, 1)]
    for shift, value in zip(far, second):
        value, held = lax.optimization_barrier((value, arrived[shift][0]))
        arrived[shift] = [held, hand_over(value, shift)]

    value = None
    for at, shift in enumerate([0] + order):
        parts = (0, 1) if shift in far else (2,)
        last = at == n_tgroup - 1
        value = correlate(
            n_chan, owners, tuple(arrived[shift]), parts, value, factor, last, samples
        )
    return value


def solution(mesh):
    in_specs = (P(("tgroup", "chan"), None), P(), P("chan"), P("chan", None))
    out_specs = P(("tgroup", "chan"), None, None, None)
    return jax.shard_map(local, mesh=mesh, in_specs=in_specs, out_specs=out_specs, check_vma=False)
```
